32 devices in a mesh: seq: 8 (over z, y), row: 4 (over x, core).
Axes of the slice: x: 2, y: 2, z: 4, core: 2. Of those that a mesh axis runs over, the one named last changes fastest.
Arguments:
- tokens: bfloat16 [2, 4, 8192, 512], P(None, 'row', 'seq'), may hold values from -6 to 6
- cotangent: float32 [2, 4, 8192, 512], P(None, 'row', 'seq'), may hold values from -6 to 6
- resets: int32 [2, 4, 8], P(None, 'row'), may hold values from 0 to 8191, as said below
- ln_gain: float32 [2, 512], replicated, may hold values from 0.25 to 1.75
- ln_bias: float32 [2, 512], replicated, may hold values from -3 to 3
- in_re: bfloat16 [2, 512, 256], replicated, may hold values from -0.1875 to 0.1875
- in_im: bfloat16 [2, 512, 256], replicated, may hold values from -0.1875 to 0.1875
- nu_log: float32 [2, 256], replicated, as said below
- theta_log: float32 [2, 256], replicated, may hold values from -6.9 to -1.2
- out_re: bfloat16 [2, 256, 512], replicated, may hold values from -0.25 to 0.25
- out_im: bfloat16 [2, 256, 512], replicated, may hold values from -0.25 to 0.25
- skip: float32 [2, 512], replicated, may hold values from -3 to 3
- glu_w: bfloat16 [2, 512, 1024], replicated, may hold values from -0.25 to 0.25
- glu_b: float32 [2, 1024], replicated, may hold values from -3 to 3
Outputs:
- activations: float32 [2, 4, 8192, 512], P(None, 'row', 'seq')
- input_grad: float32 [2, 4, 8192, 512], P(None, 'row', 'seq')
- grad_ln_gain: float32 [2, 512], replicated
- grad_ln_bias: float32 [2, 512], replicated
- grad_in_re: float32 [2, 512, 256], replicated
- grad_in_im: float32 [2, 512, 256], replicated
- grad_nu_log: float32 [2, 256], replicated
- grad_theta_log: float32 [2, 256], replicated
- grad_out_re: float32 [2, 256, 512], replicated
- grad_out_im: float32 [2, 256, 512], replicated
- grad_skip: float32 [2, 512], replicated
- grad_glu_w: float32 [2, 512, 1024], replicated
- grad_glu_b: float32 [2, 1024], replicated
The draws below stay inside these ranges and needn't reach their ends.
Inputs may be any that keep to these rules, and one draw needn't show every extreme that they name: `resets`: each row's positions rise, may repeat, and the first is 0; some row of every draw has a reset at the final position. exp(nu_log) lies between 0.2 / 8192 and 1 / 30.
All inputs are finite; a program needn't handle non-finite values.
Results may differ from the reference program's by a relative error of at most 0.017.
Values sent between devices are 32-bit elements; how exact they have to be, the bound alone decides.
No kernel may reach another device: no remote copies, remote signals or barrier semaphores. Data moves between devices by JAX's collectives and lax.ppermute only.
A program may use at most 256 MiB of HBM per device.

```python
import math
import jax
import jax.numpy as jnp
from jax import lax

D = 512
S = 256
LEN_DEV = 1024
MB = 2
LAYERS = 2
NRESET = 8
ROWS = 4
SEQLEN = 8192


def draw_resets(key, part):
    key = jax.random.fold_in(key, 11)
    key_early, key_late, key_spread, key_pick = jax.random.split(key, 4)
    shape = (MB, ROWS, NRESET)
    early = jax.random.randint(key_early, shape, 1, LEN_DEV // 2)
    late = jax.random.randint(key_late, shape, SEQLEN - LEN_DEV // 2, SEQLEN)
    spread = jax.random.randint(key_spread, shape, 1, SEQLEN)
    slot = jnp.arange(NRESET, dtype=jnp.int32)
    longest = jnp.where(slot < NRESET // 2, early, late)
    longest = jnp.where(slot == NRESET - 1, SEQLEN - 1, longest)
    chosen = jax.random.randint(key_pick, (1, ROWS, 1), 0, MB)
    micro_ids = jnp.arange(MB, dtype=jnp.int32)[:, None, None]
    starts = jnp.where(micro_ids == chosen, longest, spread)
    starts = jnp.where(slot == 0, 0, starts)
    return jnp.sort(starts, axis=-1).astype(jnp.int32)


def draw_nu_log(key, part):
    key = jax.random.fold_in(key, 23)
    key_kind, key_fast, key_mid, key_slow = jax.random.split(key, 4)
    shape = (LAYERS, S)
    fast_share = 0.3
    mid_share = 0.2
    kind = jax.random.uniform(key_kind, shape, dtype=jnp.float32)
    fast = jax.random.uniform(key_fast, shape, dtype=jnp.float32, minval=math.log(1.0 / 50.0), maxval=math.log(1.0 / 30.0))
    middle = jax.random.uniform(key_mid, shape, dtype=jnp.float32, minval=math.log(2.0) - math.log(SEQLEN), maxval=math.log(1.0 / 30.0))
    slow = jax.random.uniform(key_slow, shape, dtype=jnp.float32, minval=math.log(0.2), maxval=math.log(2.0)) - math.log(SEQLEN)
    chosen = jnp.where(kind < fast_share, fast, jnp.where(kind < fast_share + mid_share, middle, slow))
    return chosen.astype(jnp.float32)


def level_of(own_key, dims, cuts, smallest, largest):
    loudness, own = 1.0, jax.random.fold_in(own_key, 6)
    for axis_at, blocks in cuts:
        heights = jnp.exp(jax.random.uniform(jax.random.fold_in(own, axis_at), (blocks,), jnp.float32, smallest / len(cuts), largest / len(cuts)))
        loudness = loudness * jnp.repeat(heights, dims[axis_at] // blocks).reshape([-1 if axis == axis_at else 1 for axis in range(len(dims))])
    return loudness


def normal_values(key, extent, deviation, reach, cuts=(), kind=jnp.bfloat16):
    result = jax.random.normal(key, extent, jnp.float32) * deviation
    if len(cuts) > 0:
        result = level_of(key, extent, cuts, -0.22, 0.18) * result
    return jnp.clip(result, min=-reach, max=reach).astype(kind)


def setup_inputs(seed: int = 0) -> dict:
    streams_of = jax.random.split(jax.random.key(seed), 15)
    return {
        "tokens": normal_values(streams_of[0], (MB, ROWS, SEQLEN, D), 1.0, 6.0, ((1, 4), (2, 8))),
        "cotangent": normal_values(streams_of[1], (MB, ROWS, SEQLEN, D), 1.0, 6.0, ((1, 4), (2, 8)), jnp.float32),
        "resets": draw_resets(jax.random.fold_in(streams_of[14], 71), 0),
        "ln_gain": jnp.clip(1.0 + 0.15 * jax.random.normal(streams_of[3], (LAYERS, D), jnp.float32), 0.25, 1.75),
        "ln_bias": normal_values(streams_of[4], (LAYERS, D), 0.3, 3.0, (), jnp.float32),
        "in_re": normal_values(streams_of[5], (LAYERS, D, S), (2 * D) ** -0.5, 0.1875),
        "in_im": normal_values(streams_of[6], (LAYERS, D, S), (2 * D) ** -0.5, 0.1875),
        "nu_log": draw_nu_log(jax.random.fold_in(streams_of[14], 71), 0),
        "theta_log": jnp.clip(jax.random.uniform(streams_of[8], (LAYERS, S), jnp.float32, -6.9, -1.2), -6.9, -1.2),
        "out_re": normal_values(streams_of[9], (LAYERS, S, D), (2 * S) ** -0.5, 0.25),
        "out_im": normal_values(streams_of[10], (LAYERS, S, D), (2 * S) ** -0.5, 0.25),
        "skip": normal_values(streams_of[11], (LAYERS, D), 0.5, 3.0, (), jnp.float32),
        "glu_w": normal_values(streams_of[12], (LAYERS, D, 2 * D), D ** -0.5, 0.25),
        "glu_b": normal_values(streams_of[13], (LAYERS, 2 * D), 0.3, 3.0, (), jnp.float32),
    }


EPS = 1e-05

@jax.custom_vjp
def low(v):
    return lax.optimization_barrier(v.astype(jnp.bfloat16)).astype(jnp.float32)

@jax.custom_vjp
def low_back(v):
    return v

def low_keep(v):
    return (low(v), None)

def low_pass(kept, grad):
    return (grad,)

def back_keep(v):
    return (v, None)

def back_low(kept, grad):
    return (low(grad),)
low.defvjp(low_keep, low_pass)
low_back.defvjp(back_keep, back_low)

def norm_affine(inputs, scale_row, offset_row):
    centre = lax.optimization_barrier(jnp.mean(inputs, axis=-1, keepdims=True))
    centred = inputs - centre
    spread = lax.optimization_barrier(jnp.mean(centred * centred, axis=-1, keepdims=True))
    return centred * lax.rsqrt(spread + EPS) * scale_row + offset_row

def decay_terms(nu_row, theta_row):
    speed = jnp.exp(nu_row)
    radius = jnp.exp(-speed)
    phase = jnp.exp(theta_row)
    return (radius * jnp.cos(phase), radius * jnp.sin(phase), jnp.sqrt(-jnp.expm1(-2.0 * speed)))

def combine(first, second):
    first_ar, first_ai, first_br, first_bi = first
    second_ar, second_ai, second_br, second_bi = second
    return (first_ar * second_ar - first_ai * second_ai, first_ar * second_ai + first_ai * second_ar, second_ar * first_br - second_ai * first_bi + second_br, second_ar * first_bi + second_ai * first_br + second_bi)

def glu_tail(gate_pair):
    middle = gate_pair.shape[-1] // 2
    return gate_pair[..., :middle] * jax.nn.sigmoid(gate_pair[..., middle:])

def layer_apply(stream, keep_mask, params):
    gain_row, bias_row, in_real, in_imag, nu_row, theta_row, out_real, out_imag, skip_row, glu_matrix, glu_offset = params
    highest = lax.Precision.HIGHEST
    normed = norm_affine(stream, gain_row, bias_row)
    normed_low = low(normed)
    proj_real = low_back(jnp.einsum('mrtd,ds->mrts', normed_low, in_real, precision=highest))
    proj_imag = low_back(jnp.einsum('mrtd,ds->mrts', normed_low, in_imag, precision=highest))
    lam_real, lam_imag, gamma_row = decay_terms(nu_row, theta_row)
    decay_real = keep_mask[..., None] * lam_real
    decay_imag = keep_mask[..., None] * lam_imag
    scanned = lax.associative_scan(combine, (decay_real, decay_imag, gamma_row * proj_real, gamma_row * proj_imag), axis=2)
    state_real = low(scanned[2])
    state_imag = low(scanned[3])
    mixed = low_back(jnp.einsum('mrts,sd->mrtd', state_real, out_real, precision=highest) - jnp.einsum('mrts,sd->mrtd', state_imag, out_imag, precision=highest) + skip_row * normed)
    activated = low(jax.nn.gelu(mixed))
    gate_pair = low_back(jnp.einsum('mrtd,de->mrte', activated, glu_matrix, precision=highest) + glu_offset)
    return stream + glu_tail(gate_pair)

def reference(tokens, cotangent, resets, ln_gain, ln_bias, in_re, in_im, nu_log, theta_log, out_re, out_im, skip, glu_w, glu_b):
    positions = jnp.arange(SEQLEN, dtype=jnp.int32)
    reset_hits = jnp.any(resets[:, :, None, :] == positions[None, None, :, None], axis=-1)
    keep_mask = jnp.where(reset_hits, 0.0, 1.0).astype(jnp.float32)
    weights = (ln_gain.astype(jnp.float32), ln_bias.astype(jnp.float32), in_re.astype(jnp.float32), in_im.astype(jnp.float32), nu_log.astype(jnp.float32), theta_log.astype(jnp.float32), out_re.astype(jnp.float32), out_im.astype(jnp.float32), skip.astype(jnp.float32), glu_w.astype(jnp.float32), glu_b.astype(jnp.float32))

    def forward(stream, weight_set):
        for layer_no in range(LAYERS):
            stream = layer_apply(stream, keep_mask, tuple((member[layer_no] for member in weight_set)))
        return stream
    outputs, pullback = jax.vjp(forward, tokens.astype(jnp.float32), weights)
    input_grad, weight_grads = pullback(cotangent.astype(jnp.float32))
    return (outputs, input_grad, weight_grads[0], weight_grads[1], weight_grads[2], weight_grads[3], weight_grads[4], weight_grads[5], weight_grads[6], weight_grads[7], weight_grads[8], weight_grads[9], weight_grads[10])
```

```python
import functools

import jax
import jax.numpy as jnp
from jax import lax
from jax.experimental import pallas as pl
from jax.experimental.pallas import tpu as pltpu
from jax.sharding import PartitionSpec as P

EPS = 1e-05
CHUNKS = 8
LANES = 128
VMEM_LIMIT = 56 << 20
F32 = jnp.float32
BF16 = jnp.bfloat16
GELU_C = 0.7978845608028654
GELU_A = 0.044715


def dot(left, right):
    return jnp.dot(left, right, preferred_element_type=F32)


def dot_right_t(left, right):
    return lax.dot_general(left, right, (((1,), (1,)), ((), ())), preferred_element_type=F32)


def dot_left_t(left, right):
    return lax.dot_general(left, right, (((0,), (0,)), ((), ())), preferred_element_type=F32)


def normalize(inputs):
    centre = jnp.mean(inputs, axis=-1, keepdims=True)
    centred = inputs - centre
    spread = jnp.mean(centred * centred, axis=-1, keepdims=True)
    scale = lax.rsqrt(spread + EPS)
    return centred * scale, scale


def sigmoid(gate):
    return 0.5 * jnp.tanh(0.5 * gate) + 0.5


def gelu_tanh(mixed):
    return jnp.tanh(GELU_C * (mixed + GELU_A * mixed * mixed * mixed))


def gelu_slope(mixed, bend):
    inner = GELU_C * (1.0 + (3.0 * GELU_A) * mixed * mixed)
    return 0.5 * (1.0 + bend) + 0.5 * mixed * (1.0 - bend * bend) * inner


def times(left, right):
    return (
        left[0] * right[0] - left[1] * right[1],
        left[0] * right[1] + left[1] * right[0],
    )


def to_steps(block):
    return jnp.swapaxes(block, 0, 1).reshape(-1, block.shape[-1])


def from_steps(rows, group):
    return jnp.swapaxes(rows.reshape(-1, group, rows.shape[-1]), 0, 1)


def wide(keep, states):
    return jnp.concatenate([keep] * (states // LANES), axis=1)


def split(value):
    half = value.shape[-1] // 2
    return value[:, :half], value[:, half:]


def spread_row(row, count):
    return jnp.broadcast_to(row, (count, row.shape[-1]))


def rows_of(step, group):
    return slice(step * group, (step + 1) * group)


def scan_up(drive_ref, keep_ref, lam, state, steps, group, store_ref=None):
    states = lam[0].shape[-1]
    for step in range(steps):
        rows = rows_of(step, group)
        keep = wide(keep_ref[rows, :], states)
        turned = times(lam, state)
        state = (
            keep * turned[0] + drive_ref[rows, :states],
            keep * turned[1] + drive_ref[rows, states:],
        )
        if store_ref is not None:
            store_ref[rows, :states] = state[0]
            store_ref[rows, states:] = state[1]
    return state


def chunk_totals(factor, value, count, reverse):
    pieces = []
    for seq_no in range(count):
        rows = rows_of(seq_no, CHUNKS)
        a = (factor[0][rows], factor[1][rows])
        x = (value[0][rows], value[1][rows])
        place = lax.broadcasted_iota(jnp.int32, a[0].shape, 0)
        shift = 1
        while shift < CHUNKS:
            turn = CHUNKS - shift if reverse else shift
            valid = place < CHUNKS - shift if reverse else place >= shift
            a_before = tuple(pltpu.roll(part, turn, 0) for part in a)
            x_before = tuple(pltpu.roll(part, turn, 0) for part in x)
            a_new = times(a_before, a)
            x_new = times(a, x_before)
            x = tuple(jnp.where(valid, new + old, old) for new, old in zip(x_new, x))
            a = tuple(jnp.where(valid, new, old) for new, old in zip(a_new, a))
            shift *= 2
        pieces.append((a, x))
    return pieces


def write_totals(pieces, pre_ref, end_ref, reverse):
    count = len(pieces)
    edge = 0 if reverse else CHUNKS - 1
    for seq_no, (a, x) in enumerate(pieces):
        rows = rows_of(seq_no, CHUNKS)
        a_all = jnp.concatenate(a, axis=1)
        x_all = jnp.concatenate(x, axis=1)
        pre_ref[0, rows, :] = a_all
        pre_ref[1, rows, :] = x_all
        end_ref[seq_no : seq_no + 1, :] = a_all[edge : edge + 1]
        end_ref[count + seq_no : count + seq_no + 1, :] = x_all[edge : edge + 1]


def chunk_carries(pre_ref, carry_ref, count, reverse):
    reals, imags = [], []
    for seq_no in range(count):
        rows = rows_of(seq_no, CHUNKS)
        a = split(pre_ref[0, rows, :])
        x = split(pre_ref[1, rows, :])
        carry = split(carry_ref[seq_no : seq_no + 1, :])
        place = lax.broadcasted_iota(jnp.int32, a[0].shape, 0)
        first = place == (CHUNKS - 1 if reverse else 0)
        turn = CHUNKS - 1 if reverse else 1
        a = tuple(pltpu.roll(part, turn, 0) for part in a)
        x = tuple(pltpu.roll(part, turn, 0) for part in x)
        moved = times(a, carry)
        reals.append(jnp.where(first, carry[0], x[0] + moved[0]))
        imags.append(jnp.where(first, carry[1], x[1] + moved[1]))
    return jnp.concatenate(reals, axis=0), jnp.concatenate(imags, axis=0)


def chunk_factor(vec_ref, kept):
    group = kept.shape[0]
    whole = split(vec_ref[5:6, :])
    keep = wide(kept, whole[0].shape[-1])
    return tuple(spread_row(part, group) * keep for part in whole)


def lam_rows(vec_ref, group, conj=False):
    lam = split(vec_ref[4:5, :])
    real, imag = spread_row(lam[0], group), spread_row(lam[1], group)
    return (real, -imag) if conj else (real, imag)


def column_sums(value):
    return jnp.sum(value.reshape(-1, 8, value.shape[-1]), axis=0)


def drive_of(normed_low, in_re_ref, in_im_ref, vec_ref):
    gamma = vec_ref[3:4, :]
    half = gamma.shape[-1] // 2
    real = dot(normed_low, in_re_ref[0]) * gamma[:, :half]
    imag = dot(normed_low, in_im_ref[0]) * gamma[:, half:]
    return real, imag


def first_kernel(
    dims, resets_ref, tok_ref, in_re_ref, in_im_ref, vec_ref,
    drive_ref, keep_ref, kept_ref, pre_ref, end_ref, state_ref,
):
    count, group, steps, length = dims
    at = pl.program_id(0)
    states = in_re_ref.shape[-1]

    @pl.when(at == 0)
    def _():
        state_ref[...] = jnp.zeros_like(state_ref)
        kept_ref[...] = jnp.ones_like(kept_ref)

    place = lax.broadcasted_iota(jnp.int32, (CHUNKS, LANES), 0) * length + at * steps
    for step in range(steps):
        for seq_no in range(count):
            keep = jnp.ones((CHUNKS, LANES), F32)
            for slot in range(resets_ref.shape[1]):
                keep = jnp.where(place + step == resets_ref[seq_no, slot], 0.0, keep)
            start = step * group + seq_no * CHUNKS
            keep_ref[start : start + CHUNKS, :] = keep
    normed, _ = normalize(to_steps(tok_ref[...].astype(F32)))
    normed = normed * vec_ref[0:1, :] + vec_ref[1:2, :]
    drive = drive_of(normed.astype(BF16), in_re_ref, in_im_ref, vec_ref)
    drive_ref[:, :states] = drive[0]
    drive_ref[:, states:] = drive[1]
    end_of_block(dims, drive_ref, keep_ref, kept_ref, vec_ref, state_ref, pre_ref, end_ref, True)


def end_of_block(dims, drive_ref, keep_ref, kept_ref, vec_ref, state_ref, pre_ref, end_ref, track):
    count, group, steps, _ = dims
    if track:
        kept = kept_ref[...]
        for step in range(steps):
            kept = kept * keep_ref[rows_of(step, group), :]
        kept_ref[...] = kept
    state = split(state_ref[...])
    state = scan_up(drive_ref, keep_ref, lam_rows(vec_ref, group), state, steps, group)
    state_ref[...] = jnp.concatenate(state, axis=1)

    @pl.when(pl.program_id(0) == pl.num_programs(0) - 1)
    def _():
        factor = chunk_factor(vec_ref, kept_ref[...])
        pieces = chunk_totals(factor, split(state_ref[...]), count, False)
        write_totals(pieces, pre_ref, end_ref, False)


def layer_out(h_ref, normed, out_re_ref, out_im_ref, vec_ref, glu_w_ref, vec_glu):
    states = out_re_ref.shape[1]
    width = out_re_ref.shape[2]
    h_low = h_ref[...].astype(BF16)
    mixed = (
        dot(h_low[:, :states], out_re_ref[0])
        - dot(h_low[:, states:], out_im_ref[0])
        + vec_ref[2:3, :] * normed
    )
    act = (0.5 * mixed * (1.0 + gelu_tanh(mixed))).astype(BF16)
    value = dot(act, glu_w_ref[0, :, :width]) + vec_ref[9:10, :]
    gate = dot(act, glu_w_ref[0, :, width:]) + vec_ref[10:11, :]
    return mixed, value, gate


def second_kernel(
    dims, tok_ref, drive_ref, keep_ref, kept_ref, pre_in_ref, carry_ref,
    vec_ref, out_re_ref, out_im_ref, glu_w_ref, vec2_ref, in_re_ref, in_im_ref,
    h_ref, edge_ref, mixed_ref, value_ref, gate_ref, stream_ref, drive2_ref, pre_ref, end_ref,
    state_ref, state2_ref,
):
    count, group, steps, _ = dims
    states = in_re_ref.shape[-1]

    @pl.when(pl.program_id(0) == 0)
    def _():
        state_ref[...] = jnp.concatenate(chunk_carries(pre_in_ref, carry_ref, count, False), axis=1)
        state2_ref[...] = jnp.zeros_like(state2_ref)

    edge_ref[0] = state_ref[...]
    state = scan_up(
        drive_ref, keep_ref, lam_rows(vec_ref, group), split(state_ref[...]), steps, group, h_ref
    )
    state_ref[...] = jnp.concatenate(state, axis=1)
    stream = to_steps(tok_ref[...].astype(F32))
    normed, _ = normalize(stream)
    normed = normed * vec_ref[0:1, :] + vec_ref[1:2, :]
    mixed, value, gate = layer_out(
        h_ref, normed, out_re_ref, out_im_ref, vec_ref, glu_w_ref, None
    )
    mixed_ref[...] = mixed.astype(BF16)
    value_ref[...] = value.astype(BF16)
    gate_ref[...] = gate.astype(BF16)
    stream = stream + value * sigmoid(gate)
    stream_ref[...] = stream
    normed, _ = normalize(stream)
    normed = normed * vec2_ref[0:1, :] + vec2_ref[1:2, :]
    drive = drive_of(normed.astype(BF16), in_re_ref, in_im_ref, vec2_ref)
    drive2_ref[:, :states] = drive[0]
    drive2_ref[:, states:] = drive[1]
    end_of_block(
        dims, drive2_ref, keep_ref, kept_ref, vec2_ref, state2_ref, pre_ref, end_ref, False
    )


def gate_back(
    upstream, value, gate, mixed, h_low, out_re_ref, out_im_ref, glu_w_ref, sums_ref, grads_ref
):
    states = out_re_ref.shape[1]
    width = out_re_ref.shape[2]
    sig = sigmoid(gate)
    value_grad = upstream * sig
    gate_grad = (value_grad * value * (1.0 - sig)).astype(BF16)
    value_grad = value_grad.astype(BF16)
    sums_ref[:, 4 * width : 5 * width] += column_sums(value_grad.astype(F32))
    sums_ref[:, 5 * width : 6 * width] += column_sums(gate_grad.astype(F32))
    act_grad = dot_right_t(value_grad, glu_w_ref[0, :, :width]) + dot_right_t(
        gate_grad, glu_w_ref[0, :, width:]
    )
    bend = gelu_tanh(mixed)
    act = (0.5 * mixed * (1.0 + bend)).astype(BF16)
    mixed_low = (act_grad * gelu_slope(mixed, bend)).astype(BF16)
    grads_ref[:width, :] += dot_left_t(act, value_grad)
    grads_ref[width : 2 * width, :] += dot_left_t(act, gate_grad)
    base = 2 * width
    grads_ref[base : base + states, :] += dot_left_t(h_low[:, :states], mixed_low)
    grads_ref[base + states : base + 2 * states, :] -= dot_left_t(h_low[:, states:], mixed_low)
    return mixed_low, dot_right_t(mixed_low, out_re_ref[0]), -dot_right_t(mixed_low, out_im_ref[0])


def scan_down(dh_ref, keep_ref, lam, state, steps, group, base=0):
    states = lam[0].shape[-1]
    for step in range(steps - 1, -1, -1):
        rows = rows_of(step, group)
        if not isinstance(base, int):
            rows = pl.ds(base + step * group, group)
        keep = wide(keep_ref[rows, :], states)
        g = (dh_ref[rows, :states] + state[0], dh_ref[rows, states:] + state[1])
        state = times(lam, (keep * g[0], keep * g[1]))
    return state


def third_kernel(
    dims, stream_ref, drive_ref, keep_ref, keep_all_ref, kept_ref, cot_ref, pre_in_ref, carry_ref,
    vec_ref, out_re_ref, out_im_ref, glu_w_ref,
    act_ref, h_ref, edge_ref, mixed_grad_ref, dh_ref, pre_ref, end_ref, grads_ref, sums_ref,
    state_ref, dh_all_ref,
):
    count, group, steps, length = dims
    at = pl.program_id(0)
    states = out_re_ref.shape[1]

    @pl.when(at == 0)
    def _():
        state_ref[...] = jnp.concatenate(chunk_carries(pre_in_ref, carry_ref, count, False), axis=1)
        grads_ref[...] = jnp.zeros_like(grads_ref)
        sums_ref[...] = jnp.zeros_like(sums_ref)

    edge_ref[0] = state_ref[...]
    state = scan_up(
        drive_ref, keep_ref, lam_rows(vec_ref, group), split(state_ref[...]), steps, group, h_ref
    )
    state_ref[...] = jnp.concatenate(state, axis=1)
    stream = stream_ref[...]
    normed, _ = normalize(stream)
    normed = normed * vec_ref[0:1, :] + vec_ref[1:2, :]
    mixed, value, gate = layer_out(
        h_ref, normed, out_re_ref, out_im_ref, vec_ref, glu_w_ref, None
    )
    act_ref[...] = from_steps(stream + value * sigmoid(gate), group)
    upstream = to_steps(cot_ref[...])
    mixed_low, dh_re, dh_im = gate_back(
        upstream, value, gate, mixed, h_ref[...].astype(BF16),
        out_re_ref, out_im_ref, glu_w_ref, sums_ref, grads_ref,
    )
    mixed_grad_ref[...] = mixed_low
    dh_ref[:, :states] = dh_re
    dh_ref[:, states:] = dh_im
    size = steps * group
    base = pl.multiple_of(at * size, size)
    dh_all_ref[pl.ds(base, size), :states] = dh_re
    dh_all_ref[pl.ds(base, size), states:] = dh_im

    @pl.when(at == pl.num_programs(0) - 1)
    def _():
        lam = lam_rows(vec_ref, group, True)
        zero = jnp.zeros((group, states), F32)
        unroll = 16

        def turn(k, state):
            start = pl.multiple_of((length // unroll - 1 - k) * (unroll * group), unroll * group)
            return scan_down(dh_all_ref, keep_all_ref, lam, state, unroll, group, start)

        state = lax.fori_loop(0, length // unroll, turn, (zero, zero))
        factor = chunk_factor(vec_ref, kept_ref[...])
        pieces = chunk_totals((factor[0], -factor[1]), state, count, True)
        write_totals(pieces, pre_ref, end_ref, True)


def adjoint_part(
    dims, dh_ref, keep_ref, h_ref, edge_ref, drive_ref, stream, mixed_low, vec_ref,
    in_re_ref, in_im_ref, state_ref, g_ref, sums_ref, lam_sums_ref, grads_ref, grads_at,
):
    _, group, steps, _ = dims
    states = in_re_ref.shape[-1]
    width = in_re_ref.shape[1]
    lam = lam_rows(vec_ref, group, True)
    state = split(state_ref[...])
    lam_re, lam_im = split(lam_sums_ref[:, : 2 * states])
    gam = lam_sums_ref[:, 2 * states :]
    for step in range(steps - 1, -1, -1):
        rows = rows_of(step, group)
        keep = wide(keep_ref[rows, :], states)
        g = (dh_ref[rows, :states] + state[0], dh_ref[rows, states:] + state[1])
        kg = (keep * g[0], keep * g[1])
        state = times(lam, kg)
        g_ref[rows, :states] = g[0]
        g_ref[rows, states:] = g[1]
        if step > 0:
            before = rows_of(step - 1, group)
            prev = (h_ref[before, :states], h_ref[before, states:])
        else:
            prev = (edge_ref[0, :, :states], edge_ref[0, :, states:])
        lam_re = lam_re + (kg[0] * prev[0] + kg[1] * prev[1])
        lam_im = lam_im + (kg[1] * prev[0] - kg[0] * prev[1])
        gam = gam + (g[0] * drive_ref[rows, :states] + g[1] * drive_ref[rows, states:])
    state_ref[...] = jnp.concatenate(state, axis=1)
    lam_sums_ref[...] = jnp.concatenate([lam_re, lam_im, gam], axis=1)

    xhat, scale = normalize(stream)
    normed = xhat * vec_ref[0:1, :] + vec_ref[1:2, :]
    normed_low = normed.astype(BF16)
    drive_low = (g_ref[...] * vec_ref[3:4, :]).astype(BF16)
    grads_ref[grads_at : grads_at + width, :] += dot_left_t(normed_low, drive_low)
    mixed_wide = mixed_low.astype(F32)
    normed_grad = (
        dot_right_t(drive_low[:, :states], in_re_ref[0])
        + dot_right_t(drive_low[:, states:], in_im_ref[0])
        + vec_ref[2:3, :] * mixed_wide
    )
    sums_ref[:, :width] += column_sums(normed_grad * xhat)
    sums_ref[:, width : 2 * width] += column_sums(normed_grad)
    sums_ref[:, 3 * width : 4 * width] += column_sums(mixed_wide * normed)
    inner = normed_grad * vec_ref[0:1, :]
    middle = jnp.mean(inner, axis=-1, keepdims=True)
    along = jnp.mean(inner * xhat, axis=-1, keepdims=True)
    return scale * (inner - middle - xhat * along)


def finish_sums(small_ref, base, sums_ref, lam_sums_ref, vec_ref, states, width):
    total = jnp.sum(sums_ref[...], axis=0, keepdims=True)
    lam_total = jnp.sum(lam_sums_ref[...], axis=0, keepdims=True)
    lam_re, lam_im = lam_total[:, :states], lam_total[:, states : 2 * states]
    gam = lam_total[:, 2 * states :]
    nu_grad = (
        vec_ref[6:7, :states] * lam_re
        + vec_ref[6:7, states:] * lam_im
        + vec_ref[7:8, :states] * gam
    )
    theta_grad = vec_ref[8:9, :states] * lam_re + vec_ref[8:9, states:] * lam_im
    small_ref[base : base + 1, :] = total[:, :width]
    small_ref[base + 1 : base + 2, :] = total[:, width : 2 * width]
    small_ref[base + 2 : base + 3, :] = jnp.concatenate([nu_grad, theta_grad], axis=1)
    small_ref[base + 3 : base + 4, :] = total[:, 3 * width : 4 * width]
    small_ref[base + 4 : base + 5, :] = total[:, 4 * width : 5 * width]
    small_ref[base + 5 : base + 6, :] = total[:, 5 * width : 6 * width]


def fourth_kernel(
    dims, dh2_ref, keep_ref, kept_ref, h2_ref, edge2_ref, drive2_ref, stream_ref, mixed2_ref,
    cot_ref, sums2_ref, pre_in_ref, carry_ref, vec2_ref, in_re_ref, in_im_ref,
    value_ref, gate_ref, mixed_ref, h_ref, vec_ref, out_re_ref, out_im_ref, glu_w_ref,
    up_ref, mixed_grad_ref, dh_ref, pre_ref, end_ref, grads_ref, sums_ref, small_ref,
    state2_ref, state_ref, g_ref, run2_ref, lam2_ref,
):
    count, group, steps, _ = dims
    states = in_re_ref.shape[-1]
    width = in_re_ref.shape[1]
    at = pl.program_id(0)

    @pl.when(at == 0)
    def _():
        carries = chunk_carries(pre_in_ref, carry_ref, count, True)
        state2_ref[...] = jnp.concatenate(carries, axis=1)
        state_ref[...] = jnp.zeros_like(state_ref)
        grads_ref[...] = jnp.zeros_like(grads_ref)
        sums_ref[...] = jnp.zeros_like(sums_ref)
        run2_ref[...] = sums2_ref[...]
        lam2_ref[...] = jnp.zeros_like(lam2_ref)

    stream_grad = adjoint_part(
        dims, dh2_ref, keep_ref, h2_ref, edge2_ref, drive2_ref, stream_ref[...], mixed2_ref[...],
        vec2_ref, in_re_ref, in_im_ref, state2_ref, g_ref, run2_ref, lam2_ref, grads_ref,
        2 * width + 2 * states,
    )
    upstream = to_steps(cot_ref[...]) + stream_grad
    up_ref[...] = upstream
    mixed_low, dh_re, dh_im = gate_back(
        upstream, value_ref[...].astype(F32), gate_ref[...].astype(F32),
        mixed_ref[...].astype(F32), h_ref[...].astype(BF16),
        out_re_ref, out_im_ref, glu_w_ref, sums_ref, grads_ref,
    )
    mixed_grad_ref[...] = mixed_low
    dh_ref[:, :states] = dh_re
    dh_ref[:, states:] = dh_im
    lam = lam_rows(vec_ref, group, True)
    state = scan_down(dh_ref, keep_ref, lam, split(state_ref[...]), steps, group)
    state_ref[...] = jnp.concatenate(state, axis=1)

    @pl.when(at == pl.num_programs(0) - 1)
    def _():
        factor = chunk_factor(vec_ref, kept_ref[...])
        pieces = chunk_totals((factor[0], -factor[1]), split(state_ref[...]), count, True)
        write_totals(pieces, pre_ref, end_ref, True)
        small_ref[...] = jnp.zeros_like(small_ref)
        finish_sums(small_ref, 0, run2_ref, lam2_ref, vec2_ref, states, width)


def fifth_kernel(
    dims, dh_ref, keep_ref, h_ref, edge_ref, drive_ref, tok_ref, mixed_ref, up_ref, sums_in_ref,
    small_in_ref, pre_in_ref, carry_ref, vec_ref, in_re_ref, in_im_ref,
    grad_ref, grads_ref, small_ref, state_ref, g_ref, sums_ref, lam_ref,
):
    count, group, steps, _ = dims
    states = in_re_ref.shape[-1]
    width = in_re_ref.shape[1]
    at = pl.program_id(0)

    @pl.when(at == 0)
    def _():
        carries = chunk_carries(pre_in_ref, carry_ref, count, True)
        state_ref[...] = jnp.concatenate(carries, axis=1)
        grads_ref[...] = jnp.zeros_like(grads_ref)
        sums_ref[...] = sums_in_ref[...]
        lam_ref[...] = jnp.zeros_like(lam_ref)

    stream_grad = adjoint_part(
        dims, dh_ref, keep_ref, h_ref, edge_ref, drive_ref, to_steps(tok_ref[...].astype(F32)),
        mixed_ref[...], vec_ref, in_re_ref, in_im_ref, state_ref, g_ref, sums_ref, lam_ref,
        grads_ref, 0,
    )
    grad_ref[...] = from_steps(up_ref[...] + stream_grad, group)

    @pl.when(at == pl.num_programs(0) - 1)
    def _():
        small_ref[...] = small_in_ref[...]
        finish_sums(small_ref, 8, sums_ref, lam_ref, vec_ref, states, width)


def decay_rows(gain, bias, skip, nu_log, theta_log, glu_b, length):
    speed = jnp.exp(nu_log)
    phase = jnp.exp(theta_log)
    radius = jnp.exp(-speed)
    lam_re, lam_im = radius * jnp.cos(phase), radius * jnp.sin(phase)
    square = -jnp.expm1(-2.0 * speed)
    gamma = jnp.sqrt(square)
    far = jnp.exp(-speed * length)
    far_re, far_im = far * jnp.cos(phase * length), far * jnp.sin(phase * length)

    def pair(left, right):
        return jnp.concatenate([left, right], axis=-1)

    width = gain.shape[-1]
    rows = [
        gain,
        bias,
        skip,
        pair(gamma, gamma),
        pair(lam_re, lam_im),
        pair(far_re, far_im),
        pair(-speed * lam_re, -speed * lam_im),
        pair(speed * jnp.exp(-2.0 * speed) / square, jnp.zeros_like(speed)),
        pair(-phase * lam_im, phase * lam_re),
        glu_b[:, :width],
        glu_b[:, width:],
    ]
    rows += [jnp.zeros_like(gain)] * (16 - len(rows))
    return jnp.stack(rows, axis=1)


def combine_rows(first, second):
    count = first.shape[0] // 2
    first_a, first_x = split(first[:count]), split(first[count:])
    second_a, second_x = split(second[:count]), split(second[count:])
    factor = times(first_a, second_a)
    moved = times(second_a, first_x)
    value = (moved[0] + second_x[0], moved[1] + second_x[1])
    return jnp.concatenate(
        [jnp.concatenate(factor, axis=1), jnp.concatenate(value, axis=1)], axis=0
    )


def entering(total, axis, reverse):
    size, index = lax.axis_size(axis), lax.axis_index(axis)
    count = total.shape[0] // 2
    before = None
    bit = 1
    while bit < size:
        other = lax.ppermute(total, axis, [(i, i ^ bit) for i in range(size)])
        later = (index & bit) == 0 if reverse else (index & bit) != 0
        if before is None:
            joined = other
            identity = jnp.zeros_like(other).at[:count, : other.shape[1] // 2].set(1.0)
            before = jnp.where(later, joined, identity)
        else:
            before = jnp.where(later, combine_rows(other, before), before)
        if 2 * bit < size:
            total = jnp.where(later, combine_rows(other, total), combine_rows(total, other))
        bit *= 2
    return before[count:]


def flip(value, axes, sizes, bit):
    total = sizes[0] * sizes[1]
    return lax.ppermute(value, axes, [(i, i ^ (1 << bit)) for i in range(total)])


def linear_index(axes, sizes):
    return lax.axis_index(axes[0]) * sizes[1] + lax.axis_index(axes[1])


def reduce_parts(parts, orders, axes, sizes):
    index = linear_index(axes, sizes)
    for stage in range(len(orders[0])):
        sent = []
        for part, order in zip(parts, orders):
            upper = ((index >> order[stage]) & 1) == 1
            half = part.shape[0] // 2
            low, high = part[:half], part[half:]
            sent.append(
                (jnp.where(upper, high, low), flip(jnp.where(upper, low, high), axes, sizes, order[stage]))
            )
        parts = [mine + other for mine, other in sent]
    return parts


def gather_parts(parts, orders, axes, sizes):
    index = linear_index(axes, sizes)
    for stage in range(len(orders[0]) - 1, -1, -1):
        got = []
        for part, order in zip(parts, orders):
            upper = ((index >> order[stage]) & 1) == 1
            other = flip(part, axes, sizes, order[stage])
            got.append(
                jnp.concatenate(
                    [jnp.where(upper, other, part), jnp.where(upper, part, other)], axis=0
                )
            )
        parts = got
    return parts


def all_sum(value, axes, sizes):
    bits = (sizes[0] * sizes[1]).bit_length() - 1
    first = reduce_parts([value], [[0]], axes, sizes)[0]
    half = first.shape[0] // 2
    rest = list(range(1, bits))
    swapped = [rest[1], rest[0]] + rest[2:]
    orders = [rest, swapped]
    parts = reduce_parts([first[:half], first[half:]], orders, axes, sizes)
    parts = gather_parts(parts, orders, axes, sizes)
    return gather_parts([jnp.concatenate(parts, axis=0)], [[0]], axes, sizes)[0]


def all_sum_small(value, axes, sizes):
    bits = (sizes[0] * sizes[1]).bit_length() - 1
    for bit in range(bits):
        value = value + flip(value, axes, sizes, bit)
    return value


def shards(
    sizes, tokens, cotangent, resets, ln_gain, ln_bias, in_re, in_im, nu_log, theta_log,
    out_re, out_im, skip, glu_w, glu_b,
):
    axes = ("seq", "row")
    micro, rows_here, span, width = tokens.shape
    states = nu_log.shape[-1]
    count = micro * rows_here
    group = count * CHUNKS
    length = span // CHUNKS
    steps = 32 if length % 32 == 0 else length
    blocks = length // steps
    size = steps * group
    total = length * group
    dims = (count, group, steps, length)

    tok = tokens.reshape(group, length, width)
    cot = cotangent.reshape(group, length, width)
    starts = resets.reshape(count, -1) - lax.axis_index("seq") * span
    vec = decay_rows(ln_gain, ln_bias, skip, nu_log, theta_log, glu_b, length)

    def shape(*dims_, dtype=F32):
        return jax.ShapeDtypeStruct(dims_, dtype)

    def streamed(lanes, back=False):
        if back:
            return pl.BlockSpec((size, lanes), lambda i: (blocks - 1 - i, 0))
        return pl.BlockSpec((size, lanes), lambda i: (i, 0))

    def natural(back=False):
        if back:
            return pl.BlockSpec((group, steps, width), lambda i: (0, blocks - 1 - i, 0))
        return pl.BlockSpec((group, steps, width), lambda i: (0, i, 0))

    def edges(back=False):
        if back:
            return pl.BlockSpec((1, group, 2 * states), lambda i: (blocks - 1 - i, 0, 0))
        return pl.BlockSpec((1, group, 2 * states), lambda i: (i, 0, 0))

    def fixed(*dims_):
        return pl.BlockSpec(
            dims_, lambda i: (0,) * len(dims_), pipeline_mode=pl.Buffered(buffer_count=1)
        )

    def held(*dims_):
        return pl.BlockSpec(dims_, lambda i: (0,) * len(dims_))

    def layer(no, *dims_):
        return pl.BlockSpec(
            (1,) + dims_, lambda i: (no,) + (0,) * len(dims_),
            pipeline_mode=pl.Buffered(buffer_count=1),
        )

    def vec_of(no):
        return pl.BlockSpec(
            (None, 16, width), lambda i: (no, 0, 0), pipeline_mode=pl.Buffered(buffer_count=1)
        )

    def in_specs_of(no):
        return [layer(no, width, states), layer(no, width, states)]

    def out_specs_of(no):
        return [layer(no, states, width), layer(no, states, width)]

    def glu_spec(no):
        return layer(no, width, 2 * width)

    def call(kernel, in_specs, out_specs, out_shape, scratch):
        return pl.pallas_call(
            functools.partial(kernel, dims),
            grid=(blocks,),
            in_specs=in_specs,
            out_specs=out_specs,
            out_shape=out_shape,
            scratch_shapes=scratch,
            compiler_params=pltpu.CompilerParams(vmem_limit_bytes=VMEM_LIMIT),
        )

    two = 2 * states
    pre_spec, pre_shape = held(2, group, two), shape(2, group, two)
    end_spec, end_shape = held(2 * count, two), shape(2 * count, two)
    pre_in, carry_in = fixed(2, group, two), fixed(count, two)
    state = pltpu.VMEM((group, two), F32)

    drive1, keep, kept, pre1, end1 = call(
        first_kernel,
        [pl.BlockSpec(memory_space=pltpu.SMEM), natural()] + in_specs_of(0) + [vec_of(0)],
        [streamed(two), streamed(LANES), held(group, LANES), pre_spec, end_spec],
        [shape(total, two), shape(total, LANES), shape(group, LANES), pre_shape, end_shape],
        [state],
    )(starts, tok, in_re, in_im, vec)
    carry1 = entering(end1, "seq", False)

    h1, edge1, mixed1, value1, gate1, stream1, drive2, pre2, end2 = call(
        second_kernel,
        [natural(), streamed(two), streamed(LANES), fixed(group, LANES), pre_in, carry_in, vec_of(0)]
        + out_specs_of(0) + [glu_spec(0), vec_of(1)] + in_specs_of(1),
        [streamed(two), edges(), streamed(width), streamed(width), streamed(width), streamed(width),
         streamed(two), pre_spec, end_spec],
        [shape(total, two), shape(blocks, group, two), shape(total, width, dtype=BF16),
         shape(total, width, dtype=BF16), shape(total, width, dtype=BF16), shape(total, width),
         shape(total, two), pre_shape, end_shape],
        [state, state],
    )(tok, drive1, keep, kept, pre1, carry1, vec, out_re, out_im, glu_w, vec, in_re, in_im)
    carry2 = entering(end2, "seq", False)

    sums_spec, sums_shape = held(8, 6 * width), shape(8, 6 * width)
    act, h2, edge2, mixed_grad2, dh2, back2, back_end2, grads_a, sums2 = call(
        third_kernel,
        [streamed(width), streamed(two), streamed(LANES), fixed(total, LANES), fixed(group, LANES),
         natural(), pre_in, carry_in, vec_of(1)] + out_specs_of(1) + [glu_spec(1)],
        [natural(), streamed(two), edges(), streamed(width), streamed(two), pre_spec, end_spec,
         held(2 * width + two, width), sums_spec],
        [shape(group, length, width), shape(total, two), shape(blocks, group, two),
         shape(total, width, dtype=BF16), shape(total, two), pre_shape, end_shape,
         shape(2 * width + two, width), sums_shape],
        [state, pltpu.VMEM((total, two), F32)],
    )(stream1, drive2, keep, keep, kept, cot, pre2, carry2, vec, out_re, out_im, glu_w)
    back_carry2 = entering(back_end2, "seq", True)
    summed_a = all_sum(grads_a, axes, sizes)

    rows_b = 2 * width + two + width
    lam_sums = pltpu.VMEM((group, 3 * states), F32)
    run_sums = pltpu.VMEM((8, 6 * width), F32)
    up1, mixed_grad1, dh1, back1, back_end1, grads_b, sums1, small2 = call(
        fourth_kernel,
        [streamed(two, True), streamed(LANES, True), fixed(group, LANES), streamed(two, True),
         edges(True), streamed(two, True), streamed(width, True), streamed(width, True),
         natural(True), fixed(8, 6 * width), pre_in, carry_in, vec_of(1)] + in_specs_of(1)
        + [streamed(width, True), streamed(width, True), streamed(width, True), streamed(two, True),
           vec_of(0)] + out_specs_of(0) + [glu_spec(0)],
        [streamed(width, True), streamed(width, True), streamed(two, True), pre_spec, end_spec,
         held(rows_b, width), sums_spec, held(16, width)],
        [shape(total, width), shape(total, width, dtype=BF16), shape(total, two), pre_shape,
         end_shape, shape(rows_b, width), sums_shape, shape(16, width)],
        [state, state, pltpu.VMEM((size, two), F32), run_sums, lam_sums],
    )(dh2, keep, kept, h2, edge2, drive2, stream1, mixed_grad2, cot, sums2, back2, back_carry2, vec,
      in_re, in_im, value1, gate1, mixed1, h1, vec, out_re, out_im, glu_w)
    back_carry1 = entering(back_end1, "seq", True)
    summed_b = all_sum(grads_b, axes, sizes)

    input_grad, grads_c, small = call(
        fifth_kernel,
        [streamed(two, True), streamed(LANES, True), streamed(two, True), edges(True),
         streamed(two, True), natural(True), streamed(width, True), streamed(width, True),
         fixed(8, 6 * width), fixed(16, width), pre_in, carry_in, vec_of(0)] + in_specs_of(0),
        [natural(True), held(width, two), held(16, width)],
        [shape(group, length, width), shape(width, two), shape(16, width)],
        [state, pltpu.VMEM((size, two), F32), run_sums, lam_sums],
    )(dh1, keep, h1, edge1, drive1, tok, mixed_grad1, up1, sums1, small2, back1, back_carry1, vec,
      in_re, in_im)
    summed_c = all_sum(grads_c, axes, sizes)
    small = all_sum_small(small, axes, sizes)

    def two_layers(first, second):
        return jnp.stack([first, second])

    outs_at = 2 * width
    ins_at = outs_at + two
    small = small.reshape(2, 8, width)[::-1]
    grad_in2 = summed_b[ins_at:]
    return (
        act.reshape(tokens.shape),
        input_grad.reshape(tokens.shape),
        small[:, 0],
        small[:, 1],
        two_layers(summed_c[:, :states], grad_in2[:, :states]),
        two_layers(summed_c[:, states:], grad_in2[:, states:]),
        small[:, 2, :states],
        small[:, 2, states:],
        two_layers(summed_b[outs_at : outs_at + states], summed_a[outs_at : outs_at + states]),
        two_layers(summed_b[outs_at + states : ins_at], summed_a[outs_at + states : ins_at]),
        small[:, 3],
        jnp.concatenate(
            [
                two_layers(summed_b[:width], summed_a[:width]),
                two_layers(summed_b[width:outs_at], summed_a[width:outs_at]),
            ],
            axis=-1,
        ),
        small[:, 4:6].reshape(2, 2 * width),
    )


def solution(mesh):
    sizes = (mesh.shape["seq"], mesh.shape["row"])
    split_rows = P(None, "row", "seq", None)
    in_specs = (split_rows, split_rows, P(None, "row", None)) + (P(),) * 11
    out_specs = (split_rows, split_rows) + (P(),) * 11
    return jax.shard_map(
        functools.partial(shards, sizes),
        mesh=mesh,
        in_specs=in_specs,
        out_specs=out_specs,
        check_vma=False,
    )
```

```python
import functools

import jax
import jax.numpy as jnp
from jax import lax
from jax.experimental import pallas as pl
from jax.experimental.pallas import tpu as pltpu
from jax.sharding import PartitionSpec as P

EPS = 1e-05
CHUNKS = 8
LANES = 128
VMEM_LIMIT = 28 << 20
UNROLL = True
STEPS = 32
F32 = jnp.float32
BF16 = jnp.bfloat16
GELU_C = 0.7978845608028654
GELU_A = 0.044715


def dot(left, right):
    return jnp.dot(left, right, preferred_element_type=F32)


def dot_right_t(left, right):
    return lax.dot_general(left, right, (((1,), (1,)), ((), ())), preferred_element_type=F32)


def dot_left_t(left, right):
    return lax.dot_general(left, right, (((0,), (0,)), ((), ())), preferred_element_type=F32)


def normalize(inputs):
    centre = jnp.mean(inputs, axis=-1, keepdims=True)
    centred = inputs - centre
    spread = jnp.mean(centred * centred, axis=-1, keepdims=True)
    scale = lax.rsqrt(spread + EPS)
    return centred * scale, scale


def sigmoid(gate):
    return 0.5 * jnp.tanh(0.5 * gate) + 0.5


def gelu_tanh(mixed):
    return jnp.tanh(GELU_C * (mixed + GELU_A * mixed * mixed * mixed))


def gelu_slope(mixed, bend):
    inner = GELU_C * (1.0 + (3.0 * GELU_A) * mixed * mixed)
    return 0.5 * (1.0 + bend) + 0.5 * mixed * (1.0 - bend * bend) * inner


def one_minus_exp(value):
    series = jnp.ones_like(value)
    for term in range(11, 1, -1):
        series = 1.0 - value * series * (1.0 / term)
    return jnp.where(value < 0.5, value * series, 1.0 - jnp.exp(-value))


def times(left, right):
    return (
        left[0] * right[0] - left[1] * right[1],
        left[0] * right[1] + left[1] * right[0],
    )


def to_steps(block):
    return jnp.swapaxes(block, 0, 1).reshape(-1, block.shape[-1])


def from_steps(rows, group):
    return jnp.swapaxes(rows.reshape(-1, group, rows.shape[-1]), 0, 1)


def wide(keep, states):
    return jnp.concatenate([keep] * (states // LANES), axis=1)


def split(value):
    half = value.shape[-1] // 2
    return value[:, :half], value[:, half:]


def join(pair):
    return jnp.concatenate(pair, axis=1)


def spread_row(row, count):
    return jnp.broadcast_to(row, (count, row.shape[-1]))


def rows_of(step, group):
    return slice(step * group, (step + 1) * group)


def rows_at(base, step, group):
    if isinstance(base, int):
        return slice(base + step * group, base + (step + 1) * group)
    return pl.ds(pl.multiple_of(base + step * group, group), group)


def loop(count, body, carry):
    if not UNROLL:
        return lax.fori_loop(0, count, body, carry)
    for turn in range(count):
        carry = body(turn, carry)
    return carry


def maybe(condition, action):
    if isinstance(condition, bool):
        if condition:
            action()
    else:
        pl.when(condition)(action)


def scan_up(drive_ref, keep_ref, base, lam, state, steps, group, h_ref=None):
    states = lam[0].shape[-1]
    for step in range(steps):
        rows = rows_at(base, step, group)
        keep = wide(keep_ref[rows, :], states)
        turned = times(lam, state)
        state = (
            keep * turned[0] + drive_ref[rows, :states],
            keep * turned[1] + drive_ref[rows, states:],
        )
        if h_ref is not None:
            later = rows_at(base, step + 1, group)
            h_ref[later, :states] = state[0]
            h_ref[later, states:] = state[1]
    return state


def scan_down(dh_ref, keep_ref, base, lam, state, steps, group):
    states = lam[0].shape[-1]
    for step in range(steps - 1, -1, -1):
        rows = rows_at(base, step, group)
        keep = wide(keep_ref[rows, :], states)
        g = (dh_ref[rows, :states] + state[0], dh_ref[rows, states:] + state[1])
        state = times(lam, (keep * g[0], keep * g[1]))
    return state


def chunk_totals(factor, value, count, reverse):
    pieces = []
    for seq_no in range(count):
        rows = rows_of(seq_no, CHUNKS)
        a = (factor[0][rows], factor[1][rows])
        x = (value[0][rows], value[1][rows])
        place = lax.broadcasted_iota(jnp.int32, a[0].shape, 0)
        shift = 1
        while shift < CHUNKS:
            turn = CHUNKS - shift if reverse else shift
            valid = place < CHUNKS - shift if reverse else place >= shift
            a_before = tuple(pltpu.roll(part, turn, 0) for part in a)
            x_before = tuple(pltpu.roll(part, turn, 0) for part in x)
            a_new = times(a_before, a)
            x_new = times(a, x_before)
            x = tuple(jnp.where(valid, new + old, old) for new, old in zip(x_new, x))
            a = tuple(jnp.where(valid, new, old) for new, old in zip(a_new, a))
            shift *= 2
        pieces.append((a, x))
    return pieces


def write_totals(pieces, pre_ref, end_ref, reverse):
    count = len(pieces)
    edge = 0 if reverse else CHUNKS - 1
    for seq_no, (a, x) in enumerate(pieces):
        rows = rows_of(seq_no, CHUNKS)
        a_all = join(a)
        x_all = join(x)
        pre_ref[0, rows, :] = a_all
        pre_ref[1, rows, :] = x_all
        end_ref[seq_no : seq_no + 1, :] = a_all[edge : edge + 1]
        end_ref[count + seq_no : count + seq_no + 1, :] = x_all[edge : edge + 1]


def joined(first, second):
    count = first.shape[0] // 2
    second_a = split(second[:count])
    factor = times(split(first[:count]), second_a)
    moved = times(second_a, split(first[count:]))
    second_x = split(second[count:])
    value = (moved[0] + second_x[0], moved[1] + second_x[1])
    return jnp.concatenate([join(factor), join(value)], axis=0)


def combine_kernel(first_round, reverse, place_ref, at, total_ref, other_ref, *refs):
    later = place_ref[at] == (0 if reverse else 1)
    total, other = total_ref[...], other_ref[...]
    if first_round:
        total_out, before_out = refs
        half = total.shape[0] // 2
        row = lax.broadcasted_iota(jnp.int32, total.shape, 0)
        lane = lax.broadcasted_iota(jnp.int32, total.shape, 1)
        identity = jnp.where((row < half) & (lane < total.shape[1] // 2), 1.0, 0.0)
        before_out[...] = jnp.where(later, other, identity)
    else:
        before_ref, total_out, before_out = refs
        before = before_ref[...]
        before_out[...] = jnp.where(later, joined(other, before), before)
    total_out[...] = jnp.where(later, joined(other, total), joined(total, other))


def last_carry(place_ref, reverse, before_ref, other_ref):
    before, other = before_ref[...], other_ref[...]
    count = before.shape[0] // 2
    later = place_ref[place_ref.shape[0] - 1] == (0 if reverse else 1)
    return jnp.where(later, joined(other, before), before)[count:]


def chunk_carries(pre_ref, entered, count, reverse):
    reals, imags = [], []
    for seq_no in range(count):
        rows = rows_of(seq_no, CHUNKS)
        a = split(pre_ref[0, rows, :])
        x = split(pre_ref[1, rows, :])
        carry = split(entered[seq_no : seq_no + 1, :])
        place = lax.broadcasted_iota(jnp.int32, a[0].shape, 0)
        first = place == (CHUNKS - 1 if reverse else 0)
        turn = CHUNKS - 1 if reverse else 1
        a = tuple(pltpu.roll(part, turn, 0) for part in a)
        x = tuple(pltpu.roll(part, turn, 0) for part in x)
        moved = times(a, carry)
        reals.append(jnp.where(first, carry[0], x[0] + moved[0]))
        imags.append(jnp.where(first, carry[1], x[1] + moved[1]))
    return jnp.concatenate(reals, axis=0), jnp.concatenate(imags, axis=0)


def chunk_factor(vec_ref, no, kept, conj=False):
    group = kept.shape[0]
    whole = split(vec_ref[no, 5:6, :])
    keep = wide(kept, whole[0].shape[-1])
    real, imag = tuple(spread_row(part, group) * keep for part in whole)
    return (real, -imag) if conj else (real, imag)


def lam_rows(vec_ref, no, group, conj=False):
    lam = split(vec_ref[no, 4:5, :])
    real, imag = spread_row(lam[0], group), spread_row(lam[1], group)
    return (real, -imag) if conj else (real, imag)


def halve(place_ref, whole_ref, kept_ref, sent_ref):
    half = kept_ref.shape[0]
    mine = place_ref[0]
    kept_ref[...] = whole_ref[pl.ds(pl.multiple_of(mine * half, 8), half), :]
    sent_ref[...] = whole_ref[pl.ds(pl.multiple_of((1 - mine) * half, 8), half), :]


def column_sums(value):
    return jnp.sum(value.reshape(-1, 8, value.shape[-1]), axis=0)


def norm_affine(stream, vec_ref, no):
    xhat, scale = normalize(stream)
    return xhat * vec_ref[no, 0:1, :] + vec_ref[no, 1:2, :], xhat, scale


def write_drive(drive_ref, rows, normed_low, in_re_ref, in_im_ref, vec_ref, no):
    gamma = split(vec_ref[no, 3:4, :])
    states = gamma[0].shape[-1]
    drive_ref[rows, :states] = dot(normed_low, in_re_ref[...]) * gamma[0]
    drive_ref[rows, states:] = dot(normed_low, in_im_ref[...]) * gamma[1]


def time_block(ref, block, steps):
    if isinstance(block, int):
        return ref.at[:, block * steps : (block + 1) * steps, :]
    return ref.at[:, pl.ds(pl.multiple_of(block * steps, steps), steps), :]


class Weights:
    def __init__(self, sems, *copies):
        self.copies = [
            pltpu.make_async_copy(source if no is None else source.at[no], target, sems.at[at])
            for at, (source, no, target) in enumerate(copies)
        ]
        for copy in self.copies:
            copy.start()

    def wait(self, first=0, last=None):
        for copy in self.copies[first:last]:
            copy.wait()


class RowsOut:
    def __init__(self, buffer, target, sems):
        self.buffer, self.target, self.sems = buffer, target, sems
        self.running = []

    def send(self, start, end):
        copy = pltpu.make_async_copy(
            self.buffer.at[start:end], self.target.at[start:end], self.sems.at[len(self.running)]
        )
        copy.start()
        self.running.append(copy)

    def finish(self):
        for copy in self.running:
            copy.wait()


class RowsIn:
    def __init__(self, source, buffer, sems, size, blocks, skip=0):
        self.copies = {}
        for turn, at in enumerate(range(blocks - 1, -1, -1)):
            start = at * size
            self.copies[at] = pltpu.make_async_copy(
                source.at[skip + start : skip + start + size],
                buffer.at[start : start + size],
                sems.at[turn],
            )

    def start(self, at):
        self.copies[at].start()

    def wait(self, at):
        self.copies[at].wait()


class Fetch:
    def __init__(self, source, buffer, sems, steps, blocks, down=False):
        self.source, self.buffer, self.sems = source, buffer, sems
        self.steps, self.blocks, self.down = steps, blocks, down
        self.copy(0).start()

    def copy(self, turn):
        block = self.blocks - 1 - turn if self.down else turn
        slot = turn % 2
        return pltpu.make_async_copy(
            time_block(self.source, block, self.steps), self.buffer.at[slot], self.sems.at[slot]
        )

    def get(self, turn):
        maybe(turn + 1 < self.blocks, lambda: self.copy(turn + 1).start())

        self.copy(turn).wait()
        return to_steps(self.buffer[turn % 2].astype(F32))


class Store:
    def __init__(self, target, buffer, sems, steps, blocks, down=False):
        self.target, self.buffer, self.sems = target, buffer, sems
        self.steps, self.blocks, self.down = steps, blocks, down

    def copy(self, turn):
        block = self.blocks - 1 - turn if self.down else turn
        slot = turn % 2
        return pltpu.make_async_copy(
            self.buffer.at[slot], time_block(self.target, block, self.steps), self.sems.at[slot]
        )

    def put(self, turn, rows, group):
        maybe(turn >= 2, lambda: self.copy(turn - 2).wait())

        self.buffer[turn % 2] = from_steps(rows, group)
        self.copy(turn).start()

    def finish(self):
        for turn in range(max(self.blocks - 2, 0), self.blocks):
            self.copy(turn).wait()


def decay_rows(vec_ref, no, gain, bias, skip, nu_log, theta_log, glu_b, length):
    speed = jnp.exp(nu_log)
    phase = jnp.exp(theta_log)
    radius = jnp.exp(-speed)
    lam_re, lam_im = radius * jnp.cos(phase), radius * jnp.sin(phase)
    square = one_minus_exp(2.0 * speed)
    gamma = jnp.sqrt(square)
    far = jnp.exp(-speed * length)
    far_re, far_im = far * jnp.cos(phase * length), far * jnp.sin(phase * length)
    width = gain.shape[-1]
    rows = [
        gain,
        bias,
        skip,
        join([gamma, gamma]),
        join([lam_re, lam_im]),
        join([far_re, far_im]),
        join([-speed * lam_re, -speed * lam_im]),
        join([speed * jnp.exp(-2.0 * speed) / square, jnp.zeros_like(speed)]),
        join([-phase * lam_im, phase * lam_re]),
        glu_b[:, :width],
        glu_b[:, width:],
    ]
    for at, row in enumerate(rows):
        vec_ref[no, at : at + 1, :] = row


def first_kernel(
    dims, resets_ref, offset_ref, tok_ref, in_re_far, in_im_far,
    gain_far, bias_far, skip_far, nu_far, theta_far, glu_b_far,
    drive_ref, keep_ref, kept_ref, pre_ref, end_ref, vec_ref, tok_buf, tok_sems,
    in_re_ref, in_im_ref, weight_sems, gain_ref, bias_ref, skip_ref, nu_ref, theta_ref, glu_b_ref,
):
    count, group, steps, length = dims
    states = in_re_ref.shape[-1]
    weights = Weights(
        weight_sems, (gain_far, None, gain_ref), (bias_far, None, bias_ref),
        (skip_far, None, skip_ref), (nu_far, None, nu_ref), (theta_far, None, theta_ref),
        (glu_b_far, None, glu_b_ref), (in_re_far, 0, in_re_ref), (in_im_far, 0, in_im_ref),
    )
    tok = Fetch(tok_ref, tok_buf, tok_sems, steps, length // steps)
    weights.wait()
    for no in range(gain_ref.shape[0]):
        row = slice(no, no + 1)
        decay_rows(
            vec_ref, no, gain_ref[row, :], bias_ref[row, :], skip_ref[row, :], nu_ref[row, :],
            theta_ref[row, :], glu_b_ref[row, :], length,
        )
    origin = lax.broadcasted_iota(jnp.int32, (CHUNKS, LANES), 0) * length + offset_ref[0]
    lam = lam_rows(vec_ref, 0, group)

    def block(at, carry):
        base = at * (steps * group)
        state, kept = carry
        for step in range(steps):
            place = origin + (at * steps + step)
            keeps = []
            for seq_no in range(count):
                keep = jnp.ones((CHUNKS, LANES), F32)
                for slot in range(resets_ref.shape[1]):
                    keep = jnp.where(place == resets_ref[seq_no, slot], 0.0, keep)
                keeps.append(keep)
            keep = jnp.concatenate(keeps, axis=0)
            kept = kept * keep
            keep_ref[rows_at(base, step, group), :] = keep
        rows = rows_at(base, 0, steps * group)
        normed, _, _ = norm_affine(tok.get(at), vec_ref, 0)
        write_drive(drive_ref, rows, normed.astype(BF16), in_re_ref, in_im_ref, vec_ref, 0)
        state = scan_up(drive_ref, keep_ref, base, lam, state, steps, group)
        return state, kept

    zero = jnp.zeros((group, states), F32)
    state, kept = loop(
        length // steps, block, ((zero, zero), jnp.ones((group, LANES), F32))
    )
    kept_ref[...] = kept
    pieces = chunk_totals(chunk_factor(vec_ref, 0, kept), state, count, False)
    write_totals(pieces, pre_ref, end_ref, False)


def layer_out(h_low, normed, out_re_ref, out_im_ref, vec_ref, no, glu_w_ref):
    states = out_re_ref.shape[0]
    width = out_re_ref.shape[1]
    mixed = (
        dot(h_low[:, :states], out_re_ref[...])
        - dot(h_low[:, states:], out_im_ref[...])
        + vec_ref[no, 2:3, :] * normed
    )
    act = (0.5 * mixed * (1.0 + gelu_tanh(mixed))).astype(BF16)
    value = dot(act, glu_w_ref[:, :width]) + vec_ref[no, 9:10, :]
    gate = dot(act, glu_w_ref[:, width:]) + vec_ref[no, 10:11, :]
    return mixed, value, gate


def second_kernel(
    dims, place_ref, tok_ref, drive_ref, keep_ref, kept_ref, pre_in_ref, before_ref, other_ref, vec_ref,
    out_re_far, out_im_far, glu_w_far, in_re_far, in_im_far,
    h_far, mixed_far, value_far, gate_far, stream_ref, drive2_ref, pre_ref, end_ref,
    h_ref, mixed_ref, value_ref, gate_ref, row_sems, tok_buf, tok_sems, out_re_ref, out_im_ref, glu_w_ref, in_re_ref, in_im_ref, weight_sems,
):
    count, group, steps, length = dims
    weights = Weights(
        weight_sems, (out_re_far, 0, out_re_ref), (out_im_far, 0, out_im_ref),
        (glu_w_far, 0, glu_w_ref), (in_re_far, 1, in_re_ref), (in_im_far, 1, in_im_ref),
    )
    tok = Fetch(tok_ref, tok_buf, tok_sems, steps, length // steps)
    kept_rows = [
        RowsOut(buffer, target, row_sems.at[at])
        for at, (buffer, target) in enumerate(
            [(h_ref, h_far), (mixed_ref, mixed_far), (value_ref, value_far), (gate_ref, gate_far)]
        )
    ]
    states = in_re_ref.shape[-1]
    size = steps * group
    entering_state = chunk_carries(
        pre_in_ref, last_carry(place_ref, False, before_ref, other_ref), count, False
    )
    h_ref[:group, :] = join(entering_state)
    lam, lam2 = lam_rows(vec_ref, 0, group), lam_rows(vec_ref, 1, group)
    weights.wait()

    def block(at, carry):
        base = at * size
        state, state2 = carry
        rows = rows_at(base, 0, size)
        state = scan_up(drive_ref, keep_ref, base, lam, state, steps, group, h_ref)
        stream = tok.get(at)
        normed, _, _ = norm_affine(stream, vec_ref, 0)
        h_low = h_ref[rows_at(base + group, 0, size), :].astype(BF16)
        mixed, value, gate = layer_out(
            h_low, normed, out_re_ref, out_im_ref, vec_ref, 0, glu_w_ref
        )
        mixed_ref[rows, :] = mixed.astype(BF16)
        value_ref[rows, :] = value.astype(BF16)
        gate_ref[rows, :] = gate.astype(BF16)
        kept_rows[0].send(base + (group if at else 0), base + group + size)
        for one in kept_rows[1:]:
            one.send(base, base + size)
        stream = stream + value * sigmoid(gate)
        stream_ref[rows, :] = stream
        normed, _, _ = norm_affine(stream, vec_ref, 1)
        write_drive(drive2_ref, rows, normed.astype(BF16), in_re_ref, in_im_ref, vec_ref, 1)
        state2 = scan_up(drive2_ref, keep_ref, base, lam2, state2, steps, group)
        return state, state2

    zero = jnp.zeros((group, states), F32)
    _, state2 = loop(length // steps, block, (entering_state, (zero, zero)))
    pieces = chunk_totals(chunk_factor(vec_ref, 1, kept_ref[...]), state2, count, False)
    write_totals(pieces, pre_ref, end_ref, False)
    for one in kept_rows:
        one.finish()


def gate_back(
    upstream, value, gate, mixed, h_low, no, out_re_ref, out_im_ref, glu_w_ref, sums_ref, grads_ref
):
    states = out_re_ref.shape[0]
    width = out_re_ref.shape[1]
    sig = sigmoid(gate)
    value_grad = upstream * sig
    gate_grad = (value_grad * value * (1.0 - sig)).astype(BF16)
    value_grad = value_grad.astype(BF16)
    sums_ref[:, 4 * width : 5 * width] += column_sums(value_grad.astype(F32))
    sums_ref[:, 5 * width : 6 * width] += column_sums(gate_grad.astype(F32))
    act_grad = dot_right_t(value_grad, glu_w_ref[:, :width]) + dot_right_t(
        gate_grad, glu_w_ref[:, width:]
    )
    bend = gelu_tanh(mixed)
    act = (0.5 * mixed * (1.0 + bend)).astype(BF16)
    mixed_low = (act_grad * gelu_slope(mixed, bend)).astype(BF16)
    grads_ref[:width, :] += dot_left_t(act, value_grad)
    grads_ref[width : 2 * width, :] += dot_left_t(act, gate_grad)
    base = 2 * width
    grads_ref[base : base + states, :] += dot_left_t(h_low[:, :states], mixed_low)
    grads_ref[base + states : base + 2 * states, :] -= dot_left_t(h_low[:, states:], mixed_low)
    return mixed_low, dot_right_t(mixed_low, out_re_ref[...]), -dot_right_t(mixed_low, out_im_ref[...])


def third_kernel(
    dims, place_ref, stream_ref, drive_ref, keep_ref, kept_ref, cot_ref, pre_in_ref, before_ref,
    other_ref, vec_ref,
    out_re_far, out_im_far, glu_w_far,
    act_ref, h_ref, mixed_grad_ref, dh_ref, pre_ref, end_ref, kept_half, sent_half, sums_ref,
    grads_ref, cot_buf, cot_sems, act_buf, act_sems, out_re_ref, out_im_ref, glu_w_ref, weight_sems,
):
    count, group, steps, length = dims
    weights = Weights(
        weight_sems, (out_re_far, 1, out_re_ref), (out_im_far, 1, out_im_ref),
        (glu_w_far, 1, glu_w_ref),
    )
    cot = Fetch(cot_ref, cot_buf, cot_sems, steps, length // steps)
    act = Store(act_ref, act_buf, act_sems, steps, length // steps)
    states = out_re_ref.shape[0]
    size = steps * group
    entering_state = chunk_carries(
        pre_in_ref, last_carry(place_ref, False, before_ref, other_ref), count, False
    )
    h_ref[:group, :] = join(entering_state)
    grads_ref[...] = jnp.zeros_like(grads_ref)
    sums_ref[...] = jnp.zeros_like(sums_ref)
    lam = lam_rows(vec_ref, 1, group)
    weights.wait()

    def block(at, state):
        base = at * size
        rows = rows_at(base, 0, size)
        state = scan_up(drive_ref, keep_ref, base, lam, state, steps, group, h_ref)
        stream = stream_ref[rows, :]
        normed, _, _ = norm_affine(stream, vec_ref, 1)
        h_low = h_ref[rows_at(base + group, 0, size), :].astype(BF16)
        mixed, value, gate = layer_out(
            h_low, normed, out_re_ref, out_im_ref, vec_ref, 1, glu_w_ref
        )
        act.put(at, stream + value * sigmoid(gate), group)
        upstream = cot.get(at)
        mixed_low, dh_re, dh_im = gate_back(
            upstream, value, gate, mixed, h_low, 1, out_re_ref, out_im_ref, glu_w_ref,
            sums_ref, grads_ref,
        )
        mixed_grad_ref[rows, :] = mixed_low
        dh_ref[rows, :states] = dh_re
        dh_ref[rows, states:] = dh_im
        return state

    loop(length // steps, block, entering_state)
    act.finish()
    back = lam_rows(vec_ref, 1, group, True)

    def turn(k, state):
        base = (length // steps - 1 - k) * size
        return scan_down(dh_ref, keep_ref, base, back, state, steps, group)

    zero = jnp.zeros((group, states), F32)
    state = loop(length // steps, turn, (zero, zero))
    pieces = chunk_totals(chunk_factor(vec_ref, 1, kept_ref[...], True), state, count, True)
    write_totals(pieces, pre_ref, end_ref, True)
    halve(place_ref, grads_ref, kept_half, sent_half)


def adjoint_scan(dims, base, dh_ref, keep_ref, h_ref, lam, state, g_ref, lam_sums_ref):
    _, group, steps, _ = dims
    states = lam[0].shape[-1]
    lam_re, lam_im = split(lam_sums_ref[...])
    for step in range(steps - 1, -1, -1):
        rows = rows_at(base, step, group)
        here = rows_of(step, group)
        keep = wide(keep_ref[rows, :], states)
        g = (dh_ref[rows, :states] + state[0], dh_ref[rows, states:] + state[1])
        kg = (keep * g[0], keep * g[1])
        state = times(lam, kg)
        g_ref[here, :states] = g[0]
        g_ref[here, states:] = g[1]
        prev = (h_ref[rows, :states], h_ref[rows, states:])
        lam_re = lam_re + (kg[0] * prev[0] + kg[1] * prev[1])
        lam_im = lam_im + (kg[1] * prev[0] - kg[0] * prev[1])
    lam_sums_ref[...] = join([lam_re, lam_im])
    return state


def through_input_map(drive_low, mixed_wide, vec_ref, no, in_re_ref, in_im_ref):
    states = in_re_ref.shape[-1]
    return (
        dot_right_t(drive_low[:, :states], in_re_ref[...])
        + dot_right_t(drive_low[:, states:], in_im_ref[...])
        + vec_ref[no, 2:3, :] * mixed_wide
    )


def input_map_back(
    g_ref, mixed_low, normed, vec_ref, no, in_re_ref, in_im_ref, grads_ref, grads_at
):
    width = in_re_ref.shape[0]
    drive_low = (g_ref[...] * vec_ref[no, 3:4, :]).astype(BF16)
    grads_ref[grads_at : grads_at + width, :] += dot_left_t(normed.astype(BF16), drive_low)
    mixed_wide = mixed_low.astype(F32)
    return (
        drive_low,
        through_input_map(drive_low, mixed_wide, vec_ref, no, in_re_ref, in_im_ref),
        mixed_wide,
    )


def add_sums(sums_ref, normed_grad, xhat, mixed_wide, normed):
    width = xhat.shape[-1]
    sums_ref[:, :width] += column_sums(normed_grad * xhat)
    sums_ref[:, width : 2 * width] += column_sums(normed_grad)
    sums_ref[:, 3 * width : 4 * width] += column_sums(mixed_wide * normed)


def through_norm(normed_grad, xhat, scale, vec_ref, no):
    inner = normed_grad * vec_ref[no, 0:1, :]
    middle = jnp.mean(inner, axis=-1, keepdims=True)
    along = jnp.mean(inner * xhat, axis=-1, keepdims=True)
    return scale * (inner - middle - xhat * along)


def finish_sums(
    small_ref, base, sums_ref, lam_sums_ref, vec_ref, no, in_re_ref, in_im_ref, grads_ref, grads_at
):
    width, states = in_re_ref.shape
    total = jnp.sum(sums_ref[...], axis=0, keepdims=True)
    lam_re, lam_im = split(jnp.sum(lam_sums_ref[...], axis=0, keepdims=True))
    rows = slice(grads_at, grads_at + width)
    gam = jnp.sum(
        column_sums(grads_ref[rows, :states] * in_re_ref[...].astype(F32))
        + column_sums(grads_ref[rows, states:] * in_im_ref[...].astype(F32)),
        axis=0,
        keepdims=True,
    )
    nu_grad = (
        vec_ref[no, 6:7, :states] * lam_re
        + vec_ref[no, 6:7, states:] * lam_im
        + vec_ref[no, 7:8, :states] * gam
    )
    theta_grad = vec_ref[no, 8:9, :states] * lam_re + vec_ref[no, 8:9, states:] * lam_im
    small_ref[base : base + 1, :] = total[:, :width]
    small_ref[base + 1 : base + 2, :] = total[:, width : 2 * width]
    small_ref[base + 2 : base + 3, :] = join([nu_grad, theta_grad])
    small_ref[base + 3 : base + 4, :] = total[:, 3 * width : 4 * width]
    small_ref[base + 4 : base + 5, :] = total[:, 4 * width : 5 * width]
    small_ref[base + 5 : base + 6, :] = total[:, 5 * width : 6 * width]


def fourth_kernel(
    dims, place_ref, dh_ref, keep_ref, h_ref, stream_ref, mixed_ref, cot_ref, sums_in_ref,
    pre_in_ref, before_ref, other_ref, vec_ref, in_re_far, in_im_far,
    up_ref, kept_half, sent_half, small_ref,
    grads_ref, g_ref, sums_ref, lam_ref, cot_buf, cot_sems, in_re_ref, in_im_ref, weight_sems,
):
    count, group, steps, length = dims
    weights = Weights(weight_sems, (in_re_far, 1, in_re_ref), (in_im_far, 1, in_im_ref))
    cot = Fetch(cot_ref, cot_buf, cot_sems, steps, length // steps, True)
    size = steps * group
    entering_state = chunk_carries(
        pre_in_ref, last_carry(place_ref, True, before_ref, other_ref), count, True
    )
    grads_ref[...] = jnp.zeros_like(grads_ref)
    sums_ref[...] = sums_in_ref[...]
    lam_ref[...] = jnp.zeros_like(lam_ref)
    lam = lam_rows(vec_ref, 1, group, True)
    weights.wait()

    def block(k, state):
        at = length // steps - 1 - k
        base = at * size
        rows = rows_at(base, 0, size)
        state = adjoint_scan(dims, base, dh_ref, keep_ref, h_ref, lam, state, g_ref, lam_ref)
        normed, xhat, scale = norm_affine(stream_ref[rows, :], vec_ref, 1)
        _, normed_grad, mixed_wide = input_map_back(
            g_ref, mixed_ref[rows, :], normed, vec_ref, 1, in_re_ref, in_im_ref, grads_ref, 0
        )
        add_sums(sums_ref, normed_grad, xhat, mixed_wide, normed)
        stream_grad = through_norm(normed_grad, xhat, scale, vec_ref, 1)
        up_ref[rows, :] = cot.get(k) + stream_grad
        return state

    loop(length // steps, block, entering_state)
    small_ref[...] = jnp.zeros_like(small_ref)
    finish_sums(
        small_ref, 0, sums_ref, lam_ref, vec_ref, 1, in_re_ref, in_im_ref, grads_ref, 0
    )
    halve(place_ref, grads_ref, kept_half, sent_half)


def middle_kernel(
    dims, place_ref, up_ref, keep_ref, kept_ref, vec_ref, value_far, gate_far, mixed_far, h_far,
    out_re_far, out_im_far, glu_w_far,
    mixed_grad_ref, dh_ref, pre_ref, end_ref, kept_half, sent_half, sums_ref,
    grads_ref, value_ref, gate_ref, mixed_ref, h_ref, row_sems, out_re_ref, out_im_ref, glu_w_ref, weight_sems,
):
    count, group, steps, length = dims
    weights = Weights(
        weight_sems, (out_re_far, 0, out_re_ref), (out_im_far, 0, out_im_ref),
        (glu_w_far, 0, glu_w_ref),
    )
    states = out_re_ref.shape[0]
    size = steps * group
    blocks = length // steps
    old_rows = [
        RowsIn(source, buffer, row_sems.at[at], size, blocks, group if at == 3 else 0)
        for at, (source, buffer) in enumerate(
            [(value_far, value_ref), (gate_far, gate_ref), (mixed_far, mixed_ref), (h_far, h_ref)]
        )
    ]
    for at in range(blocks - 1, -1, -1):
        for one in old_rows:
            one.start(at)
    grads_ref[...] = jnp.zeros_like(grads_ref)
    sums_ref[...] = jnp.zeros_like(sums_ref)
    lam = lam_rows(vec_ref, 0, group, True)
    weights.wait()

    def block(k, state):
        at = length // steps - 1 - k
        base = at * size
        rows = rows_at(base, 0, size)
        for one in old_rows:
            one.wait(at)
        h_low = h_ref[rows, :].astype(BF16)
        mixed_low, dh_re, dh_im = gate_back(
            up_ref[rows, :], value_ref[rows, :].astype(F32), gate_ref[rows, :].astype(F32),
            mixed_ref[rows, :].astype(F32), h_low, 0, out_re_ref, out_im_ref, glu_w_ref,
            sums_ref, grads_ref,
        )
        mixed_grad_ref[rows, :] = mixed_low
        dh_ref[rows, :states] = dh_re
        dh_ref[rows, states:] = dh_im
        return scan_down(dh_ref, keep_ref, base, lam, state, steps, group)

    zero = jnp.zeros((group, states), F32)
    state = loop(length // steps, block, (zero, zero))
    pieces = chunk_totals(chunk_factor(vec_ref, 0, kept_ref[...], True), state, count, True)
    write_totals(pieces, pre_ref, end_ref, True)
    halve(place_ref, grads_ref, kept_half, sent_half)


def fifth_kernel(
    dims, place_ref, dh_ref, keep_ref, h_far, tok_ref, mixed_ref, sums_in_ref,
    small_in_ref, pre_in_ref, before_ref, other_ref, vec_ref, in_re_far, in_im_far,
    drive_ref, kept_half, sent_half,
    lanes_ref, small_ref, grads_ref, g_ref, sums_ref, lam_ref, h_ref, row_sems,
    tok_buf, tok_sems, in_re_ref, in_im_ref, weight_sems,
):
    count, group, steps, length = dims
    weights = Weights(weight_sems, (in_re_far, 0, in_re_ref), (in_im_far, 0, in_im_ref))
    tok = Fetch(tok_ref, tok_buf, tok_sems, steps, length // steps, True)
    blocks = length // steps
    size = steps * group
    old_rows = RowsIn(h_far, h_ref, row_sems, size, blocks)
    for at in range(blocks - 1, -1, -1):
        old_rows.start(at)
    entering_state = chunk_carries(
        pre_in_ref, last_carry(place_ref, True, before_ref, other_ref), count, True
    )
    grads_ref[...] = jnp.zeros_like(grads_ref)
    sums_ref[...] = sums_in_ref[...]
    lam_ref[...] = jnp.zeros_like(lam_ref)
    lam = lam_rows(vec_ref, 0, group, True)
    weights.wait()

    def block(k, state):
        at = blocks - 1 - k
        base = at * size
        rows = rows_at(base, 0, size)
        old_rows.wait(at)
        state = adjoint_scan(
            dims, base, dh_ref, keep_ref, h_ref, lam, state, g_ref, lam_ref
        )
        normed, xhat, _ = norm_affine(tok.get(k), vec_ref, 0)
        drive_low, normed_grad, mixed_wide = input_map_back(
            g_ref, mixed_ref[rows, :], normed, vec_ref, 0, in_re_ref, in_im_ref, grads_ref, 0
        )
        drive_ref[rows, :] = drive_low
        add_sums(sums_ref, normed_grad, xhat, mixed_wide, normed)
        return state

    loop(blocks, block, entering_state)
    small_ref[...] = small_in_ref[...]
    finish_sums(
        small_ref, 8, sums_ref, lam_ref, vec_ref, 0, in_re_ref, in_im_ref, grads_ref, 0
    )
    at = 0
    for source in (grads_ref, small_ref):
        for lane in range(0, source.shape[1], LANES):
            lanes_ref[at : at + source.shape[0], :] = source[:, lane : lane + LANES]
            at += source.shape[0]
    lanes_ref[at:, :] = jnp.zeros((lanes_ref.shape[0] - at, LANES), F32)
    halve(place_ref, lanes_ref, kept_half, sent_half)


def last_kernel(
    dims, tok_ref, mixed_ref, up_ref, drive_ref, vec_ref, in_re_far, in_im_far,
    grad_ref, tok_buf, tok_sems, grad_buf, grad_sems, in_re_ref, in_im_ref, weight_sems,
):
    count, group, steps, length = dims
    weights = Weights(weight_sems, (in_re_far, 0, in_re_ref), (in_im_far, 0, in_im_ref))
    tok = Fetch(tok_ref, tok_buf, tok_sems, steps, length // steps)
    grad = Store(grad_ref, grad_buf, grad_sems, steps, length // steps)
    size = steps * group
    weights.wait()

    def block(at, carry):
        rows = rows_at(at * size, 0, size)
        _, xhat, scale = norm_affine(tok.get(at), vec_ref, 0)
        normed_grad = through_input_map(
            drive_ref[rows, :], mixed_ref[rows, :].astype(F32), vec_ref, 0, in_re_ref, in_im_ref
        )
        grad.put(at, up_ref[rows, :] + through_norm(normed_grad, xhat, scale, vec_ref, 0), group)
        return carry

    loop(length // steps, block, 0)
    grad.finish()


class Running:
    def __init__(self, generator):
        self.generator, self.result = generator, None
        self.wants = self.sent = None
        self.advance(None)

    def advance(self, values):
        try:
            self.wants = self.generator.send(values)
        except StopIteration as stop:
            self.wants, self.result = None, stop.value


class Network:
    def __init__(self, axes, sizes):
        self.axes, self.sizes = axes, sizes
        self.total = sizes[0] * sizes[1]
        self.bits = self.total.bit_length() - 1
        self.index = lax.axis_index(axes[0]) * sizes[1] + lax.axis_index(axes[1])

    def bit(self, at):
        return (self.index >> at) & 1

    def flip(self, value, bits):
        if self.total == 1:
            return value
        mask = sum(1 << bit for bit in bits)
        return lax.ppermute(value, self.axes, [(i, i ^ mask) for i in range(self.total)])

    def launch(self, *running):
        for one in running:
            if one.wants is not None and one.sent is None:
                one.sent = [self.flip(value, bits) for value, bits in one.wants]

    def together(self, *running, beside=None):
        running = [one for one in running if one.wants is not None]
        self.launch(*running)
        made = beside() if beside is not None else ()
        sent, made = lax.optimization_barrier(([one.sent for one in running], made))
        for one, values in zip(running, sent):
            one.sent = None
            one.advance(values)
        return made


def entering(net, place, total, reverse):
    low = net.sizes[1].bit_length() - 1
    before = other = jnp.zeros_like(total)
    scalars = pl.BlockSpec(memory_space=pltpu.SMEM)
    whole = pl.BlockSpec(memory_space=pltpu.VMEM)
    for bit in range(low, net.bits):
        (other,) = yield [(total, (bit,))]
        if bit + 1 < net.bits:
            first = bit == low
            operands = [total, other] + ([] if first else [before])
            operands = [pltpu.with_memory_space_constraint(one, pltpu.VMEM) for one in operands]

            def kernel(place_ref, *refs, first=first, at=bit):
                combine_kernel(first, reverse, place_ref, at, *refs)

            total, before = pl.pallas_call(
                kernel,
                in_specs=[scalars] + [whole] * len(operands),
                out_specs=[whole] * 2,
                out_shape=[pltpu.VMEM(total.shape, F32)] * 2,
                compiler_params=pltpu.CompilerParams(vmem_limit_bytes=1 << 20),
            )(place, *operands)
    return before, other


def local_call(kernel, place, operands, out_shape, scratch=(), far=False, limit=16):
    whole = pl.BlockSpec(memory_space=pltpu.VMEM)
    return pl.pallas_call(
        kernel,
        in_specs=[pl.BlockSpec(memory_space=pltpu.SMEM)] + [whole] * len(operands),
        out_specs=[pl.BlockSpec(memory_space=pl.ANY) if far else whole] * len(out_shape),
        out_shape=out_shape,
        scratch_shapes=list(scratch),
        compiler_params=pltpu.CompilerParams(vmem_limit_bytes=limit << 20),
    )(place, *[pltpu.with_memory_space_constraint(one, pltpu.VMEM) for one in operands])


def position(place_ref, bits):
    return sum(place_ref[bit] << at for at, bit in enumerate(bits))


def partner(bits, k):
    return tuple(bit for at, bit in enumerate(bits) if (k >> at) & 1)


def scatter_step(place, segments, cuts, bits):
    lanes = segments[0][0].shape[1]
    total = sum(segment[0].shape[0] for segment in segments)
    packed = len(set(bits)) == 1
    pieces = [cut >> len(own) for cut, own in zip(cuts, bits)]
    groups = [list(range(len(cuts)))] if packed else [[part] for part in range(len(cuts))]
    shapes = []
    for group in groups:
        rows = sum(pieces[part] for part in group)
        shapes += [pltpu.VMEM((rows, lanes), F32)] * (1 << len(bits[group[0]]))

    def kernel(place_ref, *refs):
        refs = list(refs)
        total_ref = refs.pop()
        row = 0
        for segment in segments:
            value = refs.pop(0)[...]
            for _ in segment[1:]:
                value = value + refs.pop(0)[...]
            total_ref[row : row + value.shape[0], :] = value
            row += value.shape[0]
        for group in groups:
            own = bits[group[0]]
            mine = position(place_ref, own)
            for k in range(1 << len(own)):
                out = refs.pop(0)
                at = 0
                for part in group:
                    size = pieces[part]
                    start = sum(cuts[:part]) + (mine ^ k) * size
                    out[at : at + size, :] = total_ref[pl.ds(pl.multiple_of(start, 8), size), :]
                    at += size

    out = local_call(
        kernel, place, [one for segment in segments for one in segment], shapes,
        [pltpu.VMEM((total, lanes), F32)],
    )
    kept, sent = [], []
    for group in groups:
        own = bits[group[0]]
        many = 1 << len(own)
        kept.append(out[0])
        sent += [(one, partner(own, k)) for k, one in enumerate(out[1:many], 1)]
        out = out[many:]
    return kept, sent


def add_step(place, arrays):
    def kernel(place_ref, *refs):
        value = refs[0][...]
        for ref in refs[1:-1]:
            value = value + ref[...]
        refs[-1][...] = value

    return local_call(kernel, place, arrays, [pltpu.VMEM(arrays[0].shape, F32)])[0]


def gather_step(place, items, bits, packed):
    lanes = items[0][0][0].shape[1]
    sizes = [rows << len(own) for (_, _, rows), own in zip(items, bits)]
    if packed:
        shapes = [pltpu.VMEM((sum(sizes), lanes), F32)]
    else:
        shapes = [pltpu.VMEM((size, lanes), F32) for size in sizes]
    operands = []
    for arrays, _, _ in items:
        operands += [one for one in arrays if not any(one is other for other in operands)]

    def find(array):
        return [one is array for one in operands].index(True)

    def kernel(place_ref, *refs):
        base = 0
        for at, ((arrays, first, rows), own) in enumerate(zip(items, bits)):
            out = refs[len(operands) + (0 if packed else at)]
            mine = position(place_ref, own)
            for k, array in enumerate(arrays):
                start = base + (mine ^ k) * rows
                out[pl.ds(pl.multiple_of(start, 8), rows), :] = refs[find(array)][
                    first : first + rows, :
                ]
            base += sizes[at] if packed else 0

    return local_call(kernel, place, operands, shapes)


def all_sum(net, place, kept, sent, halves):
    got = yield [(one, (0,)) for one in sent]
    segments = [[mine, other] for mine, other in zip(kept, got)]
    total = sum(one.shape[0] for one in kept)
    far = (3, 4)
    if halves:
        cuts = [total // 2] * 2
        for bits in ([(1,), (2,)], [(2,), (1,)]):
            kept, sent = scatter_step(place, segments, cuts, bits)
            got = yield sent
            segments = [[mine, other] for mine, other in zip(kept, got)]
            cuts = [cut // 2 for cut in cuts]
    else:
        kept, sent = scatter_step(place, segments, [total], [(1, 2)])
        got = yield sent
        segments = [kept + got]
        cuts = [total // 4]
    kept, sent = scatter_step(place, segments, cuts, [far] * len(cuts))
    got = yield sent
    own = add_step(place, kept + got)
    for bit in range(5, net.bits):
        got = yield [(own, (bit,))]
        own = add_step(place, [own] + got)
    got = yield [(own, partner(far, k)) for k in (1, 2, 3)]
    rows = [cut // 4 for cut in cuts]
    items = [([own] + got, sum(rows[:at]), rows[at]) for at in range(len(rows))]
    parts = gather_step(place, items, [far] * len(rows), False)
    if halves:
        for bits, last in (([(2,), (1,)], False), ([(1,), (2,)], True)):
            got = yield [(part, own) for part, own in zip(parts, bits)]
            items = [([part, other], 0, part.shape[0]) for part, other in zip(parts, got)]
            parts = gather_step(place, items, bits, last)
    else:
        got = yield [(parts[0], partner((1, 2), k)) for k in (1, 2, 3)]
        parts = gather_step(place, [([parts[0]] + got, 0, parts[0].shape[0])], [(1, 2)], True)
    (other,) = yield [(parts[0], (0,))]
    return parts[0], other


def finish_kernel(
    width, states, place_ref, own_a, other_a, own_c, other_c, own_d, other_d,
    gain_out, bias_out, in_re_out, in_im_out, nu_out, theta_out, out_re_out, out_im_out, skip_out,
    glu_w_out, glu_b_out,
    gain_ref, bias_ref, nu_ref, theta_ref, skip_ref, glu_b_ref, sems,
):
    two = 2 * states
    first = [
        (glu_w_out, (0, width), width), (glu_w_out, (width, 2 * width), width),
        (out_re_out, (0, width), states), (out_im_out, (0, width), states),
    ]

    def ranges(rows, low, high):
        at = 0
        for target, columns, count in rows:
            begin, end = max(at, low), min(at + count, high)
            if begin < end:
                yield target, columns, begin - at, begin - low, end - begin
            at += count

    def copies(half, a_ref, c_ref, d_ref):
        out = []
        size = (2 * width + two) // 2
        for layer, ref in ((1, a_ref), (0, c_ref)):
            for target, (left, right), to, start, rows in ranges(first, half * size, (half + 1) * size):
                out.append((ref.at[start : start + rows], target.at[layer, to : to + rows, left:right]))
        rows = width // 2
        for target, left in ((in_re_out, 0), (in_im_out, states)):
            out.append((
                c_ref.at[size : size + rows, left : left + states],
                target.at[1, half * rows : (half + 1) * rows, :],
            ))
        lanes = [
            (target, (lane, lane + LANES), width)
            for target in (in_re_out, in_im_out)
            for lane in range(0, states, LANES)
        ]
        size = d_ref.shape[0]
        for target, (left, right), to, start, rows in ranges(lanes, half * size, (half + 1) * size):
            out.append((d_ref.at[start : start + rows], target.at[0, to : to + rows, left:right]))
        return out

    def small_rows(d_ref, start):
        return jnp.concatenate(
            [d_ref[start + 16 * at : start + 16 * (at + 1), :] for at in range(width // LANES)], axis=1
        )

    last = width * (two // LANES) - own_d.shape[0]
    for core in (0, 1):

        @pl.when(place_ref[0] == core)
        def _(core=core):
            refs = ((own_a, own_c, own_d), (other_a, other_c, other_d))
            lower, upper = refs[core], refs[1 - core]
            running = [
                pltpu.make_async_copy(source, target, sems.at[at])
                for at, (source, target) in enumerate(copies(0, *lower) + copies(1, *upper))
            ]
            for copy in running:
                copy.start()
            small = small_rows(upper[2], last)
            for layer, base in ((1, 0), (0, 8)):
                row = slice(layer, layer + 1)
                gain_ref[row, :] = small[base : base + 1]
                bias_ref[row, :] = small[base + 1 : base + 2]
                nu_ref[row, :] = small[base + 2 : base + 3, :states]
                theta_ref[row, :] = small[base + 2 : base + 3, states:]
                skip_ref[row, :] = small[base + 3 : base + 4]
                glu_b_ref[row, :width] = small[base + 4 : base + 5]
                glu_b_ref[row, width:] = small[base + 5 : base + 6]
            rest = [
                (gain_ref, gain_out), (bias_ref, bias_out), (nu_ref, nu_out),
                (theta_ref, theta_out), (skip_ref, skip_out), (glu_b_ref, glu_b_out),
            ]
            more = [
                pltpu.make_async_copy(source, target, sems.at[len(running) + at])
                for at, (source, target) in enumerate(rest)
            ]
            for copy in more:
                copy.start()
            for copy in running + more:
                copy.wait()


def shards(
    sizes, tokens, cotangent, resets, ln_gain, ln_bias, in_re, in_im, nu_log, theta_log,
    out_re, out_im, skip, glu_w, glu_b,
):
    axes = ("seq", "row")
    micro, rows_here, span, width = tokens.shape
    states = nu_log.shape[-1]
    count = micro * rows_here
    group = count * CHUNKS
    length = span // CHUNKS
    steps = STEPS if length % STEPS == 0 else length
    size = steps * group
    total = length * group
    dims = (count, group, steps, length)

    tok = tokens.reshape(group, length, width)
    cot = cotangent.reshape(group, length, width)
    starts = resets.reshape(count, -1)
    offset = (lax.axis_index("seq") * span).reshape(1).astype(jnp.int32)

    whole = pl.BlockSpec(memory_space=pltpu.VMEM)
    scalars = pl.BlockSpec(memory_space=pltpu.SMEM)
    anywhere = pl.BlockSpec(memory_space=pl.ANY)

    def block_buffers(dtype):
        return [pltpu.VMEM((2, group, steps, width), dtype), pltpu.SemaphoreType.DMA((2,))]

    def near(value):
        return pltpu.with_memory_space_constraint(value, pltpu.VMEM)

    def distant(value):
        return pltpu.with_memory_space_constraint(value, pltpu.HBM)

    def call(kernel, seconds, operands, out_shape, scratch=(), aliases=None):
        specs, values = [], []
        for kind, *group_values in operands:
            for value in group_values:
                specs.append({near: whole, distant: anywhere, None: scalars}[kind])
                values.append(kind(value) if kind else value)
        return pl.pallas_call(
            functools.partial(kernel, dims),
            in_specs=specs,
            out_specs=[whole if getattr(out, 'memory_space', None) == pltpu.VMEM else anywhere for out in out_shape],
            input_output_aliases=aliases or {},
            out_shape=out_shape,
            scratch_shapes=list(scratch),
            compiler_params=pltpu.CompilerParams(vmem_limit_bytes=VMEM_LIMIT),
            cost_estimate=pl.CostEstimate(
                flops=int(seconds * 1e15), bytes_accessed=1 << 20, transcendentals=0
            ),
        )(*values)

    net = Network(axes, sizes)
    place = (net.index >> jnp.arange(max(net.bits, 5), dtype=jnp.int32)) & 1
    offset, place = lax.optimization_barrier((offset, place))

    def shape(*dims_, dtype=F32):
        return pltpu.VMEM(dims_, dtype)

    two = 2 * states
    pre_shape, end_shape = shape(2, group, two), shape(2 * count, two)
    full = shape(total, two)
    low = shape(total, width, dtype=BF16)
    past = shape(group + total, two)

    natural = jax.ShapeDtypeStruct((group, length, width), F32)
    in_w = pltpu.VMEM(in_re.shape[1:], BF16)
    out_w = pltpu.VMEM(out_re.shape[1:], BF16)
    glu = pltpu.VMEM(glu_w.shape[1:], BF16)
    sems = pltpu.SemaphoreType.DMA
    blocks = length // steps
    far_h = pltpu.HBM((group + total, two), F32)
    far_low = pltpu.HBM((total, width), BF16)

    drive1, keep, kept, pre1, end1, vec = call(
        first_kernel,
        7e-6,
        [(None, starts, offset), (distant, tok, in_re, in_im),
         (distant, ln_gain, ln_bias, skip, nu_log, theta_log, glu_b)],
        [full, shape(total, LANES), shape(group, LANES), pre_shape, end_shape,
         shape(ln_gain.shape[0], 16, width)],
        block_buffers(BF16) + [in_w, in_w, sems((8,))]
        + [pltpu.VMEM(v.shape, F32) for v in (ln_gain, ln_bias, skip, nu_log, theta_log, glu_b)],
    )
    enter = Running(entering(net, place, end1, False))
    while enter.wants:
        net.together(enter)
    carry1 = enter.result

    h1, mixed1, value1, gate1, stream1, drive2, pre2, end2 = call(
        second_kernel,
        12e-6,
        [(None, place), (distant, tok), (near, drive1, keep, kept, pre1, *carry1, vec),
         (distant, out_re, out_im, glu_w, in_re, in_im)],
        [far_h, far_low, far_low, far_low, shape(total, width), full, pre_shape, end_shape],
        [past, low, low, low, sems((4, blocks))] + block_buffers(BF16) + [out_w, out_w, glu, in_w, in_w, sems((5,))],
    )
    enter = Running(entering(net, place, end2, False))
    while enter.wants:
        net.together(enter)
    carry2 = enter.result

    sums_shape = shape(8, 6 * width)
    many = 2 * width + two
    act, h2, mixed_grad2, dh2, back2, back_end2, kept_a, sent_a, sums2 = call(
        third_kernel,
        20e-6,
        [(None, place), (near, stream1, drive2, keep, kept), (distant, cot),
         (near, pre2, *carry2, vec),
         (distant, out_re, out_im, glu_w)],
        [natural, past, low, full, pre_shape, end_shape, shape(many // 2, width),
         shape(many // 2, width), sums_shape],
        [shape(many, width)] + block_buffers(F32) * 2 + [out_w, out_w, glu, sems((3,))],
    )
    enter = Running(entering(net, place, back_end2, True))
    sum_a = Running(all_sum(net, place, [kept_a], [sent_a], True))
    net.together(enter, sum_a)
    net.launch(sum_a)
    while enter.wants:
        net.together(enter)
    back_carry2 = enter.result
    net.together(sum_a)

    lam_sums = pltpu.VMEM((group, two), F32)
    run_sums = pltpu.VMEM((8, 6 * width), F32)
    g_block = pltpu.VMEM((size, two), F32)
    up1, kept_b, sent_b, small2 = net.together(sum_a, beside=lambda: call(
        fourth_kernel,
        16e-6,
        [(None, place), (near, dh2, keep, h2, stream1, mixed_grad2), (distant, cot),
         (near, sums2, back2, *back_carry2, vec), (distant, in_re, in_im)],
        [shape(total, width), shape(width // 2, two), shape(width // 2, two), shape(16, width)],
        [shape(width, two), g_block, run_sums, lam_sums] + block_buffers(F32) + [in_w, in_w, sems((2,))],
        aliases={4: 0},
    ))
    mixed_grad1, dh1, back1, back_end1, kept_c, sent_c, sums1 = net.together(sum_a, beside=lambda: call(
        middle_kernel,
        16e-6,
        [(None, place), (near, up1, keep, kept, vec), (distant, value1, gate1, mixed1, h1),
         (distant, out_re, out_im, glu_w)],
        [low, full, pre_shape, end_shape, shape(many // 2, width), shape(many // 2, width), sums_shape],
        [shape(many, width), low, low, low, full, sems((4, blocks)), out_w, out_w, glu, sems((3,))],
    ))
    enter = Running(entering(net, place, back_end1, True))
    sum_c = Running(all_sum(net, place, [kept_c, kept_b], [sent_c, sent_b], True))
    net.launch(sum_a)
    net.together(enter, sum_c)
    net.launch(sum_c)
    while enter.wants:
        net.together(enter)
    back_carry1 = enter.result
    net.together(sum_a)

    rows_d = width * (two // LANES) + 16 * (width // LANES)
    rows_d += -rows_d % (8 * 32)
    drive_grad1, kept_d, sent_d = net.together(sum_a, sum_c, beside=lambda: call(
        fifth_kernel,
        9e-6,
        [(None, place), (near, dh1, keep), (distant, h1, tok),
         (near, mixed_grad1, sums1, small2), (near, back1, *back_carry1, vec),
         (distant, in_re, in_im)],
        [low, shape(rows_d // 2, LANES), shape(rows_d // 2, LANES)],
        [shape(rows_d, LANES), shape(16, width), shape(width, two), g_block, run_sums, lam_sums, full,
         sems((blocks,))] + block_buffers(BF16) + [in_w, in_w, sems((2,))],
    ))
    sum_d = Running(all_sum(net, place, [kept_d], [sent_d], False))
    (input_grad,) = net.together(sum_a, sum_c, sum_d, beside=lambda: call(
        last_kernel,
        7e-6,
        [(distant, tok), (near, mixed_grad1, up1, drive_grad1, vec), (distant, in_re, in_im)],
        [natural],
        block_buffers(BF16) + block_buffers(F32) + [in_w, in_w, sems((2,))],
    ))
    while sum_a.wants or sum_c.wants or sum_d.wants:
        net.together(sum_a, sum_c, sum_d)

    wide_rows, narrow_rows = shape(2, width), shape(2, states)
    results = local_call(
        functools.partial(finish_kernel, width, states),
        place,
        [*sum_a.result, *sum_c.result, *sum_d.result],
        [pltpu.HBM(one.shape, F32) for one in
         (ln_gain, ln_bias, in_re, in_im, nu_log, theta_log, out_re, out_im, skip, glu_w, glu_b)],
        [wide_rows, wide_rows, narrow_rows, narrow_rows, wide_rows, shape(2, 2 * width), sems((32,))],
        True,
    )
    return (act.reshape(tokens.shape), input_grad.reshape(tokens.shape), *results)


def solution(mesh):
    sizes = (mesh.shape["seq"], mesh.shape["row"])
    split_rows = P(None, "row", "seq", None)
    in_specs = (split_rows, split_rows, P(None, "row", None)) + (P(),) * 11
    out_specs = (split_rows, split_rows) + (P(),) * 11
    return jax.shard_map(
        functools.partial(shards, sizes),
        mesh=mesh,
        in_specs=in_specs,
        out_specs=out_specs,
        check_vma=False,
    )
```

```python
import functools

import jax
import jax.numpy as jnp
from jax import lax
from jax.experimental import pallas as pl
from jax.experimental.pallas import tpu as pltpu
from jax.sharding import PartitionSpec as P

EPS = 1e-05
CHUNKS = 8
LANES = 128
VMEM_LIMIT = 16 << 20
UNROLL = True
STEPS = 32
F32 = jnp.float32
BF16 = jnp.bfloat16
GELU_C = 0.7978845608028654
GELU_A = 0.044715


def dot(left, right):
    return jnp.dot(left, right, preferred_element_type=F32)


def dot_right_t(left, right):
    return lax.dot_general(left, right, (((1,), (1,)), ((), ())), preferred_element_type=F32)


def dot_left_t(left, right):
    return lax.dot_general(left, right, (((0,), (0,)), ((), ())), preferred_element_type=F32)


def normalize(inputs):
    centre = jnp.mean(inputs, axis=-1, keepdims=True)
    centred = inputs - centre
    spread = jnp.mean(centred * centred, axis=-1, keepdims=True)
    scale = lax.rsqrt(spread + EPS)
    return centred * scale, scale


def sigmoid(gate):
    return 0.5 * jnp.tanh(0.5 * gate) + 0.5


def gelu_tanh(mixed):
    return jnp.tanh(GELU_C * (mixed + GELU_A * mixed * mixed * mixed))


def gelu_slope(mixed, bend):
    inner = GELU_C * (1.0 + (3.0 * GELU_A) * mixed * mixed)
    return 0.5 * (1.0 + bend) + 0.5 * mixed * (1.0 - bend * bend) * inner


def one_minus_exp(value):
    series = jnp.ones_like(value)
    for term in range(11, 1, -1):
        series = 1.0 - value * series * (1.0 / term)
    return jnp.where(value < 0.5, value * series, 1.0 - jnp.exp(-value))


def times(left, right):
    return (
        left[0] * right[0] - left[1] * right[1],
        left[0] * right[1] + left[1] * right[0],
    )


def to_steps(block):
    return jnp.swapaxes(block, 0, 1).reshape(-1, block.shape[-1])


def from_steps(rows, group):
    return jnp.swapaxes(rows.reshape(-1, group, rows.shape[-1]), 0, 1)


def wide(keep, states):
    return jnp.concatenate([keep] * (states // LANES), axis=1)


def split(value):
    half = value.shape[-1] // 2
    return value[:, :half], value[:, half:]


def join(pair):
    return jnp.concatenate(pair, axis=1)


def spread_row(row, count):
    return jnp.broadcast_to(row, (count, row.shape[-1]))


def rows_of(step, group):
    return slice(step * group, (step + 1) * group)


def rows_at(base, step, group):
    if isinstance(base, int):
        return slice(base + step * group, base + (step + 1) * group)
    return pl.ds(pl.multiple_of(base + step * group, group), group)


def loop(count, body, carry):
    if not UNROLL:
        return lax.fori_loop(0, count, body, carry)
    for turn in range(count):
        carry = body(turn, carry)
    return carry


def maybe(condition, action):
    if isinstance(condition, bool):
        if condition:
            action()
    else:
        pl.when(condition)(action)


def scan_up(drive_ref, keep_ref, base, lam, state, steps, group, h_ref=None):
    states = lam[0].shape[-1]
    for step in range(steps):
        rows = rows_at(base, step, group)
        keep = wide(keep_ref[rows, :], states)
        turned = times(lam, state)
        state = (
            keep * turned[0] + drive_ref[rows, :states],
            keep * turned[1] + drive_ref[rows, states:],
        )
        if h_ref is not None:
            later = rows_at(base, step + 1, group)
            h_ref[later, :states] = state[0]
            h_ref[later, states:] = state[1]
    return state


def scan_down(dh_ref, keep_ref, base, lam, state, steps, group):
    states = lam[0].shape[-1]
    for step in range(steps - 1, -1, -1):
        rows = rows_at(base, step, group)
        keep = wide(keep_ref[rows, :], states)
        g = (dh_ref[rows, :states] + state[0], dh_ref[rows, states:] + state[1])
        state = times(lam, (keep * g[0], keep * g[1]))
    return state


def chunk_totals(factor, value, count, reverse):
    pieces = []
    for seq_no in range(count):
        rows = rows_of(seq_no, CHUNKS)
        a = (factor[0][rows], factor[1][rows])
        x = (value[0][rows], value[1][rows])
        place = lax.broadcasted_iota(jnp.int32, a[0].shape, 0)
        shift = 1
        while shift < CHUNKS:
            turn = CHUNKS - shift if reverse else shift
            valid = place < CHUNKS - shift if reverse else place >= shift
            a_before = tuple(pltpu.roll(part, turn, 0) for part in a)
            x_before = tuple(pltpu.roll(part, turn, 0) for part in x)
            a_new = times(a_before, a)
            x_new = times(a, x_before)
            x = tuple(jnp.where(valid, new + old, old) for new, old in zip(x_new, x))
            a = tuple(jnp.where(valid, new, old) for new, old in zip(a_new, a))
            shift *= 2
        pieces.append((a, x))
    return pieces


def write_totals(pieces, pre_ref, end_ref, reverse):
    count = len(pieces)
    edge = 0 if reverse else CHUNKS - 1
    for seq_no, (a, x) in enumerate(pieces):
        rows = rows_of(seq_no, CHUNKS)
        a_all = join(a)
        x_all = join(x)
        pre_ref[0, rows, :] = a_all
        pre_ref[1, rows, :] = x_all
        end_ref[seq_no : seq_no + 1, :] = a_all[edge : edge + 1]
        end_ref[count + seq_no : count + seq_no + 1, :] = x_all[edge : edge + 1]


def joined(first, second):
    count = first.shape[0] // 2
    second_a = split(second[:count])
    factor = times(split(first[:count]), second_a)
    moved = times(second_a, split(first[count:]))
    second_x = split(second[count:])
    value = (moved[0] + second_x[0], moved[1] + second_x[1])
    return jnp.concatenate([join(factor), join(value)], axis=0)


def combine_kernel(first_round, reverse, place_ref, at, total_ref, other_ref, *refs):
    later = place_ref[0, at] == (0 if reverse else 1)
    total, other = total_ref[...], other_ref[...]
    if first_round:
        total_out, before_out = refs
        half = total.shape[0] // 2
        row = lax.broadcasted_iota(jnp.int32, total.shape, 0)
        lane = lax.broadcasted_iota(jnp.int32, total.shape, 1)
        identity = jnp.where((row < half) & (lane < total.shape[1] // 2), 1.0, 0.0)
        before_out[...] = jnp.where(later, other, identity)
    else:
        before_ref, total_out, before_out = refs
        before = before_ref[...]
        before_out[...] = jnp.where(later, joined(other, before), before)
    total_out[...] = jnp.where(later, joined(other, total), joined(total, other))


def last_carry(place_ref, reverse, before_ref, other_ref):
    before, other = before_ref[...], other_ref[...]
    count = before.shape[0] // 2
    later = place_ref[1, 0] == (0 if reverse else 1)
    return jnp.where(later, joined(other, before), before)[count:]


def chunk_carries(pre_ref, entered, count, reverse):
    reals, imags = [], []
    for seq_no in range(count):
        rows = rows_of(seq_no, CHUNKS)
        a = split(pre_ref[0, rows, :])
        x = split(pre_ref[1, rows, :])
        carry = split(entered[seq_no : seq_no + 1, :])
        place = lax.broadcasted_iota(jnp.int32, a[0].shape, 0)
        first = place == (CHUNKS - 1 if reverse else 0)
        turn = CHUNKS - 1 if reverse else 1
        a = tuple(pltpu.roll(part, turn, 0) for part in a)
        x = tuple(pltpu.roll(part, turn, 0) for part in x)
        moved = times(a, carry)
        reals.append(jnp.where(first, carry[0], x[0] + moved[0]))
        imags.append(jnp.where(first, carry[1], x[1] + moved[1]))
    return jnp.concatenate(reals, axis=0), jnp.concatenate(imags, axis=0)


def chunk_factor(vec_ref, no, kept, conj=False):
    group = kept.shape[0]
    whole = split(vec_ref[no, 5:6, :])
    keep = wide(kept, whole[0].shape[-1])
    real, imag = tuple(spread_row(part, group) * keep for part in whole)
    return (real, -imag) if conj else (real, imag)


def lam_rows(vec_ref, no, group, conj=False):
    lam = split(vec_ref[no, 4:5, :])
    real, imag = spread_row(lam[0], group), spread_row(lam[1], group)
    return (real, -imag) if conj else (real, imag)


def halve(place_ref, whole_ref, kept_ref, sent_ref):
    half = kept_ref.shape[0]
    mine = place_ref[0, 0]
    kept_ref[...] = whole_ref[pl.ds(pl.multiple_of(mine * half, 8), half), :]
    sent_ref[...] = whole_ref[pl.ds(pl.multiple_of((1 - mine) * half, 8), half), :]


def column_sums(value):
    return jnp.sum(value.reshape(-1, 8, value.shape[-1]), axis=0)


def norm_affine(stream, vec_ref, no):
    xhat, scale = normalize(stream)
    return xhat * vec_ref[no, 0:1, :] + vec_ref[no, 1:2, :], xhat, scale


def write_drive(drive_ref, rows, normed_low, in_re_ref, in_im_ref, vec_ref, no):
    gamma = split(vec_ref[no, 3:4, :])
    states = gamma[0].shape[-1]
    drive_ref[rows, :states] = dot(normed_low, in_re_ref[...]) * gamma[0]
    drive_ref[rows, states:] = dot(normed_low, in_im_ref[...]) * gamma[1]


def time_block(ref, block, steps):
    if isinstance(block, int):
        return ref.at[:, block * steps : (block + 1) * steps, :]
    return ref.at[:, pl.ds(pl.multiple_of(block * steps, steps), steps), :]


class Weights:
    def __init__(self, sems, *copies):
        self.copies = [
            pltpu.make_async_copy(source if no is None else source.at[no], target, sems.at[at])
            for at, (source, no, target) in enumerate(copies)
        ]
        for copy in self.copies:
            copy.start()

    def wait(self, first=0, last=None):
        for copy in self.copies[first:last]:
            copy.wait()


class Fetch:
    def __init__(self, source, buffer, sems, steps, blocks, down=False):
        self.source, self.buffer, self.sems = source, buffer, sems
        self.steps, self.blocks, self.down = steps, blocks, down
        self.copy(0).start()

    def copy(self, turn):
        block = self.blocks - 1 - turn if self.down else turn
        slot = turn % 2
        return pltpu.make_async_copy(
            time_block(self.source, block, self.steps), self.buffer.at[slot], self.sems.at[slot]
        )

    def get(self, turn):
        maybe(turn + 1 < self.blocks, lambda: self.copy(turn + 1).start())

        self.copy(turn).wait()
        return to_steps(self.buffer[turn % 2].astype(F32))


class Store:
    def __init__(self, target, buffer, sems, steps, blocks, down=False):
        self.target, self.buffer, self.sems = target, buffer, sems
        self.steps, self.blocks, self.down = steps, blocks, down

    def copy(self, turn):
        block = self.blocks - 1 - turn if self.down else turn
        slot = turn % 2
        return pltpu.make_async_copy(
            self.buffer.at[slot], time_block(self.target, block, self.steps), self.sems.at[slot]
        )

    def put(self, turn, rows, group):
        maybe(turn >= 2, lambda: self.copy(turn - 2).wait())

        self.buffer[turn % 2] = from_steps(rows, group)
        self.copy(turn).start()

    def finish(self):
        for turn in range(max(self.blocks - 2, 0), self.blocks):
            self.copy(turn).wait()


def decay_rows(vec_ref, no, gain, bias, skip, nu_log, theta_log, glu_b, length):
    speed = jnp.exp(nu_log)
    phase = jnp.exp(theta_log)
    radius = jnp.exp(-speed)
    lam_re, lam_im = radius * jnp.cos(phase), radius * jnp.sin(phase)
    square = one_minus_exp(2.0 * speed)
    gamma = jnp.sqrt(square)
    far = jnp.exp(-speed * length)
    far_re, far_im = far * jnp.cos(phase * length), far * jnp.sin(phase * length)
    width = gain.shape[-1]
    rows = [
        gain,
        bias,
        skip,
        join([gamma, gamma]),
        join([lam_re, lam_im]),
        join([far_re, far_im]),
        join([-speed * lam_re, -speed * lam_im]),
        join([speed * jnp.exp(-2.0 * speed) / square, jnp.zeros_like(speed)]),
        join([-phase * lam_im, phase * lam_re]),
        glu_b[:, :width],
        glu_b[:, width:],
    ]
    for at, row in enumerate(rows):
        vec_ref[no, at : at + 1, :] = row


def first_kernel(
    dims, index_ref, resets_far, tok_ref, in_re_far, in_im_far,
    gain_far, bias_far, skip_far, nu_far, theta_far, glu_b_far,
    drive_ref, keep_ref, kept_ref, pre_ref, end_ref, vec_ref, place_ref, tok_buf, tok_sems,
    resets_ref, in_re_ref, in_im_ref, weight_sems, gain_ref, bias_ref, skip_ref, nu_ref, theta_ref, glu_b_ref,
    bits,
):
    count, group, steps, length = dims
    states = in_re_ref.shape[-1]
    weights = Weights(
        weight_sems, (gain_far, None, gain_ref), (bias_far, None, bias_ref),
        (skip_far, None, skip_ref), (nu_far, None, nu_ref), (theta_far, None, theta_ref),
        (glu_b_far, None, glu_b_ref), (in_re_far, 0, in_re_ref), (in_im_far, 0, in_im_ref),
        (resets_far, None, resets_ref),
    )
    tok = Fetch(tok_ref, tok_buf, tok_sems, steps, length // steps)
    low, high = bits
    index = index_ref[0]
    lane = lax.broadcasted_iota(jnp.int32, place_ref.shape, 1)
    row = lax.broadcasted_iota(jnp.int32, place_ref.shape, 0)
    shift = jnp.where(row == 1, max(high - 1, 0), jnp.minimum(lane, 31))
    place_ref[...] = lax.shift_right_logical(jnp.full(place_ref.shape, index), shift) & 1
    weights.wait()
    for no in range(gain_ref.shape[0]):
        row = slice(no, no + 1)
        decay_rows(
            vec_ref, no, gain_ref[row, :], bias_ref[row, :], skip_ref[row, :], nu_ref[row, :],
            theta_ref[row, :], glu_b_ref[row, :], length,
        )
    first = lax.shift_right_logical(index, low) * (length * CHUNKS)
    origin = lax.broadcasted_iota(jnp.int32, (CHUNKS, LANES), 0) * length + first
    starts = [
        [
            jnp.broadcast_to(resets_ref[seq_no : seq_no + 1, slot : slot + 1], (CHUNKS, LANES))
            for slot in range(resets_ref.shape[1])
        ]
        for seq_no in range(count)
    ]
    lam = lam_rows(vec_ref, 0, group)

    def block(at, carry):
        base = at * (steps * group)
        state, kept = carry
        for step in range(steps):
            place = origin + (at * steps + step)
            keeps = []
            for seq_no in range(count):
                keep = jnp.ones((CHUNKS, LANES), F32)
                for start in starts[seq_no]:
                    keep = jnp.where(place == start, 0.0, keep)
                keeps.append(keep)
            keep = jnp.concatenate(keeps, axis=0)
            kept = kept * keep
            keep_ref[rows_at(base, step, group), :] = keep
        rows = rows_at(base, 0, steps * group)
        normed, _, _ = norm_affine(tok.get(at), vec_ref, 0)
        write_drive(drive_ref, rows, normed.astype(BF16), in_re_ref, in_im_ref, vec_ref, 0)
        state = scan_up(drive_ref, keep_ref, base, lam, state, steps, group)
        return state, kept

    zero = jnp.zeros((group, states), F32)
    state, kept = loop(
        length // steps, block, ((zero, zero), jnp.ones((group, LANES), F32))
    )
    kept_ref[...] = kept
    pieces = chunk_totals(chunk_factor(vec_ref, 0, kept), state, count, False)
    write_totals(pieces, pre_ref, end_ref, False)


def layer_out(h_low, normed, out_re_ref, out_im_ref, vec_ref, no, glu_w_ref):
    states = out_re_ref.shape[0]
    width = out_re_ref.shape[1]
    mixed = (
        dot(h_low[:, :states], out_re_ref[...])
        - dot(h_low[:, states:], out_im_ref[...])
        + vec_ref[no, 2:3, :] * normed
    )
    act = (0.5 * mixed * (1.0 + gelu_tanh(mixed))).astype(BF16)
    value = dot(act, glu_w_ref[:, :width]) + vec_ref[no, 9:10, :]
    gate = dot(act, glu_w_ref[:, width:]) + vec_ref[no, 10:11, :]
    return mixed, value, gate


def second_kernel(
    dims, place_ref, tok_ref, drive_ref, keep_ref, kept_ref, pre_in_ref, before_ref, other_ref, vec_ref,
    out_re_far, out_im_far, glu_w_far, in_re_far, in_im_far,
    h_ref, mixed_ref, value_ref, gate_ref, stream_ref, drive2_ref, pre_ref, end_ref,
    tok_buf, tok_sems, out_re_ref, out_im_ref, glu_w_ref, in_re_ref, in_im_ref, weight_sems,
):
    count, group, steps, length = dims
    weights = Weights(
        weight_sems, (out_re_far, 0, out_re_ref), (out_im_far, 0, out_im_ref),
        (glu_w_far, 0, glu_w_ref), (in_re_far, 1, in_re_ref), (in_im_far, 1, in_im_ref),
    )
    tok = Fetch(tok_ref, tok_buf, tok_sems, steps, length // steps)
    states = in_re_ref.shape[-1]
    size = steps * group
    entering_state = chunk_carries(
        pre_in_ref, last_carry(place_ref, False, before_ref, other_ref), count, False
    )
    h_ref[:group, :] = join(entering_state)
    lam, lam2 = lam_rows(vec_ref, 0, group), lam_rows(vec_ref, 1, group)
    weights.wait()

    def block(at, carry):
        base = at * size
        state, state2 = carry
        rows = rows_at(base, 0, size)
        state = scan_up(drive_ref, keep_ref, base, lam, state, steps, group, h_ref)
        stream = tok.get(at)
        normed, _, _ = norm_affine(stream, vec_ref, 0)
        h_low = h_ref[rows_at(base + group, 0, size), :].astype(BF16)
        mixed, value, gate = layer_out(
            h_low, normed, out_re_ref, out_im_ref, vec_ref, 0, glu_w_ref
        )
        mixed_ref[rows, :] = mixed.astype(BF16)
        value_ref[rows, :] = value.astype(BF16)
        gate_ref[rows, :] = gate.astype(BF16)
        stream = stream + value * sigmoid(gate)
        stream_ref[rows, :] = stream
        normed, _, _ = norm_affine(stream, vec_ref, 1)
        write_drive(drive2_ref, rows, normed.astype(BF16), in_re_ref, in_im_ref, vec_ref, 1)
        state2 = scan_up(drive2_ref, keep_ref, base, lam2, state2, steps, group)
        return state, state2

    zero = jnp.zeros((group, states), F32)
    _, state2 = loop(length // steps, block, (entering_state, (zero, zero)))
    pieces = chunk_totals(chunk_factor(vec_ref, 1, kept_ref[...]), state2, count, False)
    write_totals(pieces, pre_ref, end_ref, False)


def gate_back(
    rows, upstream, value, gate, mixed, out_re_ref, out_im_ref, glu_w_ref, sums_ref,
    act_ref, value_grad_ref, gate_grad_ref, mixed_grad_ref, dh_ref,
):
    states, width = out_re_ref.shape
    sig = sigmoid(gate)
    value_grad = upstream * sig
    gate_grad = (value_grad * value * (1.0 - sig)).astype(BF16)
    value_grad = value_grad.astype(BF16)
    value_grad_ref[rows, :] = value_grad
    gate_grad_ref[rows, :] = gate_grad
    sums_ref[:, 4 * width : 5 * width] += column_sums(value_grad.astype(F32))
    sums_ref[:, 5 * width : 6 * width] += column_sums(gate_grad.astype(F32))
    act_grad = dot_right_t(value_grad, glu_w_ref[:, :width]) + dot_right_t(
        gate_grad, glu_w_ref[:, width:]
    )
    bend = gelu_tanh(mixed)
    act_ref[rows, :] = (0.5 * mixed * (1.0 + bend)).astype(BF16)
    mixed_low = (act_grad * gelu_slope(mixed, bend)).astype(BF16)
    mixed_grad_ref[rows, :] = mixed_low
    dh_ref[rows, :states] = dot_right_t(mixed_low, out_re_ref[...])
    dh_ref[rows, states:] = -dot_right_t(mixed_low, out_im_ref[...])


def by_core(place_ref, kept_half, sent_half, first, second):
    @pl.when(place_ref[0, 0] == 0)
    def _():
        kept_half[...] = first()
        sent_half[...] = second()

    @pl.when(place_ref[0, 0] != 0)
    def _():
        sent_half[...] = first()
        kept_half[...] = second()


def glu_grads_kernel(place_ref, act_ref, value_grad_ref, gate_grad_ref, kept_half, sent_half):
    by_core(
        place_ref, kept_half, sent_half,
        lambda: dot_left_t(act_ref[...], value_grad_ref[...]),
        lambda: dot_left_t(act_ref[...], gate_grad_ref[...]),
    )


def out_grads_kernel(group, place_ref, h_ref, mixed_grad_ref, kept_half, sent_half):
    states = h_ref.shape[1] // 2
    by_core(
        place_ref, kept_half, sent_half,
        lambda: dot_left_t(h_ref[group:, :states].astype(BF16), mixed_grad_ref[...]),
        lambda: -dot_left_t(h_ref[group:, states:].astype(BF16), mixed_grad_ref[...]),
    )


def third_kernel(
    dims, place_ref, stream_ref, drive_ref, keep_ref, kept_ref, cot_ref, pre_in_ref, before_ref,
    other_ref, vec_ref,
    out_re_far, out_im_far, glu_w_far,
    out_far, h_ref, mixed_grad_ref, dh_ref, pre_ref, end_ref, act_ref, value_grad_ref, gate_grad_ref,
    sums_ref, cot_buf, cot_sems, out_buf, out_sems, out_re_ref, out_im_ref, glu_w_ref, weight_sems,
):
    count, group, steps, length = dims
    weights = Weights(
        weight_sems, (out_re_far, 1, out_re_ref), (out_im_far, 1, out_im_ref),
        (glu_w_far, 1, glu_w_ref),
    )
    cot = Fetch(cot_ref, cot_buf, cot_sems, steps, length // steps)
    result = Store(out_far, out_buf, out_sems, steps, length // steps)
    states = out_re_ref.shape[0]
    size = steps * group
    entering_state = chunk_carries(
        pre_in_ref, last_carry(place_ref, False, before_ref, other_ref), count, False
    )
    h_ref[:group, :] = join(entering_state)
    sums_ref[...] = jnp.zeros_like(sums_ref)
    lam = lam_rows(vec_ref, 1, group)
    weights.wait()

    def block(at, state):
        base = at * size
        rows = rows_at(base, 0, size)
        state = scan_up(drive_ref, keep_ref, base, lam, state, steps, group, h_ref)
        stream = stream_ref[rows, :]
        normed, _, _ = norm_affine(stream, vec_ref, 1)
        h_low = h_ref[rows_at(base + group, 0, size), :].astype(BF16)
        mixed, value, gate = layer_out(
            h_low, normed, out_re_ref, out_im_ref, vec_ref, 1, glu_w_ref
        )
        result.put(at, stream + value * sigmoid(gate), group)
        gate_back(
            rows, cot.get(at), value, gate, mixed, out_re_ref, out_im_ref, glu_w_ref, sums_ref,
            act_ref, value_grad_ref, gate_grad_ref, mixed_grad_ref, dh_ref,
        )
        return state

    loop(length // steps, block, entering_state)
    result.finish()
    back = lam_rows(vec_ref, 1, group, True)

    def turn(k, state):
        base = (length // steps - 1 - k) * size
        return scan_down(dh_ref, keep_ref, base, back, state, steps, group)

    zero = jnp.zeros((group, states), F32)
    state = loop(length // steps, turn, (zero, zero))
    pieces = chunk_totals(chunk_factor(vec_ref, 1, kept_ref[...], True), state, count, True)
    write_totals(pieces, pre_ref, end_ref, True)


def adjoint_scan(dims, base, dh_ref, keep_ref, h_ref, lam, state, g_ref, lam_sums_ref):
    _, group, steps, _ = dims
    states = lam[0].shape[-1]
    lam_re, lam_im = split(lam_sums_ref[...])
    for step in range(steps - 1, -1, -1):
        rows = rows_at(base, step, group)
        here = rows_of(step, group)
        keep = wide(keep_ref[rows, :], states)
        g = (dh_ref[rows, :states] + state[0], dh_ref[rows, states:] + state[1])
        kg = (keep * g[0], keep * g[1])
        state = times(lam, kg)
        g_ref[here, :states] = g[0]
        g_ref[here, states:] = g[1]
        prev = (h_ref[rows, :states], h_ref[rows, states:])
        lam_re = lam_re + (kg[0] * prev[0] + kg[1] * prev[1])
        lam_im = lam_im + (kg[1] * prev[0] - kg[0] * prev[1])
    lam_sums_ref[...] = join([lam_re, lam_im])
    return state


def through_input_map(drive_low, mixed_wide, vec_ref, no, in_re_ref, in_im_ref):
    states = in_re_ref.shape[-1]
    return (
        dot_right_t(drive_low[:, :states], in_re_ref[...])
        + dot_right_t(drive_low[:, states:], in_im_ref[...])
        + vec_ref[no, 2:3, :] * mixed_wide
    )


def input_map_back(
    g_ref, mixed_low, normed, vec_ref, no, in_re_ref, in_im_ref, grads_ref, grads_at
):
    width = in_re_ref.shape[0]
    drive_low = (g_ref[...] * vec_ref[no, 3:4, :]).astype(BF16)
    grads_ref[grads_at : grads_at + width, :] += dot_left_t(normed.astype(BF16), drive_low)
    mixed_wide = mixed_low.astype(F32)
    return (
        drive_low,
        through_input_map(drive_low, mixed_wide, vec_ref, no, in_re_ref, in_im_ref),
        mixed_wide,
    )


def add_sums(sums_ref, normed_grad, xhat, mixed_wide, normed):
    width = xhat.shape[-1]
    sums_ref[:, :width] += column_sums(normed_grad * xhat)
    sums_ref[:, width : 2 * width] += column_sums(normed_grad)
    sums_ref[:, 3 * width : 4 * width] += column_sums(mixed_wide * normed)


def through_norm(normed_grad, xhat, scale, vec_ref, no):
    inner = normed_grad * vec_ref[no, 0:1, :]
    middle = jnp.mean(inner, axis=-1, keepdims=True)
    along = jnp.mean(inner * xhat, axis=-1, keepdims=True)
    return scale * (inner - middle - xhat * along)


def finish_sums(
    small_ref, base, sums_ref, lam_sums_ref, vec_ref, no, in_re_ref, in_im_ref, grads_ref, grads_at
):
    width, states = in_re_ref.shape
    total = jnp.sum(sums_ref[...], axis=0, keepdims=True)
    lam_re, lam_im = split(jnp.sum(lam_sums_ref[...], axis=0, keepdims=True))
    rows = slice(grads_at, grads_at + width)
    gam = jnp.sum(
        column_sums(grads_ref[rows, :states] * in_re_ref[...].astype(F32))
        + column_sums(grads_ref[rows, states:] * in_im_ref[...].astype(F32)),
        axis=0,
        keepdims=True,
    )
    nu_grad = (
        vec_ref[no, 6:7, :states] * lam_re
        + vec_ref[no, 6:7, states:] * lam_im
        + vec_ref[no, 7:8, :states] * gam
    )
    theta_grad = vec_ref[no, 8:9, :states] * lam_re + vec_ref[no, 8:9, states:] * lam_im
    small_ref[base : base + 1, :] = total[:, :width]
    small_ref[base + 1 : base + 2, :] = total[:, width : 2 * width]
    small_ref[base + 2 : base + 3, :] = join([nu_grad, theta_grad])
    small_ref[base + 3 : base + 4, :] = total[:, 3 * width : 4 * width]
    small_ref[base + 4 : base + 5, :] = total[:, 4 * width : 5 * width]
    small_ref[base + 5 : base + 6, :] = total[:, 5 * width : 6 * width]


def fourth_kernel(
    dims, place_ref, dh_ref, keep_ref, h_ref, stream_ref, mixed_ref, cot_ref, sums_in_ref,
    pre_in_ref, before_ref, other_ref, vec_ref, in_re_far, in_im_far,
    up_ref, kept_half, sent_half, small_ref,
    grads_ref, g_ref, sums_ref, lam_ref, cot_buf, cot_sems, in_re_ref, in_im_ref, weight_sems,
):
    count, group, steps, length = dims
    weights = Weights(weight_sems, (in_re_far, 1, in_re_ref), (in_im_far, 1, in_im_ref))
    cot = Fetch(cot_ref, cot_buf, cot_sems, steps, length // steps, True)
    size = steps * group
    entering_state = chunk_carries(
        pre_in_ref, last_carry(place_ref, True, before_ref, other_ref), count, True
    )
    grads_ref[...] = jnp.zeros_like(grads_ref)
    sums_ref[...] = sums_in_ref[...]
    lam_ref[...] = jnp.zeros_like(lam_ref)
    lam = lam_rows(vec_ref, 1, group, True)
    weights.wait()

    def block(k, state):
        at = length // steps - 1 - k
        base = at * size
        rows = rows_at(base, 0, size)
        state = adjoint_scan(dims, base, dh_ref, keep_ref, h_ref, lam, state, g_ref, lam_ref)
        normed, xhat, scale = norm_affine(stream_ref[rows, :], vec_ref, 1)
        _, normed_grad, mixed_wide = input_map_back(
            g_ref, mixed_ref[rows, :], normed, vec_ref, 1, in_re_ref, in_im_ref, grads_ref, 0
        )
        add_sums(sums_ref, normed_grad, xhat, mixed_wide, normed)
        stream_grad = through_norm(normed_grad, xhat, scale, vec_ref, 1)
        up_ref[rows, :] = cot.get(k) + stream_grad
        return state

    loop(length // steps, block, entering_state)
    small_ref[...] = jnp.zeros_like(small_ref)
    finish_sums(
        small_ref, 0, sums_ref, lam_ref, vec_ref, 1, in_re_ref, in_im_ref, grads_ref, 0
    )
    halve(place_ref, grads_ref, kept_half, sent_half)


def middle_kernel(
    dims, place_ref, up_ref, keep_ref, kept_ref, vec_ref, value_ref, gate_ref, mixed_ref,
    out_re_far, out_im_far, glu_w_far,
    mixed_grad_ref, dh_ref, pre_ref, end_ref, act_ref, value_grad_ref, gate_grad_ref, sums_ref,
    out_re_ref, out_im_ref, glu_w_ref, weight_sems,
):
    count, group, steps, length = dims
    weights = Weights(
        weight_sems, (out_re_far, 0, out_re_ref), (out_im_far, 0, out_im_ref),
        (glu_w_far, 0, glu_w_ref),
    )
    states = out_re_ref.shape[0]
    size = steps * group
    blocks = length // steps
    sums_ref[...] = jnp.zeros_like(sums_ref)
    lam = lam_rows(vec_ref, 0, group, True)
    weights.wait()

    def block(k, state):
        at = length // steps - 1 - k
        base = at * size
        rows = rows_at(base, 0, size)
        gate_back(
            rows, up_ref[rows, :], value_ref[rows, :].astype(F32), gate_ref[rows, :].astype(F32),
            mixed_ref[rows, :].astype(F32), out_re_ref, out_im_ref, glu_w_ref, sums_ref,
            act_ref, value_grad_ref, gate_grad_ref, mixed_grad_ref, dh_ref,
        )
        return scan_down(dh_ref, keep_ref, base, lam, state, steps, group)

    zero = jnp.zeros((group, states), F32)
    state = loop(length // steps, block, (zero, zero))
    pieces = chunk_totals(chunk_factor(vec_ref, 0, kept_ref[...], True), state, count, True)
    write_totals(pieces, pre_ref, end_ref, True)


def fifth_kernel(
    dims, place_ref, dh_ref, keep_ref, h_ref, tok_ref, mixed_ref, sums_in_ref,
    small_in_ref, pre_in_ref, before_ref, other_ref, vec_ref, in_re_far, in_im_far,
    drive_ref, kept_half, sent_half,
    lanes_ref, small_ref, grads_ref, g_ref, sums_ref, lam_ref,
    tok_buf, tok_sems, in_re_ref, in_im_ref, weight_sems,
):
    count, group, steps, length = dims
    weights = Weights(weight_sems, (in_re_far, 0, in_re_ref), (in_im_far, 0, in_im_ref))
    tok = Fetch(tok_ref, tok_buf, tok_sems, steps, length // steps, True)
    blocks = length // steps
    size = steps * group
    entering_state = chunk_carries(
        pre_in_ref, last_carry(place_ref, True, before_ref, other_ref), count, True
    )
    grads_ref[...] = jnp.zeros_like(grads_ref)
    sums_ref[...] = sums_in_ref[...]
    lam_ref[...] = jnp.zeros_like(lam_ref)
    lam = lam_rows(vec_ref, 0, group, True)
    weights.wait()

    def block(k, state):
        at = blocks - 1 - k
        base = at * size
        rows = rows_at(base, 0, size)
        state = adjoint_scan(
            dims, base, dh_ref, keep_ref, h_ref, lam, state, g_ref, lam_ref
        )
        normed, xhat, _ = norm_affine(tok.get(k), vec_ref, 0)
        drive_low, normed_grad, mixed_wide = input_map_back(
            g_ref, mixed_ref[rows, :], normed, vec_ref, 0, in_re_ref, in_im_ref, grads_ref, 0
        )
        drive_ref[rows, :] = drive_low
        add_sums(sums_ref, normed_grad, xhat, mixed_wide, normed)
        return state

    loop(blocks, block, entering_state)
    small_ref[...] = small_in_ref[...]
    finish_sums(
        small_ref, 8, sums_ref, lam_ref, vec_ref, 0, in_re_ref, in_im_ref, grads_ref, 0
    )
    at = 0
    for source in (grads_ref, small_ref):
        for lane in range(0, source.shape[1], LANES):
            lanes_ref[at : at + source.shape[0], :] = source[:, lane : lane + LANES]
            at += source.shape[0]
    lanes_ref[at:, :] = jnp.zeros((lanes_ref.shape[0] - at, LANES), F32)
    halve(place_ref, lanes_ref, kept_half, sent_half)


def last_kernel(
    dims, tok_ref, mixed_ref, up_ref, drive_ref, vec_ref, in_re_far, in_im_far,
    grad_ref, tok_buf, tok_sems, grad_buf, grad_sems, in_re_ref, in_im_ref, weight_sems,
):
    count, group, steps, length = dims
    weights = Weights(weight_sems, (in_re_far, 0, in_re_ref), (in_im_far, 0, in_im_ref))
    tok = Fetch(tok_ref, tok_buf, tok_sems, steps, length // steps)
    grad = Store(grad_ref, grad_buf, grad_sems, steps, length // steps)
    size = steps * group
    weights.wait()

    def block(at, carry):
        rows = rows_at(at * size, 0, size)
        _, xhat, scale = norm_affine(tok.get(at), vec_ref, 0)
        normed_grad = through_input_map(
            drive_ref[rows, :], mixed_ref[rows, :].astype(F32), vec_ref, 0, in_re_ref, in_im_ref
        )
        grad.put(at, up_ref[rows, :] + through_norm(normed_grad, xhat, scale, vec_ref, 0), group)
        return carry

    loop(length // steps, block, 0)
    grad.finish()


class Running:
    def __init__(self, generator):
        self.generator, self.result = generator, None
        self.wants = self.sent = None
        self.advance(None)

    def advance(self, values):
        try:
            self.wants = self.generator.send(values)
        except StopIteration as stop:
            self.wants, self.result = None, stop.value


class Network:
    def __init__(self, axes, sizes):
        self.axes, self.sizes = axes, sizes
        self.total = sizes[0] * sizes[1]
        self.bits = self.total.bit_length() - 1
        self.index = lax.axis_index(axes[0]) * sizes[1] + lax.axis_index(axes[1])

    def bit(self, at):
        return (self.index >> at) & 1

    def flip(self, value, bits):
        if self.total == 1:
            return value
        mask = sum(1 << bit for bit in bits)
        return lax.ppermute(value, self.axes, [(i, i ^ mask) for i in range(self.total)])

    def launch(self, *running):
        for one in running:
            if one.wants is not None and one.sent is None:
                one.sent = [self.flip(value, bits) for value, bits in one.wants]

    def together(self, *running, beside=None, hold=True):
        running = [one for one in running if one.wants is not None]
        if hold:
            values = lax.optimization_barrier(
                [[value for value, _ in one.wants] for one in running if one.sent is None]
            )
            for one in running:
                if one.sent is None:
                    one.wants = list(zip(values.pop(0), [bits for _, bits in one.wants]))
        self.launch(*running)
        made = beside() if beside is not None else ()
        sent, made = lax.optimization_barrier(([one.sent for one in running], made))
        for one, values in zip(running, sent):
            one.sent = None
            one.advance(values)
        return made


def entering(net, place, total, reverse):
    low = net.sizes[1].bit_length() - 1
    before = other = jnp.zeros_like(total)
    whole = pl.BlockSpec(memory_space=pltpu.VMEM)
    for bit in range(low, net.bits):
        (other,) = yield [(total, (bit,))]
        if bit + 1 < net.bits:
            first = bit == low
            operands = [place, total, other] + ([] if first else [before])
            operands = [pltpu.with_memory_space_constraint(one, pltpu.VMEM) for one in operands]

            def kernel(place_ref, *refs, first=first, at=bit):
                combine_kernel(first, reverse, place_ref, at, *refs)

            total, before = pl.pallas_call(
                kernel,
                in_specs=[whole] * len(operands),
                out_specs=[whole] * 2,
                out_shape=[pltpu.VMEM(total.shape, F32)] * 2,
                compiler_params=pltpu.CompilerParams(vmem_limit_bytes=1 << 20),
            )(*operands)
    return before, other


def local_call(
    kernel, place, operands, out_shape, scratch=(), far=False, limit=16, seconds=5e-7, distant=()
):
    whole = pl.BlockSpec(memory_space=pltpu.VMEM)
    return pl.pallas_call(
        kernel,
        in_specs=[whole] * (1 + len(operands)) + [pl.BlockSpec(memory_space=pl.ANY)] * len(distant),
        input_output_aliases={1 + len(operands) + at: at for at in range(len(distant))},
        out_specs=[pl.BlockSpec(memory_space=pl.ANY) if far else whole] * len(out_shape),
        out_shape=out_shape,
        scratch_shapes=list(scratch),
        compiler_params=pltpu.CompilerParams(vmem_limit_bytes=limit << 20),
        cost_estimate=pl.CostEstimate(
            flops=int(seconds * 1e15), bytes_accessed=1 << 10, transcendentals=0
        ),
    )(
        *[pltpu.with_memory_space_constraint(one, pltpu.VMEM) for one in [place, *operands]],
        *[pltpu.with_memory_space_constraint(one, pltpu.HBM) for one in distant],
    )


def position(place_ref, bits):
    return sum(place_ref[0, bit] << at for at, bit in enumerate(bits))


def partner(bits, k):
    return tuple(bit for at, bit in enumerate(bits) if (k >> at) & 1)


def scatter_step(place, segments, cuts, bits):
    lanes = segments[0][0].shape[1]
    total = sum(segment[0].shape[0] for segment in segments)
    packed = len(set(bits)) == 1
    pieces = [cut >> len(own) for cut, own in zip(cuts, bits)]
    groups = [list(range(len(cuts)))] if packed else [[part] for part in range(len(cuts))]
    shapes = []
    for group in groups:
        rows = sum(pieces[part] for part in group)
        shapes += [pltpu.VMEM((rows, lanes), F32)] * (1 << len(bits[group[0]]))

    def kernel(place_ref, *refs):
        refs = list(refs)
        total_ref = refs.pop()
        row = 0
        for segment in segments:
            value = refs.pop(0)[...]
            for _ in segment[1:]:
                value = value + refs.pop(0)[...]
            total_ref[row : row + value.shape[0], :] = value
            row += value.shape[0]
        for group in groups:
            own = bits[group[0]]
            mine = position(place_ref, own)
            for k in range(1 << len(own)):
                out = refs.pop(0)
                at = 0
                for part in group:
                    size = pieces[part]
                    start = sum(cuts[:part]) + (mine ^ k) * size
                    out[at : at + size, :] = total_ref[pl.ds(pl.multiple_of(start, 8), size), :]
                    at += size

    out = local_call(
        kernel, place, [one for segment in segments for one in segment], shapes,
        [pltpu.VMEM((total, lanes), F32)],
    )
    kept, sent = [], []
    for group in groups:
        own = bits[group[0]]
        many = 1 << len(own)
        kept.append(out[0])
        sent += [(one, partner(own, k)) for k, one in enumerate(out[1:many], 1)]
        out = out[many:]
    return kept, sent


def add_step(place, arrays):
    def kernel(place_ref, *refs):
        value = refs[0][...]
        for ref in refs[1:-1]:
            value = value + ref[...]
        refs[-1][...] = value

    return local_call(kernel, place, arrays, [pltpu.VMEM(arrays[0].shape, F32)])[0]


def gather_step(place, items, bits, packed):
    lanes = items[0][0][0].shape[1]
    sizes = [rows << len(own) for (_, _, rows), own in zip(items, bits)]
    if packed:
        shapes = [pltpu.VMEM((sum(sizes), lanes), F32)]
    else:
        shapes = [pltpu.VMEM((size, lanes), F32) for size in sizes]
    operands = []
    for arrays, _, _ in items:
        operands += [one for one in arrays if not any(one is other for other in operands)]

    def find(array):
        return [one is array for one in operands].index(True)

    def kernel(place_ref, *refs):
        base = 0
        for at, ((arrays, first, rows), own) in enumerate(zip(items, bits)):
            out = refs[len(operands) + (0 if packed else at)]
            mine = position(place_ref, own)
            for k, array in enumerate(arrays):
                start = base + (mine ^ k) * rows
                out[pl.ds(pl.multiple_of(start, 8), rows), :] = refs[find(array)][
                    first : first + rows, :
                ]
            base += sizes[at] if packed else 0

    return local_call(kernel, place, operands, shapes)


def swap_cores(kept, sent):
    (got,) = yield [(sent, (0,))]
    return [kept, got]


def all_sum(net, place, segments, halves, far=((3, 4),)):
    total = sum(segment[0].shape[0] for segment in segments)
    if halves:
        cuts = [total // 2] * 2
        for bits in ([(1,), (2,)], [(2,), (1,)]):
            kept, sent = scatter_step(place, segments, cuts, bits)
            got = yield sent
            segments = [[mine, other] for mine, other in zip(kept, got)]
            cuts = [cut // 2 for cut in cuts]
    else:
        kept, sent = scatter_step(place, segments, [total], [(1, 2)])
        got = yield sent
        segments = [kept + got]
        cuts = [total // 4]
    for bits in far:
        kept, sent = scatter_step(place, segments, cuts, [bits] * len(cuts))
        got = yield sent
        segments = [kept + got]
        cuts = [cut >> len(bits) for cut in cuts]
    own = add_step(place, segments[0])
    for bit in range(5, net.bits):
        got = yield [(own, (bit,))]
        own = add_step(place, [own] + got)
    parts = [own]
    for bits in far[::-1]:
        own = parts[0]
        got = yield [(own, partner(bits, k)) for k in range(1, 1 << len(bits))]
        items = [([own] + got, sum(cuts[:at]), cuts[at]) for at in range(len(cuts))]
        parts = gather_step(place, items, [bits] * len(cuts), bits is not far[0])
        cuts = [cut << len(bits) for cut in cuts]
    if halves:
        for bits, last in (([(2,), (1,)], False), ([(1,), (2,)], True)):
            got = yield [(part, own) for part, own in zip(parts, bits)]
            items = [([part, other], 0, part.shape[0]) for part, other in zip(parts, got)]
            parts = gather_step(place, items, bits, last)
    else:
        got = yield [(parts[0], partner((1, 2), k)) for k in (1, 2, 3)]
        parts = gather_step(place, [([parts[0]] + got, 0, parts[0].shape[0])], [(1, 2)], True)
    (other,) = yield [(parts[0], (0,))]
    return parts[0], other


def half_copies(half, width, states, outs, layer, first_ref, input_ref=None, lanes_ref=None):
    in_re_out, in_im_out, out_re_out, out_im_out, glu_w_out = outs
    out = []
    if first_ref is not None:
        out += [
            (first_ref.at[:width], glu_w_out.at[layer, :, half * width : (half + 1) * width]),
            (first_ref.at[width : width + states], (out_re_out, out_im_out)[half].at[layer]),
        ]
    if input_ref is not None:
        size, rows = width + states, width // 2
        for target, left in ((in_re_out, 0), (in_im_out, states)):
            out.append((
                input_ref.at[size : size + rows, left : left + states],
                target.at[1, half * rows : (half + 1) * rows, :],
            ))
    if lanes_ref is not None:
        size, at = lanes_ref.shape[0], 0
        for target in (in_re_out, in_im_out):
            for lane in range(0, states, LANES):
                begin, end = max(at, half * size), min(at + width, (half + 1) * size)
                if begin < end:
                    start = begin - half * size
                    out.append((
                        lanes_ref.at[start : start + end - begin],
                        target.at[0, begin - at : end - at, lane : lane + LANES],
                    ))
                at += width
    return out


def run_copies(pairs, sems, first=0):
    running = [
        pltpu.make_async_copy(source, target, sems.at[first + at])
        for at, (source, target) in enumerate(pairs)
    ]
    for copy in running:
        copy.start()
    return running


def own_results_kernel(width, states, place_ref, own_a, other_a, own_c, own_d, *refs):
    *outs, sems = refs
    for core in (0, 1):

        @pl.when(place_ref[0, 0] == core)
        def _(core=core):
            pairs = half_copies(core, width, states, outs, 1, own_a)
            pairs += half_copies(1 - core, width, states, outs, 1, other_a)
            pairs += half_copies(core, width, states, outs, 0, own_c, own_c, own_d)
            for copy in run_copies(pairs, sems):
                copy.wait()


def other_results_kernel(width, states, place_ref, other_c, own_d, other_d, *refs):
    outs, small_outs = refs[5:10], refs[10:16]
    small_refs, sems = refs[16:22], refs[22]
    gain_ref, bias_ref, nu_ref, theta_ref, skip_ref, glu_b_ref = small_refs
    last = width * (2 * states // LANES) - own_d.shape[0]
    for core in (0, 1):

        @pl.when(place_ref[0, 0] == core)
        def _(core=core):
            pairs = half_copies(1 - core, width, states, outs, 0, other_c, other_c, other_d)
            running = run_copies(pairs, sems)
            upper = own_d if core else other_d
            small = jnp.concatenate(
                [
                    upper[last + 16 * at : last + 16 * (at + 1), :]
                    for at in range(width // LANES)
                ],
                axis=1,
            )
            for layer, base in ((1, 0), (0, 8)):
                row = slice(layer, layer + 1)
                gain_ref[row, :] = small[base : base + 1]
                bias_ref[row, :] = small[base + 1 : base + 2]
                nu_ref[row, :] = small[base + 2 : base + 3, :states]
                theta_ref[row, :] = small[base + 2 : base + 3, states:]
                skip_ref[row, :] = small[base + 3 : base + 4]
                glu_b_ref[row, :width] = small[base + 4 : base + 5]
                glu_b_ref[row, width:] = small[base + 5 : base + 6]
            for copy in running + run_copies(list(zip(small_refs, small_outs)), sems, len(running)):
                copy.wait()


def shards(
    sizes, tokens, cotangent, resets, ln_gain, ln_bias, in_re, in_im, nu_log, theta_log,
    out_re, out_im, skip, glu_w, glu_b,
):
    axes = ("seq", "row")
    micro, rows_here, span, width = tokens.shape
    states = nu_log.shape[-1]
    count = micro * rows_here
    group = count * CHUNKS
    length = span // CHUNKS
    steps = STEPS if length % STEPS == 0 else length
    size = steps * group
    total = length * group
    dims = (count, group, steps, length)

    tok = tokens.reshape(group, length, width)
    cot = cotangent.reshape(group, length, width)
    starts = resets.reshape(count, -1)

    whole = pl.BlockSpec(memory_space=pltpu.VMEM)
    scalars = pl.BlockSpec(memory_space=pltpu.SMEM)
    anywhere = pl.BlockSpec(memory_space=pl.ANY)

    def block_buffers(dtype):
        return [pltpu.VMEM((2, group, steps, width), dtype), pltpu.SemaphoreType.DMA((2,))]

    def near(value):
        return pltpu.with_memory_space_constraint(value, pltpu.VMEM)

    def distant(value):
        return pltpu.with_memory_space_constraint(value, pltpu.HBM)

    def call(kernel, seconds, operands, out_shape, scratch=(), aliases=None):
        specs, values = [], []
        for kind, *group_values in operands:
            for value in group_values:
                specs.append({near: whole, distant: anywhere, None: scalars}[kind])
                values.append(kind(value) if kind else value)
        return pl.pallas_call(
            functools.partial(kernel, dims),
            in_specs=specs,
            out_specs=[whole if getattr(out, 'memory_space', None) == pltpu.VMEM else anywhere for out in out_shape],
            input_output_aliases=aliases or {},
            out_shape=out_shape,
            scratch_shapes=list(scratch),
            compiler_params=pltpu.CompilerParams(vmem_limit_bytes=VMEM_LIMIT),
            cost_estimate=pl.CostEstimate(
                flops=int(seconds * 1e15), bytes_accessed=1 << 20, transcendentals=0
            ),
        )(*values)

    net = Network(axes, sizes)
    low_bits = sizes[1].bit_length() - 1

    def shape(*dims_, dtype=F32):
        return pltpu.VMEM(dims_, dtype)

    two = 2 * states
    pre_shape, end_shape = shape(2, group, two), shape(2 * count, two)
    full = shape(total, two)
    low = shape(total, width, dtype=BF16)
    past = shape(group + total, two)

    natural = jax.ShapeDtypeStruct((group, length, width), F32)
    in_w = pltpu.VMEM(in_re.shape[1:], BF16)
    out_w = pltpu.VMEM(out_re.shape[1:], BF16)
    glu = pltpu.VMEM(glu_w.shape[1:], BF16)
    sems = pltpu.SemaphoreType.DMA
    blocks = length // steps
    drive1, keep, kept, pre1, end1, vec, place = call(
        functools.partial(first_kernel, bits=(low_bits, net.bits)),
        7e-6,
        [(None, net.index.reshape(1).astype(jnp.int32)), (distant, starts, tok, in_re, in_im),
         (distant, ln_gain, ln_bias, skip, nu_log, theta_log, glu_b)],
        [full, shape(total, LANES), shape(group, LANES), pre_shape, end_shape,
         shape(ln_gain.shape[0], 16, width), shape(8, LANES, dtype=jnp.int32)],
        block_buffers(BF16) + [pltpu.VMEM(starts.shape, jnp.int32), in_w, in_w, sems((9,))]
        + [pltpu.VMEM(v.shape, F32) for v in (ln_gain, ln_bias, skip, nu_log, theta_log, glu_b)],
    )
    enter = Running(entering(net, place, end1, False))
    while enter.wants:
        net.together(enter)
    carry1 = enter.result

    h1, mixed1, value1, gate1, stream1, drive2, pre2, end2 = call(
        second_kernel,
        12e-6,
        [(near, place), (distant, tok), (near, drive1, keep, kept, pre1, *carry1, vec),
         (distant, out_re, out_im, glu_w, in_re, in_im)],
        [past, low, low, low, shape(total, width), full, pre_shape, end_shape],
        block_buffers(BF16) + [out_w, out_w, glu, in_w, in_w, sems((5,))],
    )
    enter = Running(entering(net, place, end2, False))
    while enter.wants:
        net.together(enter)
    carry2 = enter.result

    sums_shape = shape(8, 6 * width)
    act, h2, mixed_grad2, dh2, back2, back_end2, act2, value_grad2, gate_grad2, sums2 = call(
        third_kernel,
        20e-6,
        [(near, place, stream1, drive2, keep, kept), (distant, cot),
         (near, pre2, *carry2, vec), (distant, out_re, out_im, glu_w)],
        [natural, past, low, full, pre_shape, end_shape, low, low, low, sums_shape],
        block_buffers(F32) * 2 + [out_w, out_w, glu, sems((3,))],
    )

    def glu_grads(act_low, value_grad, gate_grad):
        return local_call(
            glu_grads_kernel, place, [act_low, value_grad, gate_grad], [shape(width, width)] * 2,
            seconds=3e-6,
        )

    def out_grads(h, mixed_grad):
        return local_call(
            functools.partial(out_grads_kernel, group), place, [h, mixed_grad],
            [shape(states, width)] * 2, seconds=2e-6,
        )

    enter = Running(entering(net, place, back_end2, True))
    glu_a = Running(swap_cores(
        *net.together(enter, beside=lambda: glu_grads(act2, value_grad2, gate_grad2))
    ))
    out_a = Running(swap_cores(
        *net.together(enter, glu_a, beside=lambda: out_grads(h2, mixed_grad2))
    ))
    net.together(enter, out_a)
    while enter.wants:
        net.together(enter)
    back_carry2 = enter.result
    sum_a = Running(all_sum(net, place, [glu_a.result, out_a.result], True))

    lam_sums = pltpu.VMEM((group, two), F32)
    run_sums = pltpu.VMEM((8, 6 * width), F32)
    g_block = pltpu.VMEM((size, two), F32)
    up1, kept_b, sent_b, small2 = net.together(sum_a, beside=lambda: call(
        fourth_kernel,
        16e-6,
        [(near, place, dh2, keep, h2, stream1, mixed_grad2), (distant, cot),
         (near, sums2, back2, *back_carry2, vec), (distant, in_re, in_im)],
        [shape(total, width), shape(width // 2, two), shape(width // 2, two), shape(16, width)],
        [shape(width, two), g_block, run_sums, lam_sums] + block_buffers(F32) + [in_w, in_w, sems((2,))],
        aliases={4: 0},
    ))
    core_b = Running(swap_cores(kept_b, sent_b))
    mixed_grad1, dh1, back1, back_end1, act1, value_grad1, gate_grad1, sums1 = net.together(
        sum_a, core_b, beside=lambda: call(
        middle_kernel,
        16e-6,
        [(near, place, up1, keep, kept, vec, value1, gate1, mixed1), (distant, out_re, out_im, glu_w)],
        [low, full, pre_shape, end_shape, low, low, low, sums_shape],
        [out_w, out_w, glu, sems((3,))],
        aliases={7: 4, 5: 5, 6: 6},
    ))
    enter = Running(entering(net, place, back_end1, True))
    glu_c = Running(swap_cores(
        *net.together(enter, beside=lambda: glu_grads(act1, value_grad1, gate_grad1))
    ))
    out_c = Running(swap_cores(
        *net.together(enter, glu_c, beside=lambda: out_grads(h1, mixed_grad1))
    ))
    net.together(enter, out_c)
    while enter.wants:
        net.together(enter)
    back_carry1 = enter.result
    sum_c = Running(all_sum(net, place, [glu_c.result, out_c.result, core_b.result], True))
    rows_d = width * (two // LANES) + 16 * (width // LANES)
    rows_d += -rows_d % (8 * 32)
    drive_grad1, kept_d, sent_d = net.together(sum_a, sum_c, hold=False, beside=lambda: call(
        fifth_kernel,
        9e-6,
        [(near, place, dh1, keep, h1), (distant, tok),
         (near, mixed_grad1, sums1, small2), (near, back1, *back_carry1, vec),
         (distant, in_re, in_im)],
        [low, shape(rows_d // 2, LANES), shape(rows_d // 2, LANES)],
        [shape(rows_d, LANES), shape(16, width), shape(width, two), g_block, run_sums, lam_sums]
        + block_buffers(BF16) + [in_w, in_w, sems((2,))],
    ))
    core_d = Running(swap_cores(kept_d, sent_d))
    net.together(sum_c, core_d, sum_a)
    sum_d = Running(all_sum(net, place, [core_d.result], False))
    net.together(sum_c, sum_d, sum_a)
    net.together(sum_c, sum_d, sum_a)
    net.together(sum_c, sum_d, sum_a)
    (input_grad,) = net.together(sum_c, sum_d, beside=lambda: call(
        last_kernel,
        7e-6,
        [(distant, tok), (near, mixed_grad1, up1, drive_grad1, vec), (distant, in_re, in_im)],
        [natural],
        block_buffers(BF16) + block_buffers(F32) + [in_w, in_w, sems((2,))],
    ))

    def at_last(one):
        return one.wants[0][1] == (0,)

    while sum_a.wants or not (at_last(sum_c) and at_last(sum_d)):
        net.together(sum_a, *[one for one in (sum_c, sum_d) if not at_last(one)])
    own_c, own_d = sum_c.wants[0][0], sum_d.wants[0][0]
    wide_rows, narrow_rows = shape(2, width), shape(2, states)
    large = [pltpu.HBM(one.shape, F32) for one in (in_re, in_im, out_re, out_im, glu_w)]
    tiny = [pltpu.HBM(one.shape, F32) for one in (ln_gain, ln_bias, nu_log, theta_log, skip, glu_b)]
    results = net.together(sum_c, sum_d, beside=lambda: local_call(
        functools.partial(own_results_kernel, width, states), place,
        [*sum_a.result, own_c, own_d], large, [sems((32,))], True, seconds=2e-6,
    ))
    results = local_call(
        functools.partial(other_results_kernel, width, states), place,
        [sum_c.result[1], own_d, sum_d.result[1]], large + tiny,
        [wide_rows, wide_rows, narrow_rows, narrow_rows, wide_rows, shape(2, 2 * width), sems((32,))],
        True, distant=results,
    )
    in_re_g, in_im_g, out_re_g, out_im_g, glu_w_g, gain_g, bias_g, nu_g, theta_g, skip_g, glu_b_g = results
    return (
        act.reshape(tokens.shape), input_grad.reshape(tokens.shape), gain_g, bias_g, in_re_g, in_im_g,
        nu_g, theta_g, out_re_g, out_im_g, skip_g, glu_w_g, glu_b_g,
    )


def solution(mesh):
    sizes = (mesh.shape["seq"], mesh.shape["row"])
    split_rows = P(None, "row", "seq", None)
    in_specs = (split_rows, split_rows, P(None, "row", None)) + (P(),) * 11
    out_specs = (split_rows, split_rows) + (P(),) * 11
    return jax.shard_map(
        functools.partial(shards, sizes),
        mesh=mesh,
        in_specs=in_specs,
        out_specs=out_specs,
        check_vma=False,
    )
```

```python
import functools

import jax
import jax.numpy as jnp
from jax import lax
from jax.experimental import pallas as pl
from jax.experimental.pallas import tpu as pltpu
from jax.sharding import PartitionSpec as P

EPS = 1e-05
CHUNKS = 8
LANES = 128
VMEM_LIMIT = 16 << 20
UNROLL = True
STEPS = 32
F32 = jnp.float32
BF16 = jnp.bfloat16
GELU_C = 0.7978845608028654
GELU_A = 0.044715


def dot(left, right):
    return jnp.dot(left, right, preferred_element_type=F32)


def dot_right_t(left, right):
    return lax.dot_general(left, right, (((1,), (1,)), ((), ())), preferred_element_type=F32)


def dot_left_t(left, right):
    return lax.dot_general(left, right, (((0,), (0,)), ((), ())), preferred_element_type=F32)


def normalize(inputs):
    centre = jnp.mean(inputs, axis=-1, keepdims=True)
    centred = inputs - centre
    spread = jnp.mean(centred * centred, axis=-1, keepdims=True)
    scale = lax.rsqrt(spread + EPS)
    return centred * scale, scale


def sigmoid(gate):
    return 0.5 * jnp.tanh(0.5 * gate) + 0.5


def gelu_tanh(mixed):
    return jnp.tanh(GELU_C * (mixed + GELU_A * mixed * mixed * mixed))


def gelu_slope(mixed, bend):
    inner = GELU_C * (1.0 + (3.0 * GELU_A) * mixed * mixed)
    return 0.5 * (1.0 + bend) + 0.5 * mixed * (1.0 - bend * bend) * inner


def one_minus_exp(value):
    series = jnp.ones_like(value)
    for term in range(11, 1, -1):
        series = 1.0 - value * series * (1.0 / term)
    return jnp.where(value < 0.5, value * series, 1.0 - jnp.exp(-value))


def times(left, right):
    return (
        left[0] * right[0] - left[1] * right[1],
        left[0] * right[1] + left[1] * right[0],
    )


def to_steps(block):
    return jnp.swapaxes(block, 0, 1).reshape(-1, block.shape[-1])


def from_steps(rows, group):
    return jnp.swapaxes(rows.reshape(-1, group, rows.shape[-1]), 0, 1)


def wide(keep, states):
    return jnp.concatenate([keep] * (states // LANES), axis=1)


def split(value):
    half = value.shape[-1] // 2
    return value[:, :half], value[:, half:]


def join(pair):
    return jnp.concatenate(pair, axis=1)


def spread_row(row, count):
    return jnp.broadcast_to(row, (count, row.shape[-1]))


def rows_of(step, group):
    return slice(step * group, (step + 1) * group)


def rows_at(base, step, group):
    if isinstance(base, int):
        return slice(base + step * group, base + (step + 1) * group)
    return pl.ds(pl.multiple_of(base + step * group, group), group)


def loop(count, body, carry):
    if not UNROLL:
        return lax.fori_loop(0, count, body, carry)
    for turn in range(count):
        carry = body(turn, carry)
    return carry


def maybe(condition, action):
    if isinstance(condition, bool):
        if condition:
            action()
    else:
        pl.when(condition)(action)


def scan_up(drive_ref, keep_ref, base, lam, state, steps, group, h_ref=None):
    states = lam[0].shape[-1]
    for step in range(steps):
        rows = rows_at(base, step, group)
        keep = wide(keep_ref[rows, :], states)
        turned = times(lam, state)
        state = (
            keep * turned[0] + drive_ref[rows, :states],
            keep * turned[1] + drive_ref[rows, states:],
        )
        if h_ref is not None:
            later = rows_at(base, step + 1, group)
            h_ref[later, :states] = state[0]
            h_ref[later, states:] = state[1]
    return state


def scan_down(dh_ref, keep_ref, base, lam, state, steps, group):
    states = lam[0].shape[-1]
    for step in range(steps - 1, -1, -1):
        rows = rows_at(base, step, group)
        keep = wide(keep_ref[rows, :], states)
        g = (dh_ref[rows, :states] + state[0], dh_ref[rows, states:] + state[1])
        state = times(lam, (keep * g[0], keep * g[1]))
    return state


def chunk_totals(factor, value, count, reverse):
    pieces = []
    for seq_no in range(count):
        rows = rows_of(seq_no, CHUNKS)
        a = (factor[0][rows], factor[1][rows])
        x = (value[0][rows], value[1][rows])
        place = lax.broadcasted_iota(jnp.int32, a[0].shape, 0)
        shift = 1
        while shift < CHUNKS:
            turn = CHUNKS - shift if reverse else shift
            valid = place < CHUNKS - shift if reverse else place >= shift
            a_before = tuple(pltpu.roll(part, turn, 0) for part in a)
            x_before = tuple(pltpu.roll(part, turn, 0) for part in x)
            a_new = times(a_before, a)
            x_new = times(a, x_before)
            x = tuple(jnp.where(valid, new + old, old) for new, old in zip(x_new, x))
            a = tuple(jnp.where(valid, new, old) for new, old in zip(a_new, a))
            shift *= 2
        pieces.append((a, x))
    return pieces


def write_totals(pieces, pre_ref, end_ref, reverse):
    count = len(pieces)
    edge = 0 if reverse else CHUNKS - 1
    for seq_no, (a, x) in enumerate(pieces):
        rows = rows_of(seq_no, CHUNKS)
        a_all = join(a)
        x_all = join(x)
        pre_ref[0, rows, :] = a_all
        pre_ref[1, rows, :] = x_all
        end_ref[seq_no : seq_no + 1, :] = a_all[edge : edge + 1]
        end_ref[count + seq_no : count + seq_no + 1, :] = x_all[edge : edge + 1]


def joined(first, second):
    count = first.shape[0] // 2
    second_a = split(second[:count])
    factor = times(split(first[:count]), second_a)
    moved = times(second_a, split(first[count:]))
    second_x = split(second[count:])
    value = (moved[0] + second_x[0], moved[1] + second_x[1])
    return jnp.concatenate([join(factor), join(value)], axis=0)


def combine_kernel(first_round, reverse, place_ref, at, total_ref, other_ref, *refs):
    later = place_ref[0, at] == (0 if reverse else 1)
    total, other = total_ref[...], other_ref[...]
    if first_round:
        total_out, before_out = refs
        half = total.shape[0] // 2
        row = lax.broadcasted_iota(jnp.int32, total.shape, 0)
        lane = lax.broadcasted_iota(jnp.int32, total.shape, 1)
        identity = jnp.where((row < half) & (lane < total.shape[1] // 2), 1.0, 0.0)
        before_out[...] = jnp.where(later, other, identity)
    else:
        before_ref, total_out, before_out = refs
        before = before_ref[...]
        before_out[...] = jnp.where(later, joined(other, before), before)
    total_out[...] = jnp.where(later, joined(other, total), joined(total, other))


def last_carry(place_ref, reverse, before_ref, other_ref):
    before, other = before_ref[...], other_ref[...]
    count = before.shape[0] // 2
    later = place_ref[1, 0] == (0 if reverse else 1)
    return jnp.where(later, joined(other, before), before)[count:]


def chunk_carries(pre_ref, entered, count, reverse):
    reals, imags = [], []
    for seq_no in range(count):
        rows = rows_of(seq_no, CHUNKS)
        a = split(pre_ref[0, rows, :])
        x = split(pre_ref[1, rows, :])
        carry = split(entered[seq_no : seq_no + 1, :])
        place = lax.broadcasted_iota(jnp.int32, a[0].shape, 0)
        first = place == (CHUNKS - 1 if reverse else 0)
        turn = CHUNKS - 1 if reverse else 1
        a = tuple(pltpu.roll(part, turn, 0) for part in a)
        x = tuple(pltpu.roll(part, turn, 0) for part in x)
        moved = times(a, carry)
        reals.append(jnp.where(first, carry[0], x[0] + moved[0]))
        imags.append(jnp.where(first, carry[1], x[1] + moved[1]))
    return jnp.concatenate(reals, axis=0), jnp.concatenate(imags, axis=0)


def chunk_factor(vec_ref, no, kept, conj=False):
    group = kept.shape[0]
    whole = split(vec_ref[no, 5:6, :])
    keep = wide(kept, whole[0].shape[-1])
    real, imag = tuple(spread_row(part, group) * keep for part in whole)
    return (real, -imag) if conj else (real, imag)


def lam_rows(vec_ref, no, group, conj=False):
    lam = split(vec_ref[no, 4:5, :])
    real, imag = spread_row(lam[0], group), spread_row(lam[1], group)
    return (real, -imag) if conj else (real, imag)


def halve(place_ref, whole_ref, kept_ref, sent_ref):
    half = kept_ref.shape[0]
    mine = place_ref[0, 0]
    kept_ref[...] = whole_ref[pl.ds(pl.multiple_of(mine * half, 8), half), :]
    sent_ref[...] = whole_ref[pl.ds(pl.multiple_of((1 - mine) * half, 8), half), :]


def column_sums(value):
    return jnp.sum(value.reshape(-1, 8, value.shape[-1]), axis=0)


def norm_affine(stream, vec_ref, no):
    xhat, scale = normalize(stream)
    return xhat * vec_ref[no, 0:1, :] + vec_ref[no, 1:2, :], xhat, scale


def write_drive(drive_ref, rows, normed_low, in_re_ref, in_im_ref, vec_ref, no):
    gamma = split(vec_ref[no, 3:4, :])
    states = gamma[0].shape[-1]
    drive_ref[rows, :states] = dot(normed_low, in_re_ref[...]) * gamma[0]
    drive_ref[rows, states:] = dot(normed_low, in_im_ref[...]) * gamma[1]


def time_block(ref, block, steps):
    if isinstance(block, int):
        return ref.at[:, block * steps : (block + 1) * steps, :]
    return ref.at[:, pl.ds(pl.multiple_of(block * steps, steps), steps), :]


class Weights:
    def __init__(self, sems, *copies):
        self.copies = [
            pltpu.make_async_copy(source if no is None else source.at[no], target, sems.at[at])
            for at, (source, no, target) in enumerate(copies)
        ]
        for copy in self.copies:
            copy.start()

    def wait(self, first=0, last=None):
        for copy in self.copies[first:last]:
            copy.wait()


class Fetch:
    def __init__(self, source, buffer, sems, steps, blocks, down=False):
        self.source, self.buffer, self.sems = source, buffer, sems
        self.steps, self.blocks, self.down = steps, blocks, down
        self.copy(0).start()

    def copy(self, turn):
        block = self.blocks - 1 - turn if self.down else turn
        slot = turn % 2
        return pltpu.make_async_copy(
            time_block(self.source, block, self.steps), self.buffer.at[slot], self.sems.at[slot]
        )

    def get(self, turn):
        maybe(turn + 1 < self.blocks, lambda: self.copy(turn + 1).start())

        self.copy(turn).wait()
        return to_steps(self.buffer[turn % 2]).astype(F32)


class Store:
    def __init__(self, target, buffer, sems, steps, blocks, down=False):
        self.target, self.buffer, self.sems = target, buffer, sems
        self.steps, self.blocks, self.down = steps, blocks, down

    def copy(self, turn):
        block = self.blocks - 1 - turn if self.down else turn
        slot = turn % 2
        return pltpu.make_async_copy(
            self.buffer.at[slot], time_block(self.target, block, self.steps), self.sems.at[slot]
        )

    def put(self, turn, rows, group):
        maybe(turn >= 2, lambda: self.copy(turn - 2).wait())

        self.buffer[turn % 2] = from_steps(rows, group)
        self.copy(turn).start()

    def finish(self):
        for turn in range(max(self.blocks - 2, 0), self.blocks):
            self.copy(turn).wait()


def decay_rows(vec_ref, no, gain, bias, skip, nu_log, theta_log, glu_b, length):
    speed = jnp.exp(nu_log)
    phase = jnp.exp(theta_log)
    radius = jnp.exp(-speed)
    lam_re, lam_im = radius * jnp.cos(phase), radius * jnp.sin(phase)
    square = one_minus_exp(2.0 * speed)
    gamma = jnp.sqrt(square)
    far = jnp.exp(-speed * length)
    far_re, far_im = far * jnp.cos(phase * length), far * jnp.sin(phase * length)
    width = gain.shape[-1]
    rows = [
        gain,
        bias,
        skip,
        join([gamma, gamma]),
        join([lam_re, lam_im]),
        join([far_re, far_im]),
        join([-speed * lam_re, -speed * lam_im]),
        join([speed * jnp.exp(-2.0 * speed) / square, jnp.zeros_like(speed)]),
        join([-phase * lam_im, phase * lam_re]),
        glu_b[:, :width],
        glu_b[:, width:],
    ]
    for at, row in enumerate(rows):
        vec_ref[no, at : at + 1, :] = row


def first_kernel(
    dims, index_ref, resets_far, tok_ref, in_re_far, in_im_far,
    gain_far, bias_far, skip_far, nu_far, theta_far, glu_b_far,
    drive_ref, keep_ref, kept_ref, pre_ref, end_ref, vec_ref, place_ref, tok_buf, tok_sems,
    resets_ref, in_re_ref, in_im_ref, weight_sems, gain_ref, bias_ref, skip_ref, nu_ref, theta_ref, glu_b_ref,
    bits,
):
    count, group, steps, length = dims
    states = in_re_ref.shape[-1]
    weights = Weights(
        weight_sems, (gain_far, None, gain_ref), (bias_far, None, bias_ref),
        (skip_far, None, skip_ref), (nu_far, None, nu_ref), (theta_far, None, theta_ref),
        (glu_b_far, None, glu_b_ref), (in_re_far, 0, in_re_ref), (in_im_far, 0, in_im_ref),
        (resets_far, None, resets_ref),
    )
    tok = Fetch(tok_ref, tok_buf, tok_sems, steps, length // steps)
    low, high = bits
    index = index_ref[0]
    lane = lax.broadcasted_iota(jnp.int32, place_ref.shape, 1)
    row = lax.broadcasted_iota(jnp.int32, place_ref.shape, 0)
    shift = jnp.where(row == 1, max(high - 1, 0), jnp.minimum(lane, 31))
    place_ref[...] = lax.shift_right_logical(jnp.full(place_ref.shape, index), shift) & 1
    weights.wait()
    for no in range(gain_ref.shape[0]):
        row = slice(no, no + 1)
        decay_rows(
            vec_ref, no, gain_ref[row, :], bias_ref[row, :], skip_ref[row, :], nu_ref[row, :],
            theta_ref[row, :], glu_b_ref[row, :], length,
        )
    first = lax.shift_right_logical(index, low) * (length * CHUNKS)
    origin = lax.broadcasted_iota(jnp.int32, (CHUNKS, LANES), 0) * length + first
    starts = [
        [
            jnp.broadcast_to(resets_ref[seq_no : seq_no + 1, slot : slot + 1], (CHUNKS, LANES))
            for slot in range(resets_ref.shape[1])
        ]
        for seq_no in range(count)
    ]
    lam = lam_rows(vec_ref, 0, group)

    def block(at, carry):
        base = at * (steps * group)
        state, kept = carry
        for step in range(steps):
            place = origin + (at * steps + step)
            keeps = []
            for seq_no in range(count):
                keep = jnp.ones((CHUNKS, LANES), F32)
                for start in starts[seq_no]:
                    keep = jnp.where(place == start, 0.0, keep)
                keeps.append(keep)
            keep = jnp.concatenate(keeps, axis=0)
            kept = kept * keep
            keep_ref[rows_at(base, step, group), :] = keep
        rows = rows_at(base, 0, steps * group)
        normed, _, _ = norm_affine(tok.get(at), vec_ref, 0)
        write_drive(drive_ref, rows, normed.astype(BF16), in_re_ref, in_im_ref, vec_ref, 0)
        state = scan_up(drive_ref, keep_ref, base, lam, state, steps, group)
        return state, kept

    zero = jnp.zeros((group, states), F32)
    state, kept = loop(
        length // steps, block, ((zero, zero), jnp.ones((group, LANES), F32))
    )
    kept_ref[...] = kept
    pieces = chunk_totals(chunk_factor(vec_ref, 0, kept), state, count, False)
    write_totals(pieces, pre_ref, end_ref, False)


def layer_out(h_low, normed, out_re_ref, out_im_ref, vec_ref, no, glu_w_ref):
    states = out_re_ref.shape[0]
    width = out_re_ref.shape[1]
    mixed = (
        dot(h_low[:, :states], out_re_ref[...])
        - dot(h_low[:, states:], out_im_ref[...])
        + vec_ref[no, 2:3, :] * normed
    )
    act = (0.5 * mixed * (1.0 + gelu_tanh(mixed))).astype(BF16)
    value = dot(act, glu_w_ref[:, :width]) + vec_ref[no, 9:10, :]
    gate = dot(act, glu_w_ref[:, width:]) + vec_ref[no, 10:11, :]
    return mixed, value, gate


def second_kernel(
    dims, place_ref, tok_ref, drive_ref, keep_ref, kept_ref, pre_in_ref, before_ref, other_ref, vec_ref,
    out_re_far, out_im_far, glu_w_far, in_re_far, in_im_far,
    h_ref, mixed_ref, value_ref, gate_ref, stream_ref, drive2_ref, pre_ref, end_ref,
    tok_buf, tok_sems, out_re_ref, out_im_ref, glu_w_ref, in_re_ref, in_im_ref, weight_sems,
):
    count, group, steps, length = dims
    weights = Weights(
        weight_sems, (out_re_far, 0, out_re_ref), (out_im_far, 0, out_im_ref),
        (glu_w_far, 0, glu_w_ref), (in_re_far, 1, in_re_ref), (in_im_far, 1, in_im_ref),
    )
    tok = Fetch(tok_ref, tok_buf, tok_sems, steps, length // steps)
    states = in_re_ref.shape[-1]
    size = steps * group
    entering_state = chunk_carries(
        pre_in_ref, last_carry(place_ref, False, before_ref, other_ref), count, False
    )
    h_ref[:group, :] = join(entering_state)
    lam, lam2 = lam_rows(vec_ref, 0, group), lam_rows(vec_ref, 1, group)
    weights.wait()

    def block(at, carry):
        base = at * size
        state, state2 = carry
        rows = rows_at(base, 0, size)
        state = scan_up(drive_ref, keep_ref, base, lam, state, steps, group, h_ref)
        stream = tok.get(at)
        normed, _, _ = norm_affine(stream, vec_ref, 0)
        h_low = h_ref[rows_at(base + group, 0, size), :].astype(BF16)
        mixed, value, gate = layer_out(
            h_low, normed, out_re_ref, out_im_ref, vec_ref, 0, glu_w_ref
        )
        mixed_ref[rows, :] = mixed.astype(BF16)
        value_ref[rows, :] = value.astype(BF16)
        gate_ref[rows, :] = gate.astype(BF16)
        stream = stream + value * sigmoid(gate)
        stream_ref[rows, :] = stream
        normed, _, _ = norm_affine(stream, vec_ref, 1)
        write_drive(drive2_ref, rows, normed.astype(BF16), in_re_ref, in_im_ref, vec_ref, 1)
        state2 = scan_up(drive2_ref, keep_ref, base, lam2, state2, steps, group)
        return state, state2

    zero = jnp.zeros((group, states), F32)
    _, state2 = loop(length // steps, block, (entering_state, (zero, zero)))
    pieces = chunk_totals(chunk_factor(vec_ref, 1, kept_ref[...]), state2, count, False)
    write_totals(pieces, pre_ref, end_ref, False)


def gate_back(
    rows, upstream, value, gate, mixed, out_re_ref, out_im_ref, glu_w_ref, sums_ref,
    act_ref, value_grad_ref, gate_grad_ref, mixed_grad_ref, dh_ref,
):
    states, width = out_re_ref.shape
    sig = sigmoid(gate)
    value_grad = upstream * sig
    gate_grad = (value_grad * value * (1.0 - sig)).astype(BF16)
    value_grad = value_grad.astype(BF16)
    value_grad_ref[rows, :] = value_grad
    gate_grad_ref[rows, :] = gate_grad
    sums_ref[:, 4 * width : 5 * width] += column_sums(value_grad.astype(F32))
    sums_ref[:, 5 * width : 6 * width] += column_sums(gate_grad.astype(F32))
    act_grad = dot_right_t(value_grad, glu_w_ref[:, :width]) + dot_right_t(
        gate_grad, glu_w_ref[:, width:]
    )
    bend = gelu_tanh(mixed)
    act_ref[rows, :] = (0.5 * mixed * (1.0 + bend)).astype(BF16)
    mixed_low = (act_grad * gelu_slope(mixed, bend)).astype(BF16)
    mixed_grad_ref[rows, :] = mixed_low
    dh_ref[rows, :states] = dot_right_t(mixed_low, out_re_ref[...])
    dh_ref[rows, states:] = -dot_right_t(mixed_low, out_im_ref[...])


def by_core(place_ref, kept_half, sent_half, first, second):
    @pl.when(place_ref[0, 0] == 0)
    def _():
        kept_half[...] = first()
        sent_half[...] = second()

    @pl.when(place_ref[0, 0] != 0)
    def _():
        sent_half[...] = first()
        kept_half[...] = second()


def glu_grads_kernel(place_ref, act_ref, value_grad_ref, gate_grad_ref, kept_half, sent_half):
    by_core(
        place_ref, kept_half, sent_half,
        lambda: dot_left_t(act_ref[...], value_grad_ref[...]),
        lambda: dot_left_t(act_ref[...], gate_grad_ref[...]),
    )


def out_grads_kernel(group, place_ref, h_ref, mixed_grad_ref, kept_half, sent_half):
    states = h_ref.shape[1] // 2
    by_core(
        place_ref, kept_half, sent_half,
        lambda: dot_left_t(h_ref[group:, :states].astype(BF16), mixed_grad_ref[...]),
        lambda: -dot_left_t(h_ref[group:, states:].astype(BF16), mixed_grad_ref[...]),
    )


def third_kernel(
    dims, place_ref, stream_ref, drive_ref, keep_ref, kept_ref, cot_ref, pre_in_ref, before_ref,
    other_ref, vec_ref,
    out_re_far, out_im_far, glu_w_far,
    out_far, h_ref, mixed_grad_ref, dh_ref, pre_ref, end_ref, act_ref, value_grad_ref, gate_grad_ref,
    sums_ref, cot_buf, cot_sems, out_buf, out_sems, out_re_ref, out_im_ref, glu_w_ref, weight_sems,
):
    count, group, steps, length = dims
    weights = Weights(
        weight_sems, (out_re_far, 1, out_re_ref), (out_im_far, 1, out_im_ref),
        (glu_w_far, 1, glu_w_ref),
    )
    cot = Fetch(cot_ref, cot_buf, cot_sems, steps, length // steps)
    result = Store(out_far, out_buf, out_sems, steps, length // steps)
    states = out_re_ref.shape[0]
    size = steps * group
    entering_state = chunk_carries(
        pre_in_ref, last_carry(place_ref, False, before_ref, other_ref), count, False
    )
    h_ref[:group, :] = join(entering_state)
    sums_ref[...] = jnp.zeros_like(sums_ref)
    lam = lam_rows(vec_ref, 1, group)
    weights.wait()

    def block(at, state):
        base = at * size
        rows = rows_at(base, 0, size)
        state = scan_up(drive_ref, keep_ref, base, lam, state, steps, group, h_ref)
        stream = stream_ref[rows, :]
        normed, _, _ = norm_affine(stream, vec_ref, 1)
        h_low = h_ref[rows_at(base + group, 0, size), :].astype(BF16)
        mixed, value, gate = layer_out(
            h_low, normed, out_re_ref, out_im_ref, vec_ref, 1, glu_w_ref
        )
        result.put(at, stream + value * sigmoid(gate), group)
        gate_back(
            rows, cot.get(at), value, gate, mixed, out_re_ref, out_im_ref, glu_w_ref, sums_ref,
            act_ref, value_grad_ref, gate_grad_ref, mixed_grad_ref, dh_ref,
        )
        return state

    loop(length // steps, block, entering_state)
    result.finish()
    back = lam_rows(vec_ref, 1, group, True)

    def turn(k, state):
        base = (length // steps - 1 - k) * size
        return scan_down(dh_ref, keep_ref, base, back, state, steps, group)

    zero = jnp.zeros((group, states), F32)
    state = loop(length // steps, turn, (zero, zero))
    pieces = chunk_totals(chunk_factor(vec_ref, 1, kept_ref[...], True), state, count, True)
    write_totals(pieces, pre_ref, end_ref, True)


def adjoint_scan(dims, base, dh_ref, keep_ref, h_ref, lam, state, g_ref, lam_sums_ref):
    _, group, steps, _ = dims
    states = lam[0].shape[-1]
    lam_re, lam_im = split(lam_sums_ref[...])
    for step in range(steps - 1, -1, -1):
        rows = rows_at(base, step, group)
        here = rows_of(step, group)
        keep = wide(keep_ref[rows, :], states)
        g = (dh_ref[rows, :states] + state[0], dh_ref[rows, states:] + state[1])
        kg = (keep * g[0], keep * g[1])
        state = times(lam, kg)
        g_ref[here, :states] = g[0]
        g_ref[here, states:] = g[1]
        prev = (h_ref[rows, :states], h_ref[rows, states:])
        lam_re = lam_re + (kg[0] * prev[0] + kg[1] * prev[1])
        lam_im = lam_im + (kg[1] * prev[0] - kg[0] * prev[1])
    lam_sums_ref[...] = join([lam_re, lam_im])
    return state


def through_input_map(drive_low, mixed_wide, vec_ref, no, in_re_ref, in_im_ref):
    states = in_re_ref.shape[-1]
    return (
        dot_right_t(drive_low[:, :states], in_re_ref[...])
        + dot_right_t(drive_low[:, states:], in_im_ref[...])
        + vec_ref[no, 2:3, :] * mixed_wide
    )


def input_map_back(
    g_ref, mixed_low, normed, vec_ref, no, in_re_ref, in_im_ref, grads_ref, grads_at
):
    width = in_re_ref.shape[0]
    drive_low = (g_ref[...] * vec_ref[no, 3:4, :]).astype(BF16)
    grads_ref[grads_at : grads_at + width, :] += dot_left_t(normed.astype(BF16), drive_low)
    mixed_wide = mixed_low.astype(F32)
    return (
        drive_low,
        through_input_map(drive_low, mixed_wide, vec_ref, no, in_re_ref, in_im_ref),
        mixed_wide,
    )


def add_sums(sums_ref, normed_grad, xhat, mixed_wide, normed):
    width = xhat.shape[-1]
    sums_ref[:, :width] += column_sums(normed_grad * xhat)
    sums_ref[:, width : 2 * width] += column_sums(normed_grad)
    sums_ref[:, 3 * width : 4 * width] += column_sums(mixed_wide * normed)


def through_norm(normed_grad, xhat, scale, vec_ref, no):
    inner = normed_grad * vec_ref[no, 0:1, :]
    middle = jnp.mean(inner, axis=-1, keepdims=True)
    along = jnp.mean(inner * xhat, axis=-1, keepdims=True)
    return scale * (inner - middle - xhat * along)


def finish_sums(
    small_ref, base, sums_ref, lam_sums_ref, vec_ref, no, in_re_ref, in_im_ref, grads_ref, grads_at
):
    width, states = in_re_ref.shape
    total = jnp.sum(sums_ref[...], axis=0, keepdims=True)
    lam_re, lam_im = split(jnp.sum(lam_sums_ref[...], axis=0, keepdims=True))
    rows = slice(grads_at, grads_at + width)
    gam = jnp.sum(
        column_sums(grads_ref[rows, :states] * in_re_ref[...].astype(F32))
        + column_sums(grads_ref[rows, states:] * in_im_ref[...].astype(F32)),
        axis=0,
        keepdims=True,
    )
    nu_grad = (
        vec_ref[no, 6:7, :states] * lam_re
        + vec_ref[no, 6:7, states:] * lam_im
        + vec_ref[no, 7:8, :states] * gam
    )
    theta_grad = vec_ref[no, 8:9, :states] * lam_re + vec_ref[no, 8:9, states:] * lam_im
    small_ref[base : base + 1, :] = total[:, :width]
    small_ref[base + 1 : base + 2, :] = total[:, width : 2 * width]
    small_ref[base + 2 : base + 3, :] = join([nu_grad, theta_grad])
    small_ref[base + 3 : base + 4, :] = total[:, 3 * width : 4 * width]
    small_ref[base + 4 : base + 5, :] = total[:, 4 * width : 5 * width]
    small_ref[base + 5 : base + 6, :] = total[:, 5 * width : 6 * width]


def fourth_kernel(
    dims, place_ref, dh_ref, keep_ref, h_ref, stream_ref, mixed_ref, cot_ref, sums_in_ref,
    pre_in_ref, before_ref, other_ref, vec_ref, in_re_far, in_im_far,
    up_ref, kept_half, sent_half, small_ref,
    grads_ref, g_ref, sums_ref, lam_ref, cot_buf, cot_sems, in_re_ref, in_im_ref, weight_sems,
):
    count, group, steps, length = dims
    weights = Weights(weight_sems, (in_re_far, 1, in_re_ref), (in_im_far, 1, in_im_ref))
    cot = Fetch(cot_ref, cot_buf, cot_sems, steps, length // steps, True)
    size = steps * group
    entering_state = chunk_carries(
        pre_in_ref, last_carry(place_ref, True, before_ref, other_ref), count, True
    )
    grads_ref[...] = jnp.zeros_like(grads_ref)
    sums_ref[...] = sums_in_ref[...]
    lam_ref[...] = jnp.zeros_like(lam_ref)
    lam = lam_rows(vec_ref, 1, group, True)
    weights.wait()

    def block(k, state):
        at = length // steps - 1 - k
        base = at * size
        rows = rows_at(base, 0, size)
        state = adjoint_scan(dims, base, dh_ref, keep_ref, h_ref, lam, state, g_ref, lam_ref)
        normed, xhat, scale = norm_affine(stream_ref[rows, :], vec_ref, 1)
        _, normed_grad, mixed_wide = input_map_back(
            g_ref, mixed_ref[rows, :], normed, vec_ref, 1, in_re_ref, in_im_ref, grads_ref, 0
        )
        add_sums(sums_ref, normed_grad, xhat, mixed_wide, normed)
        stream_grad = through_norm(normed_grad, xhat, scale, vec_ref, 1)
        up_ref[rows, :] = cot.get(k) + stream_grad
        return state

    loop(length // steps, block, entering_state)
    small_ref[...] = jnp.zeros_like(small_ref)
    finish_sums(
        small_ref, 0, sums_ref, lam_ref, vec_ref, 1, in_re_ref, in_im_ref, grads_ref, 0
    )
    halve(place_ref, grads_ref, kept_half, sent_half)


def middle_kernel(
    dims, place_ref, up_ref, keep_ref, kept_ref, vec_ref, value_ref, gate_ref, mixed_ref,
    out_re_far, out_im_far, glu_w_far,
    mixed_grad_ref, dh_ref, pre_ref, end_ref, act_ref, value_grad_ref, gate_grad_ref, sums_ref,
    out_re_ref, out_im_ref, glu_w_ref, weight_sems,
):
    count, group, steps, length = dims
    weights = Weights(
        weight_sems, (out_re_far, 0, out_re_ref), (out_im_far, 0, out_im_ref),
        (glu_w_far, 0, glu_w_ref),
    )
    states = out_re_ref.shape[0]
    size = steps * group
    blocks = length // steps
    sums_ref[...] = jnp.zeros_like(sums_ref)
    lam = lam_rows(vec_ref, 0, group, True)
    weights.wait()

    def block(k, state):
        at = length // steps - 1 - k
        base = at * size
        rows = rows_at(base, 0, size)
        gate_back(
            rows, up_ref[rows, :], value_ref[rows, :].astype(F32), gate_ref[rows, :].astype(F32),
            mixed_ref[rows, :].astype(F32), out_re_ref, out_im_ref, glu_w_ref, sums_ref,
            act_ref, value_grad_ref, gate_grad_ref, mixed_grad_ref, dh_ref,
        )
        return scan_down(dh_ref, keep_ref, base, lam, state, steps, group)

    zero = jnp.zeros((group, states), F32)
    state = loop(length // steps, block, (zero, zero))
    pieces = chunk_totals(chunk_factor(vec_ref, 0, kept_ref[...], True), state, count, True)
    write_totals(pieces, pre_ref, end_ref, True)


def fifth_kernel(
    dims, place_ref, dh_ref, keep_ref, h_ref, tok_ref, mixed_ref, sums_in_ref,
    small_in_ref, pre_in_ref, before_ref, other_ref, vec_ref, in_re_far, in_im_far,
    drive_ref, kept_half, sent_half,
    lanes_ref, small_ref, grads_ref, g_ref, sums_ref, lam_ref,
    tok_buf, tok_sems, in_re_ref, in_im_ref, weight_sems,
):
    count, group, steps, length = dims
    weights = Weights(weight_sems, (in_re_far, 0, in_re_ref), (in_im_far, 0, in_im_ref))
    tok = Fetch(tok_ref, tok_buf, tok_sems, steps, length // steps, True)
    blocks = length // steps
    size = steps * group
    entering_state = chunk_carries(
        pre_in_ref, last_carry(place_ref, True, before_ref, other_ref), count, True
    )
    grads_ref[...] = jnp.zeros_like(grads_ref)
    sums_ref[...] = sums_in_ref[...]
    lam_ref[...] = jnp.zeros_like(lam_ref)
    lam = lam_rows(vec_ref, 0, group, True)
    weights.wait()

    def block(k, state):
        at = blocks - 1 - k
        base = at * size
        rows = rows_at(base, 0, size)
        state = adjoint_scan(
            dims, base, dh_ref, keep_ref, h_ref, lam, state, g_ref, lam_ref
        )
        normed, xhat, _ = norm_affine(tok.get(k), vec_ref, 0)
        drive_low, normed_grad, mixed_wide = input_map_back(
            g_ref, mixed_ref[rows, :], normed, vec_ref, 0, in_re_ref, in_im_ref, grads_ref, 0
        )
        drive_ref[rows, :] = drive_low
        add_sums(sums_ref, normed_grad, xhat, mixed_wide, normed)
        return state

    loop(blocks, block, entering_state)
    small_ref[...] = small_in_ref[...]
    finish_sums(
        small_ref, 8, sums_ref, lam_ref, vec_ref, 0, in_re_ref, in_im_ref, grads_ref, 0
    )
    at = 0
    for source in (grads_ref, small_ref):
        for lane in range(0, source.shape[1], LANES):
            lanes_ref[at : at + source.shape[0], :] = source[:, lane : lane + LANES]
            at += source.shape[0]
    lanes_ref[at:, :] = jnp.zeros((lanes_ref.shape[0] - at, LANES), F32)
    halve(place_ref, lanes_ref, kept_half, sent_half)


def last_kernel(
    dims, tok_ref, mixed_ref, up_ref, drive_ref, vec_ref, in_re_far, in_im_far,
    grad_ref, tok_buf, tok_sems, grad_buf, grad_sems, in_re_ref, in_im_ref, weight_sems,
):
    count, group, steps, length = dims
    weights = Weights(weight_sems, (in_re_far, 0, in_re_ref), (in_im_far, 0, in_im_ref))
    tok = Fetch(tok_ref, tok_buf, tok_sems, steps, length // steps)
    grad = Store(grad_ref, grad_buf, grad_sems, steps, length // steps)
    size = steps * group
    weights.wait()

    def block(at, carry):
        rows = rows_at(at * size, 0, size)
        _, xhat, scale = norm_affine(tok.get(at), vec_ref, 0)
        normed_grad = through_input_map(
            drive_ref[rows, :], mixed_ref[rows, :].astype(F32), vec_ref, 0, in_re_ref, in_im_ref
        )
        grad.put(at, up_ref[rows, :] + through_norm(normed_grad, xhat, scale, vec_ref, 0), group)
        return carry

    loop(length // steps, block, 0)
    grad.finish()


class Running:
    def __init__(self, generator):
        self.generator, self.result = generator, None
        self.wants = self.sent = None
        self.advance(None)

    def advance(self, values):
        try:
            self.wants = self.generator.send(values)
        except StopIteration as stop:
            self.wants, self.result = None, stop.value


class Network:
    def __init__(self, axes, sizes):
        self.axes, self.sizes = axes, sizes
        self.total = sizes[0] * sizes[1]
        self.bits = self.total.bit_length() - 1
        self.index = lax.axis_index(axes[0]) * sizes[1] + lax.axis_index(axes[1])

    def bit(self, at):
        return (self.index >> at) & 1

    def flip(self, value, bits):
        if self.total == 1:
            return value
        mask = sum(1 << bit for bit in bits)
        return lax.ppermute(value, self.axes, [(i, i ^ mask) for i in range(self.total)])

    def launch(self, *running):
        for one in running:
            if one.wants is not None and one.sent is None:
                one.sent = [self.flip(value, bits) for value, bits in one.wants]

    def together(self, *running, beside=None, hold=False):
        running = [one for one in running if one.wants is not None]
        if hold:
            values = lax.optimization_barrier(
                [[value for value, _ in one.wants] for one in running if one.sent is None]
            )
            for one in running:
                if one.sent is None:
                    one.wants = list(zip(values.pop(0), [bits for _, bits in one.wants]))
        self.launch(*running)
        made = beside() if beside is not None else ()
        sent, made = lax.optimization_barrier(([one.sent for one in running], made))
        for one, values in zip(running, sent):
            one.sent = None
            one.advance(values)
        return made


def entering(net, place, total, reverse):
    low = net.sizes[1].bit_length() - 1
    before = other = jnp.zeros_like(total)
    whole = pl.BlockSpec(memory_space=pltpu.VMEM)
    for bit in range(low, net.bits):
        (other,) = yield [(total, (bit,))]
        if bit + 1 < net.bits:
            first = bit == low
            operands = [place, total, other] + ([] if first else [before])
            operands = [pltpu.with_memory_space_constraint(one, pltpu.VMEM) for one in operands]

            def kernel(place_ref, *refs, first=first, at=bit):
                combine_kernel(first, reverse, place_ref, at, *refs)

            total, before = pl.pallas_call(
                kernel,
                in_specs=[whole] * len(operands),
                out_specs=[whole] * 2,
                out_shape=[pltpu.VMEM(total.shape, F32)] * 2,
                compiler_params=pltpu.CompilerParams(vmem_limit_bytes=1 << 20),
            )(*operands)
    return before, other


def local_call(
    kernel, place, operands, out_shape, scratch=(), far=False, limit=16, seconds=5e-7, distant=()
):
    whole = pl.BlockSpec(memory_space=pltpu.VMEM)
    return pl.pallas_call(
        kernel,
        in_specs=[whole] * (1 + len(operands)) + [pl.BlockSpec(memory_space=pl.ANY)] * len(distant),
        input_output_aliases={1 + len(operands) + at: at for at in range(len(distant))},
        out_specs=[pl.BlockSpec(memory_space=pl.ANY) if far else whole] * len(out_shape),
        out_shape=out_shape,
        scratch_shapes=list(scratch),
        compiler_params=pltpu.CompilerParams(vmem_limit_bytes=limit << 20),
        cost_estimate=pl.CostEstimate(
            flops=int(seconds * 1e15), bytes_accessed=1 << 10, transcendentals=0
        ),
    )(
        *[pltpu.with_memory_space_constraint(one, pltpu.VMEM) for one in [place, *operands]],
        *[pltpu.with_memory_space_constraint(one, pltpu.HBM) for one in distant],
    )


def position(place_ref, bits):
    return sum(place_ref[0, bit] << at for at, bit in enumerate(bits))


def partner(bits, k):
    return tuple(bit for at, bit in enumerate(bits) if (k >> at) & 1)


def scatter_step(place, segments, cuts, bits):
    lanes = segments[0][0].shape[1]
    total = sum(segment[0].shape[0] for segment in segments)
    packed = len(set(bits)) == 1
    pieces = [cut >> len(own) for cut, own in zip(cuts, bits)]
    groups = [list(range(len(cuts)))] if packed else [[part] for part in range(len(cuts))]
    shapes = []
    for group in groups:
        rows = sum(pieces[part] for part in group)
        shapes += [pltpu.VMEM((rows, lanes), F32)] * (1 << len(bits[group[0]]))

    def kernel(place_ref, *refs):
        refs = list(refs)
        total_ref = refs.pop()
        row = 0
        for segment in segments:
            value = refs.pop(0)[...]
            for _ in segment[1:]:
                value = value + refs.pop(0)[...]
            total_ref[row : row + value.shape[0], :] = value
            row += value.shape[0]
        for group in groups:
            own = bits[group[0]]
            mine = position(place_ref, own)
            for k in range(1 << len(own)):
                out = refs.pop(0)
                at = 0
                for part in group:
                    size = pieces[part]
                    start = sum(cuts[:part]) + (mine ^ k) * size
                    out[at : at + size, :] = total_ref[pl.ds(pl.multiple_of(start, 8), size), :]
                    at += size

    out = local_call(
        kernel, place, [one for segment in segments for one in segment], shapes,
        [pltpu.VMEM((total, lanes), F32)],
    )
    kept, sent = [], []
    for group in groups:
        own = bits[group[0]]
        many = 1 << len(own)
        kept.append(out[0])
        sent += [(one, partner(own, k)) for k, one in enumerate(out[1:many], 1)]
        out = out[many:]
    return kept, sent


def add_step(place, arrays):
    def kernel(place_ref, *refs):
        value = refs[0][...]
        for ref in refs[1:-1]:
            value = value + ref[...]
        refs[-1][...] = value

    return local_call(kernel, place, arrays, [pltpu.VMEM(arrays[0].shape, F32)])[0]


def gather_step(place, items, bits, packed):
    lanes = items[0][0][0].shape[1]
    sizes = [rows << len(own) for (_, _, rows), own in zip(items, bits)]
    if packed:
        shapes = [pltpu.VMEM((sum(sizes), lanes), F32)]
    else:
        shapes = [pltpu.VMEM((size, lanes), F32) for size in sizes]
    operands = []
    for arrays, _, _ in items:
        operands += [one for one in arrays if not any(one is other for other in operands)]

    def find(array):
        return [one is array for one in operands].index(True)

    def kernel(place_ref, *refs):
        base = 0
        for at, ((arrays, first, rows), own) in enumerate(zip(items, bits)):
            out = refs[len(operands) + (0 if packed else at)]
            mine = position(place_ref, own)
            for k, array in enumerate(arrays):
                start = base + (mine ^ k) * rows
                out[pl.ds(pl.multiple_of(start, 8), rows), :] = refs[find(array)][
                    first : first + rows, :
                ]
            base += sizes[at] if packed else 0

    return local_call(kernel, place, operands, shapes)


def swap_cores(kept, sent):
    (got,) = yield [(sent, (0,))]
    return [kept, got]


def all_sum(net, place, segments, halves, far=((3, 4),)):
    total = sum(segment[0].shape[0] for segment in segments)
    if halves:
        cuts = [total // 2] * 2
        for bits in ([(1,), (2,)], [(2,), (1,)]):
            kept, sent = scatter_step(place, segments, cuts, bits)
            got = yield sent
            segments = [[mine, other] for mine, other in zip(kept, got)]
            cuts = [cut // 2 for cut in cuts]
    else:
        kept, sent = scatter_step(place, segments, [total], [(1, 2)])
        got = yield sent
        segments = [kept + got]
        cuts = [total // 4]
    for bits in far:
        kept, sent = scatter_step(place, segments, cuts, [bits] * len(cuts))
        got = yield sent
        segments = [kept + got]
        cuts = [cut >> len(bits) for cut in cuts]
    own = add_step(place, segments[0])
    for bit in range(5, net.bits):
        got = yield [(own, (bit,))]
        own = add_step(place, [own] + got)
    parts = [own]
    for bits in far[::-1]:
        own = parts[0]
        got = yield [(own, partner(bits, k)) for k in range(1, 1 << len(bits))]
        items = [([own] + got, sum(cuts[:at]), cuts[at]) for at in range(len(cuts))]
        parts = gather_step(place, items, [bits] * len(cuts), bits is not far[0])
        cuts = [cut << len(bits) for cut in cuts]
    if halves:
        for bits, last in (([(2,), (1,)], False), ([(1,), (2,)], True)):
            got = yield [(part, own) for part, own in zip(parts, bits)]
            items = [([part, other], 0, part.shape[0]) for part, other in zip(parts, got)]
            parts = gather_step(place, items, bits, last)
    else:
        got = yield [(parts[0], partner((1, 2), k)) for k in (1, 2, 3)]
        parts = gather_step(place, [([parts[0]] + got, 0, parts[0].shape[0])], [(1, 2)], True)
    (other,) = yield [(parts[0], (0,))]
    return parts[0], other


def half_copies(half, width, states, outs, layer, first_ref, input_ref=None, lanes_ref=None):
    in_re_out, in_im_out, out_re_out, out_im_out, glu_w_out = outs
    out = []
    if first_ref is not None:
        out += [
            (first_ref.at[:width], glu_w_out.at[layer, :, half * width : (half + 1) * width]),
            (first_ref.at[width : width + states], (out_re_out, out_im_out)[half].at[layer]),
        ]
    if input_ref is not None:
        size, rows = width + states, width // 2
        for target, left in ((in_re_out, 0), (in_im_out, states)):
            out.append((
                input_ref.at[size : size + rows, left : left + states],
                target.at[1, half * rows : (half + 1) * rows, :],
            ))
    if lanes_ref is not None:
        size, at = lanes_ref.shape[0], 0
        for target in (in_re_out, in_im_out):
            for lane in range(0, states, LANES):
                begin, end = max(at, half * size), min(at + width, (half + 1) * size)
                if begin < end:
                    start = begin - half * size
                    out.append((
                        lanes_ref.at[start : start + end - begin],
                        target.at[0, begin - at : end - at, lane : lane + LANES],
                    ))
                at += width
    return out


def run_copies(pairs, sems, first=0):
    running = [
        pltpu.make_async_copy(source, target, sems.at[first + at])
        for at, (source, target) in enumerate(pairs)
    ]
    for copy in running:
        copy.start()
    return running


def own_results_kernel(width, states, place_ref, own_a, other_a, own_c, own_d, *refs):
    *outs, sems = refs
    for core in (0, 1):

        @pl.when(place_ref[0, 0] == core)
        def _(core=core):
            pairs = half_copies(core, width, states, outs, 1, own_a)
            pairs += half_copies(1 - core, width, states, outs, 1, other_a)
            pairs += half_copies(core, width, states, outs, 0, own_c, own_c, own_d)
            for copy in run_copies(pairs, sems):
                copy.wait()


def other_results_kernel(width, states, place_ref, other_c, own_d, other_d, *refs):
    outs, small_outs = refs[5:10], refs[10:16]
    small_refs, sems = refs[16:22], refs[22]
    gain_ref, bias_ref, nu_ref, theta_ref, skip_ref, glu_b_ref = small_refs
    last = width * (2 * states // LANES) - own_d.shape[0]
    for core in (0, 1):

        @pl.when(place_ref[0, 0] == core)
        def _(core=core):
            pairs = half_copies(1 - core, width, states, outs, 0, other_c, other_c, other_d)
            running = run_copies(pairs, sems)
            upper = own_d if core else other_d
            small = jnp.concatenate(
                [
                    upper[last + 16 * at : last + 16 * (at + 1), :]
                    for at in range(width // LANES)
                ],
                axis=1,
            )
            for layer, base in ((1, 0), (0, 8)):
                row = slice(layer, layer + 1)
                gain_ref[row, :] = small[base : base + 1]
                bias_ref[row, :] = small[base + 1 : base + 2]
                nu_ref[row, :] = small[base + 2 : base + 3, :states]
                theta_ref[row, :] = small[base + 2 : base + 3, states:]
                skip_ref[row, :] = small[base + 3 : base + 4]
                glu_b_ref[row, :width] = small[base + 4 : base + 5]
                glu_b_ref[row, width:] = small[base + 5 : base + 6]
            for copy in running + run_copies(list(zip(small_refs, small_outs)), sems, len(running)):
                copy.wait()


def shards(
    sizes, tokens, cotangent, resets, ln_gain, ln_bias, in_re, in_im, nu_log, theta_log,
    out_re, out_im, skip, glu_w, glu_b,
):
    axes = ("seq", "row")
    micro, rows_here, span, width = tokens.shape
    states = nu_log.shape[-1]
    count = micro * rows_here
    group = count * CHUNKS
    length = span // CHUNKS
    steps = STEPS if length % STEPS == 0 else length
    size = steps * group
    total = length * group
    dims = (count, group, steps, length)

    tok = tokens.reshape(group, length, width)
    cot = cotangent.reshape(group, length, width)
    starts = resets.reshape(count, -1)

    whole = pl.BlockSpec(memory_space=pltpu.VMEM)
    scalars = pl.BlockSpec(memory_space=pltpu.SMEM)
    anywhere = pl.BlockSpec(memory_space=pl.ANY)

    def block_buffers(dtype):
        return [pltpu.VMEM((2, group, steps, width), dtype), pltpu.SemaphoreType.DMA((2,))]

    def near(value):
        return pltpu.with_memory_space_constraint(value, pltpu.VMEM)

    def distant(value):
        return pltpu.with_memory_space_constraint(value, pltpu.HBM)

    def call(kernel, seconds, operands, out_shape, scratch=(), aliases=None):
        specs, values = [], []
        for kind, *group_values in operands:
            for value in group_values:
                specs.append({near: whole, distant: anywhere, None: scalars}[kind])
                values.append(kind(value) if kind else value)
        return pl.pallas_call(
            functools.partial(kernel, dims),
            in_specs=specs,
            out_specs=[whole if getattr(out, 'memory_space', None) == pltpu.VMEM else anywhere for out in out_shape],
            input_output_aliases=aliases or {},
            out_shape=out_shape,
            scratch_shapes=list(scratch),
            compiler_params=pltpu.CompilerParams(vmem_limit_bytes=VMEM_LIMIT),
            cost_estimate=pl.CostEstimate(
                flops=int(seconds * 1e15), bytes_accessed=1 << 20, transcendentals=0
            ),
        )(*values)

    net = Network(axes, sizes)
    low_bits = sizes[1].bit_length() - 1

    def shape(*dims_, dtype=F32):
        return pltpu.VMEM(dims_, dtype)

    two = 2 * states
    pre_shape, end_shape = shape(2, group, two), shape(2 * count, two)
    full = shape(total, two)
    low = shape(total, width, dtype=BF16)
    past = shape(group + total, two)

    natural = jax.ShapeDtypeStruct((group, length, width), F32)
    in_w = pltpu.VMEM(in_re.shape[1:], BF16)
    out_w = pltpu.VMEM(out_re.shape[1:], BF16)
    glu = pltpu.VMEM(glu_w.shape[1:], BF16)
    sems = pltpu.SemaphoreType.DMA
    blocks = length // steps
    drive1, keep, kept, pre1, end1, vec, place = call(
        functools.partial(first_kernel, bits=(low_bits, net.bits)),
        7e-6,
        [(None, net.index.reshape(1).astype(jnp.int32)), (distant, starts, tok, in_re, in_im),
         (distant, ln_gain, ln_bias, skip, nu_log, theta_log, glu_b)],
        [full, shape(total, LANES), shape(group, LANES), pre_shape, end_shape,
         shape(ln_gain.shape[0], 16, width), shape(8, LANES, dtype=jnp.int32)],
        block_buffers(BF16) + [pltpu.VMEM(starts.shape, jnp.int32), in_w, in_w, sems((9,))]
        + [pltpu.VMEM(v.shape, F32) for v in (ln_gain, ln_bias, skip, nu_log, theta_log, glu_b)],
    )
    enter = Running(entering(net, place, end1, False))
    while enter.wants:
        net.together(enter)
    carry1 = enter.result

    h1, mixed1, value1, gate1, stream1, drive2, pre2, end2 = call(
        second_kernel,
        12e-6,
        [(near, place), (distant, tok), (near, drive1, keep, kept, pre1, *carry1, vec),
         (distant, out_re, out_im, glu_w, in_re, in_im)],
        [past, low, low, low, shape(total, width), full, pre_shape, end_shape],
        block_buffers(BF16) + [out_w, out_w, glu, in_w, in_w, sems((5,))],
    )
    enter = Running(entering(net, place, end2, False))
    while enter.wants:
        net.together(enter)
    carry2 = enter.result

    sums_shape = shape(8, 6 * width)
    act, h2, mixed_grad2, dh2, back2, back_end2, act2, value_grad2, gate_grad2, sums2 = call(
        third_kernel,
        20e-6,
        [(near, place, stream1, drive2, keep, kept), (distant, cot),
         (near, pre2, *carry2, vec), (distant, out_re, out_im, glu_w)],
        [natural, past, low, full, pre_shape, end_shape, low, low, low, sums_shape],
        block_buffers(F32) * 2 + [out_w, out_w, glu, sems((3,))],
    )

    def glu_grads(act_low, value_grad, gate_grad):
        return local_call(
            glu_grads_kernel, place, [act_low, value_grad, gate_grad], [shape(width, width)] * 2,
            seconds=3e-6,
        )

    def out_grads(h, mixed_grad):
        return local_call(
            functools.partial(out_grads_kernel, group), place, [h, mixed_grad],
            [shape(states, width)] * 2, seconds=2e-6,
        )

    enter = Running(entering(net, place, back_end2, True))
    glu_a = Running(swap_cores(
        *net.together(enter, beside=lambda: glu_grads(act2, value_grad2, gate_grad2))
    ))
    out_a = Running(swap_cores(
        *net.together(enter, glu_a, beside=lambda: out_grads(h2, mixed_grad2))
    ))
    net.together(enter, out_a)
    while enter.wants:
        net.together(enter)
    back_carry2 = enter.result
    sum_a = Running(all_sum(net, place, [glu_a.result, out_a.result], True))

    lam_sums = pltpu.VMEM((group, two), F32)
    run_sums = pltpu.VMEM((8, 6 * width), F32)
    g_block = pltpu.VMEM((size, two), F32)
    up1, kept_b, sent_b, small2 = net.together(sum_a, beside=lambda: call(
        fourth_kernel,
        16e-6,
        [(near, place, dh2, keep, h2, stream1, mixed_grad2), (distant, cot),
         (near, sums2, back2, *back_carry2, vec), (distant, in_re, in_im)],
        [shape(total, width), shape(width // 2, two), shape(width // 2, two), shape(16, width)],
        [shape(width, two), g_block, run_sums, lam_sums] + block_buffers(F32) + [in_w, in_w, sems((2,))],
        aliases={4: 0},
    ))
    core_b = Running(swap_cores(kept_b, sent_b))
    mixed_grad1, dh1, back1, back_end1, act1, value_grad1, gate_grad1, sums1 = net.together(
        sum_a, core_b, beside=lambda: call(
        middle_kernel,
        16e-6,
        [(near, place, up1, keep, kept, vec, value1, gate1, mixed1), (distant, out_re, out_im, glu_w)],
        [low, full, pre_shape, end_shape, low, low, low, sums_shape],
        [out_w, out_w, glu, sems((3,))],
        aliases={7: 4, 5: 5, 6: 6},
    ))
    enter = Running(entering(net, place, back_end1, True))
    glu_c = Running(swap_cores(
        *net.together(enter, beside=lambda: glu_grads(act1, value_grad1, gate_grad1))
    ))
    out_c = Running(swap_cores(
        *net.together(enter, glu_c, beside=lambda: out_grads(h1, mixed_grad1))
    ))
    net.together(enter, out_c)
    while enter.wants:
        net.together(enter)
    back_carry1 = enter.result
    sum_c = Running(all_sum(net, place, [glu_c.result, out_c.result, core_b.result], True))
    rows_d = width * (two // LANES) + 16 * (width // LANES)
    rows_d += -rows_d % (8 * 32)
    drive_grad1, kept_d, sent_d = net.together(sum_a, sum_c, hold=False, beside=lambda: call(
        fifth_kernel,
        9e-6,
        [(near, place, dh1, keep, h1), (distant, tok),
         (near, mixed_grad1, sums1, small2), (near, back1, *back_carry1, vec),
         (distant, in_re, in_im)],
        [low, shape(rows_d // 2, LANES), shape(rows_d // 2, LANES)],
        [shape(rows_d, LANES), shape(16, width), shape(width, two), g_block, run_sums, lam_sums]
        + block_buffers(BF16) + [in_w, in_w, sems((2,))],
    ))
    core_d = Running(swap_cores(kept_d, sent_d))
    net.together(sum_c, core_d, sum_a)
    sum_d = Running(all_sum(net, place, [core_d.result], False))
    net.together(sum_c, sum_d, sum_a)
    net.together(sum_c, sum_d, sum_a)
    net.together(sum_c, sum_d, sum_a)
    (input_grad,) = net.together(sum_c, sum_d, beside=lambda: call(
        last_kernel,
        7e-6,
        [(distant, tok), (near, mixed_grad1, up1, drive_grad1, vec), (distant, in_re, in_im)],
        [natural],
        block_buffers(BF16) + block_buffers(F32) + [in_w, in_w, sems((2,))],
    ))

    def at_last(one):
        return one.wants[0][1] == (0,)

    while sum_a.wants or not (at_last(sum_c) and at_last(sum_d)):
        net.together(sum_a, *[one for one in (sum_c, sum_d) if not at_last(one)])
    own_c, own_d = sum_c.wants[0][0], sum_d.wants[0][0]
    wide_rows, narrow_rows = shape(2, width), shape(2, states)
    large = [pltpu.HBM(one.shape, F32) for one in (in_re, in_im, out_re, out_im, glu_w)]
    tiny = [pltpu.HBM(one.shape, F32) for one in (ln_gain, ln_bias, nu_log, theta_log, skip, glu_b)]
    results = net.together(sum_c, sum_d, beside=lambda: local_call(
        functools.partial(own_results_kernel, width, states), place,
        [*sum_a.result, own_c, own_d], large, [sems((32,))], True, seconds=2e-6,
    ))
    results = local_call(
        functools.partial(other_results_kernel, width, states), place,
        [sum_c.result[1], own_d, sum_d.result[1]], large + tiny,
        [wide_rows, wide_rows, narrow_rows, narrow_rows, wide_rows, shape(2, 2 * width), sems((32,))],
        True, distant=results,
    )
    in_re_g, in_im_g, out_re_g, out_im_g, glu_w_g, gain_g, bias_g, nu_g, theta_g, skip_g, glu_b_g = results
    return (
        act.reshape(tokens.shape), input_grad.reshape(tokens.shape), gain_g, bias_g, in_re_g, in_im_g,
        nu_g, theta_g, out_re_g, out_im_g, skip_g, glu_w_g, glu_b_g,
    )


def solution(mesh):
    sizes = (mesh.shape["seq"], mesh.shape["row"])
    split_rows = P(None, "row", "seq", None)
    in_specs = (split_rows, split_rows, P(None, "row", None)) + (P(),) * 11
    out_specs = (split_rows, split_rows) + (P(),) * 11
    return jax.shard_map(
        functools.partial(shards, sizes),
        mesh=mesh,
        in_specs=in_specs,
        out_specs=out_specs,
        check_vma=False,
    )
```
